32 devices in a mesh: section: 2 (over x), dp: 4 (over z), ctx: 4 (over y, core).
Axes of the slice: x: 2, y: 2, z: 4, core: 2. Of those that a mesh axis runs over, the one named last changes fastest.
Arguments:
- block_in: bfloat16 [2, 4, 512, 1024], P(None, 'dp', 'ctx'), may hold values from -6 to 6
- doc_lengths: int32 [2, 4, 8], P(None, 'dp'), may hold values from 1 to 204, 512 in all within a row
- w_query: bfloat16 [2, 1024, 512], P('section', ('dp', 'ctx')), may hold values from -0.1875 to 0.1875
- w_key: bfloat16 [2, 1024, 512], P('section', ('dp', 'ctx')), may hold values from -0.1875 to 0.1875
- w_value: bfloat16 [2, 1024, 1024], P('section', ('dp', 'ctx')), may hold values from -0.1875 to 0.1875
- forget_down: bfloat16 [2, 1024, 16], P('section', ('dp', 'ctx')), may hold values from -0.1875 to 0.1875
- forget_up: bfloat16 [2, 16, 512], P('section', None, ('dp', 'ctx')), may hold values from -1.5 to 1.5
- forget_bias: bfloat16 [2, 512], P('section', ('dp', 'ctx')), may hold values from 0.5 to 7
- w_gate: bfloat16 [2, 1024, 1024], P('section', ('dp', 'ctx')), may hold values from -0.1875 to 0.1875
- w_out: bfloat16 [2, 1024, 1024], P('section', ('dp', 'ctx')), may hold values from -0.375 to 0.375
- mix_gain: bfloat16 [2, 1024], P('section', ('dp', 'ctx')), may hold values from 0.5 to 1.5
- ffn_gain: bfloat16 [2, 1024], P('section', ('dp', 'ctx')), may hold values from 0.5 to 1.5
- ff_gate: bfloat16 [2, 1024, 2816], P('section', ('dp', 'ctx')), may hold values from -0.1875 to 0.1875
- ff_up: bfloat16 [2, 1024, 2816], P('section', ('dp', 'ctx')), may hold values from -0.1875 to 0.1875
- ff_down: bfloat16 [2, 2816, 1024], P('section', ('dp', 'ctx')), may hold values from -0.21875 to 0.21875
- out_grad: bfloat16 [2, 4, 512, 1024], P(None, 'dp', 'ctx'), may hold values from -6 to 6
Outputs:
- section_outputs: bfloat16 [2, 2, 4, 512, 1024], P('section', None, 'dp', 'ctx')
- section_input_grads: float32 [2, 2, 4, 512, 1024], P('section', None, 'dp', 'ctx')
- grad_w_query: float32 [2, 1024, 512], P('section', ('dp', 'ctx'))
- grad_w_key: float32 [2, 1024, 512], P('section', ('dp', 'ctx'))
- grad_w_value: float32 [2, 1024, 1024], P('section', ('dp', 'ctx'))
- grad_forget_down: float32 [2, 1024, 16], P('section', ('dp', 'ctx'))
- grad_forget_up: float32 [2, 16, 512], P('section', None, ('dp', 'ctx'))
- grad_forget_bias: float32 [2, 512], P('section', ('dp', 'ctx'))
- grad_w_gate: float32 [2, 1024, 1024], P('section', ('dp', 'ctx'))
- grad_w_out: float32 [2, 1024, 1024], P('section', ('dp', 'ctx'))
- grad_mix_gain: float32 [2, 1024], P('section', ('dp', 'ctx'))
- grad_ffn_gain: float32 [2, 1024], P('section', ('dp', 'ctx'))
- grad_ff_gate: float32 [2, 1024, 2816], P('section', ('dp', 'ctx'))
- grad_ff_up: float32 [2, 1024, 2816], P('section', ('dp', 'ctx'))
- grad_ff_down: float32 [2, 2816, 1024], P('section', ('dp', 'ctx'))
The draws below stay inside these ranges and needn't reach their ends.
Inputs may be any that keep to these rules, and one draw needn't show every extreme that they name: `doc_lengths`: each sequence's lengths sum to 512; the longest is 204.
All inputs are finite; a program needn't handle non-finite values.
Results may differ from the reference program's by a relative error of at most 0.0208.
Values may be sent and summed in bfloat16 or wider, within the bound.
No kernel may reach another device: no remote copies, remote signals or barrier semaphores. Data moves between devices by JAX's collectives and lax.ppermute only.
A program may use at most 256 MiB of HBM per device.

```python
import math
import jax
import jax.numpy as jnp
import numpy as np
from jax import lax

D = 1024
HEADS = 4
KD = 512
VD = 1024
RANK = 16
FF = 2816
STRETCH = 64
MICRO = 2
DOCS = 8
KH = 128
VH = 256
SEQS = 4
SEQ_LEN = 512
MOST = 204


def draw_forget_bias(key, part):
    key = jax.random.fold_in(key, 7)
    values = jnp.exp(jax.random.uniform(key, (2, KD), jnp.float32, math.log(0.5), math.log(6.0)))
    return values.astype(jnp.bfloat16)


def block_scale(key, shape, shards, low, top_value):
    def one(dim, shards_of):
        heights = jax.random.uniform(jax.random.fold_in(jax.random.fold_in(key, 6), dim), (shards_of,), jnp.float32, low / len(shards), top_value / len(shards))
        return jnp.repeat(jnp.exp(heights), shape[dim] // shards_of).reshape((-1,) + (1,) * (len(shape) - dim - 1))

    factor_of = one(*shards[0])
    for cut in shards[1:]:
        factor_of = factor_of * one(*cut)
    return factor_of


def profile(amount, total, most, slope):
    weights = [(1 << 20) // math.isqrt(standing ** slope) + 1 for standing in range(2, amount + 1)]
    rest, holding = total - most - (amount - 1), [1] * (amount - 1)
    while rest > 0:
        candidates = [i for i in range(amount - 1) if holding[i] < most]
        mass, left = sum([weights[i] for i in candidates]), rest
        for i in candidates:
            addition = min(most - holding[i], max(1, left * weights[i] // mass), rest)
            holding[i] = holding[i] + addition
            rest = rest - addition
    return np.array([most] + holding)


def ragged(stream_key, number_of, total, limit, skew):
    if number_of == 2:
        one = jax.random.randint(stream_key, (), max(1, total - limit), min(limit, total - 1) + 1)
        return jnp.stack([one, total - one])
    tallies = jnp.asarray(profile(number_of, total, limit, skew), jnp.int32)
    pairs = (number_of - 1) // 2
    donor, receiver = tallies[1:1 + 2 * pairs:2], tallies[2:2 + 2 * pairs:2]
    slack = jnp.minimum(donor - 1, limit - receiver)
    moved = jax.random.randint(jax.random.fold_in(stream_key, 1), (pairs,), 0, 1 << 20) % (slack + 1)
    tallies = tallies.at[1:1 + 2 * pairs:2].set(donor - moved).at[2:2 + 2 * pairs:2].set(receiver + moved)
    return tallies[jax.random.permutation(jax.random.fold_in(stream_key, 2), number_of)]


def gaussian(stream_key, extent, scale, reach, cuts=(), kind=jnp.bfloat16):
    values = scale * jax.random.normal(stream_key, extent, jnp.float32)
    if cuts:
        values = values * block_scale(stream_key, extent, cuts, -0.22, 0.18)
    return jnp.clip(values, -reach, reach).astype(kind)


def setup_inputs(seed: int = 0) -> dict:
    seeds = jax.random.split(jax.random.key(seed), 17)
    return {
        "block_in": gaussian(seeds[0], (MICRO, SEQS, SEQ_LEN, D), 1.0, 6.0, ((1, 4), (2, 4))),
        "doc_lengths": jax.vmap(lambda own: ragged(own, DOCS, SEQ_LEN, MOST, 0))(jax.random.split(seeds[1], MICRO * SEQS)).reshape((MICRO, SEQS, DOCS)).astype(jnp.int32),
        "w_query": gaussian(seeds[2], (2, D, KD), D ** -0.5, 0.1875, ((0, 2), (1, 16))),
        "w_key": gaussian(seeds[3], (2, D, KD), D ** -0.5, 0.1875, ((0, 2), (1, 16))),
        "w_value": gaussian(seeds[4], (2, D, VD), D ** -0.5, 0.1875, ((0, 2), (1, 16))),
        "forget_down": gaussian(seeds[5], (2, D, RANK), D ** -0.5, 0.1875, ((0, 2), (1, 16))),
        "forget_up": gaussian(seeds[6], (2, RANK, KD), RANK ** -0.5, 1.5, ((0, 2), (2, 16))),
        "forget_bias": draw_forget_bias(jax.random.fold_in(seeds[16], 71), 0),
        "w_gate": gaussian(seeds[8], (2, D, VD), D ** -0.5, 0.1875, ((0, 2), (1, 16))),
        "w_out": gaussian(seeds[9], (2, VD, D), (VD // 4) ** -0.5, 0.375, ((0, 2), (1, 16))),
        "mix_gain": jnp.clip(1.0 + 0.1 * jax.random.normal(seeds[10], (2, D), jnp.float32), 0.5, 1.5).astype(jnp.bfloat16),
        "ffn_gain": jnp.clip(1.0 + 0.1 * jax.random.normal(seeds[11], (2, D), jnp.float32), 0.5, 1.5).astype(jnp.bfloat16),
        "ff_gate": gaussian(seeds[12], (2, D, FF), D ** -0.5, 0.1875, ((0, 2), (1, 16))),
        "ff_up": gaussian(seeds[13], (2, D, FF), D ** -0.5, 0.1875, ((0, 2), (1, 16))),
        "ff_down": gaussian(seeds[14], (2, FF, D), (FF // 4) ** -0.5, 0.21875, ((0, 2), (1, 16))),
        "out_grad": gaussian(seeds[15], (MICRO, SEQS, SEQ_LEN, D), 1.0, 6.0, ((1, 4), (2, 4))),
    }


@jax.custom_vjp
def low(v):
    return lax.optimization_barrier(v.astype(jnp.bfloat16)).astype(jnp.float32)

@jax.custom_vjp
def low_back(v):
    return v

def low_keep(v):
    return (low(v), None)

def low_pass(kept, grad):
    return (grad,)

def back_keep(v):
    return (v, None)

def back_low(kept, grad):
    return (low(grad),)
low.defvjp(low_keep, low_pass)
low_back.defvjp(back_keep, back_low)
highest = lax.Precision.HIGHEST
norm_eps = 1e-06
head_eps = 0.1

def matmul_high(left, right):
    return jnp.matmul(left, right, precision=highest)

def rms_scale(values, weight):
    return values * lax.rsqrt(lax.optimization_barrier(jnp.mean(values * values, axis=-1, keepdims=True)) + norm_eps) * weight

def doc_starts(doc_lengths, positions):
    ends = jnp.cumsum(doc_lengths, axis=-1)
    begins = ends - doc_lengths
    matches = positions[:, None] == begins[..., None, :]
    return jnp.any(matches, axis=-1).astype(jnp.float32)

def split_heads(query_pre, key_pre, value_pre, forget_pre, forget_shift):
    leading = query_pre.shape[:-1]
    queries = (query_pre * KH ** (-0.5)).reshape(leading + (HEADS, KH))
    key_rows = key_pre.reshape(leading + (HEADS, KH))
    val_rows = value_pre.reshape(leading + (HEADS, VH))
    decays = (jax.nn.log_sigmoid(forget_pre + forget_shift) / 16.0).reshape(leading + (HEADS, KH))
    return (queries, key_rows, val_rows, decays)

def head_gate(mixed, gate_pre):
    normed = mixed * lax.rsqrt(lax.optimization_barrier(jnp.mean(mixed * mixed, axis=-1, keepdims=True)) + head_eps)
    return normed.reshape(gate_pre.shape) * jax.nn.silu(gate_pre)

def stretch_mix(queries, key_rows, val_rows, decays, resets, initial):
    seq_count, tok_count = (queries.shape[0], queries.shape[1])
    blk_count = tok_count // STRETCH

    def to_blocks(array):
        shaped = array.reshape((seq_count, blk_count, STRETCH) + array.shape[2:])
        return jnp.moveaxis(shaped, 1, 0)
    causal = jnp.tril(jnp.ones((STRETCH, STRETCH), jnp.float32))

    def advance(memory, pieces):
        q_blk, k_blk, v_blk, g_blk, r_blk = pieces
        cumulative = jnp.cumsum(g_blk, axis=1)
        segment = jnp.cumsum(r_blk, axis=1)
        no_reset = (segment == 0).astype(jnp.float32)
        q_exp = q_blk * jnp.exp(cumulative)
        k_exp = k_blk * jnp.exp(-cumulative)
        scores = jnp.einsum('bihk,bjhk->bhij', q_exp, k_exp, precision=highest)
        same_doc = (segment[:, :, None] == segment[:, None, :]).astype(jnp.float32) * causal
        scores = scores * same_doc[:, None]
        within = jnp.einsum('bhij,bjhv->bihv', scores, v_blk, precision=highest)
        carried = jnp.einsum('bihk,bhkv->bihv', q_exp, memory, precision=highest) * no_reset[:, :, None, None]
        last_sum = cumulative[:, -1]
        tail_doc = (segment == segment[:, -1:]).astype(jnp.float32)
        k_last = k_blk * jnp.exp(last_sum[:, None] - cumulative) * tail_doc[:, :, None, None]
        retain = jnp.exp(last_sum) * no_reset[:, -1][:, None, None]
        memory = memory * retain[..., None] + jnp.einsum('bjhk,bjhv->bhkv', k_last, v_blk, precision=highest)
        return (memory, within + carried)
    final_state, outputs = lax.scan(jax.checkpoint(advance), initial, (to_blocks(queries), to_blocks(key_rows), to_blocks(val_rows), to_blocks(decays), to_blocks(resets)))
    outputs = jnp.moveaxis(outputs, 0, 1).reshape((seq_count, tok_count, HEADS, VH))
    return (outputs, final_state)

def gla_layer(layer_x, weights, resets):
    w_query, w_key, w_value, forget_down, forget_up, forget_bias, w_gate, w_out, mix_gain, ffn_gain, ff_gate, ff_up, ff_down = weights
    normed_in = low(rms_scale(layer_x, mix_gain))
    query_pre = low_back(matmul_high(normed_in, w_query))
    key_pre = low_back(matmul_high(normed_in, w_key))
    value_pre = low_back(matmul_high(normed_in, w_value))
    gate_pre = low_back(matmul_high(normed_in, w_gate))
    low_rank = low(low_back(matmul_high(normed_in, forget_down)))
    forget_pre = low_back(matmul_high(low_rank, forget_up))
    queries, key_rows, val_rows, decays = split_heads(query_pre, key_pre, value_pre, forget_pre, forget_bias)
    initial = jnp.zeros((layer_x.shape[0], HEADS, KH, VH), jnp.float32)
    mixed, _ = stretch_mix(queries, key_rows, val_rows, decays, resets, initial)
    gated = low(head_gate(mixed, gate_pre))
    middle = layer_x + low_back(matmul_high(gated, w_out))
    normed_mid = low(rms_scale(middle, ffn_gain))
    hidden = low(jax.nn.silu(low_back(matmul_high(normed_mid, ff_gate))) * low_back(matmul_high(normed_mid, ff_up)))
    return middle + low_back(matmul_high(hidden, ff_down))

def reference(block_in, doc_lengths, w_query, w_key, w_value, forget_down, forget_up, forget_bias, w_gate, w_out, mix_gain, ffn_gain, ff_gate, ff_up, ff_down, out_grad):
    positions = jnp.arange(SEQ_LEN, dtype=jnp.int32)
    resets = doc_starts(doc_lengths, positions).reshape((MICRO * SEQS, SEQ_LEN))
    block_x = block_in.astype(jnp.float32).reshape((MICRO * SEQS, SEQ_LEN, D))
    params = tuple((weight_arr.astype(jnp.float32) for weight_arr in (w_query, w_key, w_value, forget_down, forget_up, forget_bias, w_gate, w_out, mix_gain, ffn_gain, ff_gate, ff_up, ff_down)))

    def forward(layer_in, layers, offset):
        lower_layer = tuple((stacked[0] for stacked in layers))
        upper_layer = tuple((stacked[1] for stacked in layers))
        lower_out = gla_layer(layer_in, lower_layer, resets)
        upper_in = low_back(low(lower_out)) + offset
        upper_out = gla_layer(upper_in, upper_layer, resets)
        return (lower_out, upper_out)
    offset = jnp.zeros_like(block_x)
    (lower_out, upper_out), pullback = jax.vjp(forward, block_x, params, offset)
    seed_grad = out_grad.astype(jnp.float32).reshape(block_x.shape)
    grad_in, weight_grads, grad_mid = pullback((jnp.zeros_like(lower_out), seed_grad))
    shape_out = (2, MICRO, SEQS, SEQ_LEN, D)
    section_outputs = jnp.stack([lower_out, upper_out]).astype(jnp.bfloat16).reshape(shape_out)
    section_input_grads = jnp.stack([grad_in, grad_mid]).reshape(shape_out)
    return (section_outputs, section_input_grads, weight_grads[0], weight_grads[1], weight_grads[2], weight_grads[3], weight_grads[4], weight_grads[5], weight_grads[6], weight_grads[7], weight_grads[8], weight_grads[9], weight_grads[10], weight_grads[11], weight_grads[12])
```

```python
import functools

import jax
import jax.numpy as jnp
from jax import lax
from jax.experimental import pallas as pl
from jax.experimental.pallas import tpu as pltpu
from jax.sharding import PartitionSpec as P

HEADS = 4
KH = 128
VH = 256
RANK = 16
STRETCH = 64
CHUNK = 2 * STRETCH

norm_eps = 1e-06
head_eps = 0.1
BF = jnp.bfloat16
F32 = jnp.float32
highest = lax.Precision.HIGHEST


def mm(left, right):
    return jnp.dot(left, right, preferred_element_type=F32)


def mm_back(left, right):
    return lax.dot_general(left, right, (((1,), (1,)), ((), ())), preferred_element_type=F32)


def mm_rows(left, right):
    return lax.dot_general(left, right, (((0,), (0,)), ((), ())), preferred_element_type=F32)


def dot_nn(a, b):
    return lax.dot_general(
        a, b, (((1,), (0,)), ((), ())), precision=highest, preferred_element_type=F32
    )


def dot_nt(a, b):
    return lax.dot_general(
        a, b, (((1,), (1,)), ((), ())), precision=highest, preferred_element_type=F32
    )


def dot_tn(a, b):
    return lax.dot_general(
        a, b, (((0,), (0,)), ((), ())), precision=highest, preferred_element_type=F32
    )


def chunk_parts(n, q_ref, k_ref, g_ref, seg_col_ref, seg_row_ref, low_tri):
    at = pl.ds(n * CHUNK, CHUNK)
    summed = dot_nn(low_tri, g_ref[at, :])
    middle = summed[STRETCH - 1 : STRETCH, :]
    last = summed[CHUNK - 1 : CHUNK, :]
    seg = seg_col_ref[at, :]
    seg_last = seg[CHUNK - 1 : CHUNK, :]
    seg_row = seg_row_ref[:, at]
    if n > 0:
        seg_prev = seg_col_ref[pl.ds(n * CHUNK - 1, 1), :]
    else:
        seg_prev = jnp.full((1, 1), -1.0, F32)
    up = jnp.exp(summed - middle)
    down = jnp.exp(middle - summed)
    entry = jnp.where(seg == seg_prev, jnp.exp(summed), 0.0)
    tail = jnp.where(seg == seg_last, jnp.exp(last - summed), 0.0)
    keep = jnp.where(seg_last == seg_prev, jnp.exp(last), 0.0)
    return at, seg, seg_row, up, down, entry, tail, keep


def tri_masks():
    rows = lax.broadcasted_iota(jnp.int32, (CHUNK, CHUNK), 0)
    cols = lax.broadcasted_iota(jnp.int32, (CHUNK, CHUNK), 1)
    return rows >= cols, rows <= cols


def gla_fwd_kernel(count, q_ref, k_ref, v_ref, g_ref, seg_col_ref, seg_row_ref, mixed_ref, st_ref):
    lower, _ = tri_masks()
    low_tri = lower.astype(F32)
    state = jnp.zeros(st_ref.shape[1:], F32)
    for n in range(count):
        at, seg, seg_row, up, down, entry, tail, keep = chunk_parts(
            n, q_ref, k_ref, g_ref, seg_col_ref, seg_row_ref, low_tri
        )
        q, k, v = q_ref[at, :], k_ref[at, :], v_ref[at, :]
        scores = dot_nt(q * up, k * down)
        scores = jnp.where(lower & (seg == seg_row), scores, 0.0)
        out = dot_nn(scores, v)
        st_ref[n] = state
        if n > 0:
            out = out + dot_nt(q * entry, state)
        mixed_ref[at, :] = out
        if n + 1 < count:
            state = state * keep + dot_tn(v, k * tail)


def gla_bwd_kernel(
    count,
    q_ref,
    k_ref,
    v_ref,
    g_ref,
    seg_col_ref,
    seg_row_ref,
    st_ref,
    do_ref,
    dq_ref,
    dk_ref,
    dv_ref,
    dg_ref,
):
    lower, upper = tri_masks()
    low_tri = lower.astype(F32)
    up_tri = upper.astype(F32)
    d_state = jnp.zeros(st_ref.shape[1:], F32)
    for n in reversed(range(count)):
        at, seg, seg_row, up, down, entry, tail, keep = chunk_parts(
            n, q_ref, k_ref, g_ref, seg_col_ref, seg_row_ref, low_tri
        )
        q, k, v, do = q_ref[at, :], k_ref[at, :], v_ref[at, :], do_ref[at, :]
        mask = lower & (seg == seg_row)
        q_up, k_down = q * up, k * down
        scores = jnp.where(mask, dot_nt(q_up, k_down), 0.0)
        d_scores = jnp.where(mask, dot_nt(do, v), 0.0)
        dq = dot_nn(d_scores, k_down) * up
        dk = dot_tn(d_scores, q_up) * down
        dv = dot_tn(scores, do)
        d_last = None
        if n + 1 < count:
            k_tail = k * tail
            dk_tail = dot_nn(v, d_state)
            dk = dk + dk_tail * tail
            dv = dv + dot_nt(k_tail, d_state)
            d_last = jnp.sum(dk_tail * k_tail, axis=0, keepdims=True)
        if n > 0:
            state = st_ref[n]
            dq = dq + dot_nn(do, state) * entry
            if d_last is not None:
                d_last = d_last + keep * jnp.sum(d_state * state, axis=0, keepdims=True)
            d_state = d_state * keep + dot_tn(do, q * entry)
        dg = dot_nn(up_tri, q * dq - k * dk)
        if d_last is not None:
            dg = dg + d_last
        dq_ref[at, :] = dq
        dk_ref[at, :] = dk
        dv_ref[at, :] = dv
        dg_ref[at, :] = dg


KERNEL_PARAMS = pltpu.CompilerParams(vmem_limit_bytes=40 * 1024 * 1024)


def gla_fwd(q, k, v, g, seg_col, seg_row):
    length, width = v.shape
    count = length // CHUNK
    return pl.pallas_call(
        functools.partial(gla_fwd_kernel, count),
        out_shape=(
            jax.ShapeDtypeStruct((length, width), F32),
            jax.ShapeDtypeStruct((count, width, KH), F32),
        ),
        compiler_params=KERNEL_PARAMS,
        name="gla_fwd",
    )(q, k, v, g, seg_col, seg_row)


def gla_bwd(q, k, v, g, seg_col, seg_row, states, do):
    length, width = v.shape
    count = length // CHUNK
    return pl.pallas_call(
        functools.partial(gla_bwd_kernel, count),
        out_shape=(
            jax.ShapeDtypeStruct((length, KH), F32),
            jax.ShapeDtypeStruct((length, KH), F32),
            jax.ShapeDtypeStruct((length, width), F32),
            jax.ShapeDtypeStruct((length, KH), F32),
        ),
        compiler_params=KERNEL_PARAMS,
        name="gla_bwd",
    )(q, k, v, g, seg_col, seg_row, states, do)


def shift(block, distance):
    size = lax.axis_size("ctx")
    return lax.ppermute(block, "ctx", [(i, (i + distance) % size) for i in range(size)])


def gather_blocks(block):
    return [block] + [shift(block, s) for s in range(1, lax.axis_size("ctx"))]


def in_order(blocks):
    size, place = lax.axis_size("ctx"), lax.axis_index("ctx")
    rows = blocks[0].shape[0]
    whole = jnp.zeros((size * rows,) + blocks[0].shape[1:], blocks[0].dtype)
    for s, block in enumerate(blocks):
        whole = lax.dynamic_update_slice_in_dim(whole, block, ((place - s) % size) * rows, 0)
    return whole


def return_blocks(whole):
    size = lax.axis_size("ctx")
    rows = whole.shape[0] // size
    total = whole[:rows].astype(F32)
    for s in range(1, size):
        total = total + shift(whole[s * rows : (s + 1) * rows].astype(BF), -s).astype(F32)
    return total


def return_ordered(whole):
    size, place = lax.axis_size("ctx"), lax.axis_index("ctx")
    rows = whole.shape[0] // size
    total = lax.dynamic_slice_in_dim(whole, place * rows, rows, 0).astype(F32)
    for s in range(1, size):
        part = lax.dynamic_slice_in_dim(whole, ((place - s) % size) * rows, rows, 0)
        total = total + shift(part.astype(BF), -s).astype(F32)
    return total


def over_head(values, repeats):
    if repeats == 1:
        return values
    size = lax.axis_size("ctx")
    total = values
    for s in range(1, repeats):
        route = [(i, i - i % repeats + (i + s) % repeats) for i in range(size)]
        total = total + lax.ppermute(values, "ctx", route)
    return total


def swap_sections(block):
    return lax.ppermute(block, "section", [(0, 1), (1, 0)])


def inv_rms(values):
    return lax.rsqrt(jnp.mean(values * values, axis=-1, keepdims=True) + norm_eps)


def norm_back(values, scale, gain, d_out):
    normed = values * scale
    d_normed = d_out * gain
    inner = jnp.mean(d_normed * normed, axis=-1, keepdims=True)
    return scale * (d_normed - normed * inner), jnp.sum(d_out * normed, axis=0)


def per_device(
    block_in,
    doc_lengths,
    w_query,
    w_key,
    w_value,
    forget_down,
    forget_up,
    forget_bias,
    w_gate,
    w_out,
    mix_gain,
    ffn_gain,
    ff_gate,
    ff_up,
    ff_down,
    out_grad,
):
    sections = lax.axis_size("section")
    dp, ctx = lax.axis_size("dp"), lax.axis_size("ctx")
    section, place = lax.axis_index("section"), lax.axis_index("ctx")
    first = section == 0
    owners = dp * ctx
    repeats = ctx // HEADS
    width = VH // repeats
    span = block_in.shape[2]
    model = block_in.shape[3]
    rows = w_query.shape[1]
    ff_rows = ff_down.shape[1]
    ff_own = ff_rows * dp
    ff_pad = -(-ff_own // 128) * 128
    up_cols, bias_cols, gain_cols = forget_up.shape[2], forget_bias.shape[1], mix_gain.shape[1]
    small_count = RANK * up_cols + bias_cols + 2 * gain_cols
    small_cols = -(-small_count // rows)
    head = place // repeats

    def own_micro(array):
        return jnp.where(first, array[0], array[1])[0]

    lengths = own_micro(doc_lengths)
    begins = jnp.cumsum(lengths) - lengths
    positions = jnp.arange(span * ctx, dtype=jnp.int32)
    seg = jnp.sum((begins[None, :] <= positions[:, None]).astype(F32), axis=1)
    seg_col, seg_row = seg[:, None], seg[None, :]

    def head_blocks(shard):
        parts = shard[0].reshape(rows, HEADS, KH).transpose(1, 0, 2)
        return jnp.repeat(parts, repeats, axis=0) if repeats > 1 else parts

    def value_blocks(shard):
        return shard[0].reshape(rows, ctx, width).transpose(1, 0, 2)

    def hidden_blocks(shard):
        parts = shard[0].reshape(rows, dp, ctx, ff_rows).transpose(2, 0, 1, 3)
        parts = parts.reshape(ctx, rows, ff_own)
        return jnp.pad(parts, ((0, 0), (0, 0), (0, ff_pad - ff_own)))

    def to_all(block):
        return jnp.broadcast_to(block[None], (ctx,) + block.shape)

    small = jnp.concatenate(
        [forget_up[0].reshape(-1), forget_bias[0], mix_gain[0], ffn_gain[0]]
    )
    small = jnp.pad(small, (0, small_cols * rows - small_count)).reshape(rows, small_cols)
    mix_cols = 2 * KH + 2 * width
    low_end = mix_cols + RANK
    attn_cols = -(-(low_end + small_cols) // 128) * 128
    attn_send = jnp.concatenate(
        [
            head_blocks(w_query),
            head_blocks(w_key),
            value_blocks(w_value),
            value_blocks(w_gate),
            to_all(forget_down[0]),
            to_all(small),
            jnp.zeros((ctx, rows, attn_cols - low_end - small_cols), BF),
        ],
        axis=2,
    )
    ff_send = jnp.concatenate([hidden_blocks(ff_gate), hidden_blocks(ff_up)], axis=2)

    def spread(send):
        got = lax.all_to_all(send, "ctx", 0, 0, tiled=True)
        whole = lax.all_gather(
            got.reshape(ctx * rows, send.shape[2]), ("section", "dp"), axis=0, tiled=True
        )
        return whole.reshape(sections, model, send.shape[2])

    attn_all = spread(attn_send)
    out_all = lax.all_gather(w_out[0], ("section", "dp"), axis=0, tiled=True)
    out_all = out_all.reshape(sections, dp, rows, model)
    out_all = lax.all_to_all(out_all, "ctx", 1, 1, tiled=True).reshape(sections, width, model)
    ff_all = spread(ff_send)
    down_all = lax.all_gather(ff_down[0], ("section", "dp"), axis=0, tiled=True)
    down_all = down_all.reshape(sections, ff_own, model)

    def layer_weights(layer):
        attn = attn_all[layer]
        tiny = attn[:, low_end : low_end + small_cols].reshape(owners, small_cols * rows)
        cuts = [RANK * up_cols, bias_cols, gain_cols, gain_cols]
        pieces, start = [], 0
        for cut in cuts:
            pieces.append(tiny[:, start : start + cut])
            start += cut
        up_whole = pieces[0].reshape(owners, RANK, up_cols).transpose(1, 0, 2)
        up_whole = up_whole.reshape(RANK, HEADS * KH)
        forget_up_own = lax.dynamic_slice_in_dim(up_whole, head * KH, KH, 1)
        bias_own = lax.dynamic_slice_in_dim(pieces[1].reshape(-1), head * KH, KH, 0)
        return (
            attn[:, :low_end],
            forget_up_own,
            bias_own.astype(F32),
            pieces[2].reshape(-1).astype(F32),
            pieces[3].reshape(-1).astype(F32),
            out_all[layer],
            ff_all[layer],
            down_all[layer],
        )

    def forward(x, weights):
        w_attn, w_up, bias, gain_in, gain_mid, w_mix, w_ff, w_down = weights
        x_all = in_order(gather_blocks(x)).astype(F32)
        normed_in = (x_all * inv_rms(x_all) * gain_in).astype(BF)
        pre = mm(normed_in, w_attn)
        low_rank = pre[:, mix_cols:low_end].astype(BF)
        forget_pre = mm(low_rank, w_up) + bias
        decays = jax.nn.log_sigmoid(forget_pre) / 16.0
        q = pre[:, :KH] * KH ** (-0.5)
        k = pre[:, KH : 2 * KH]
        v = pre[:, 2 * KH : 2 * KH + width]
        gate_pre = pre[:, 2 * KH + width : mix_cols]
        mixed, states = gla_fwd(q, k, v, decays, seg_col, seg_row)
        square = over_head(jnp.sum(mixed * mixed, axis=-1, keepdims=True), repeats)
        scale = lax.rsqrt(square / VH + head_eps)
        gated = (mixed * scale * jax.nn.silu(gate_pre)).astype(BF)
        middle = x.astype(F32) + return_ordered(mm(gated, w_mix))
        scale_mid = inv_rms(middle)
        normed_mid = jnp.concatenate(
            gather_blocks((middle * scale_mid * gain_mid).astype(BF)), axis=0
        )
        ff_pre = mm(normed_mid, w_ff)
        a, b = ff_pre[:, :ff_pad], ff_pre[:, ff_pad:]
        hidden = (jax.nn.silu(a) * b).astype(BF)[:, :ff_own]
        out = middle + return_blocks(mm(hidden, w_down))
        kept = (
            normed_in,
            low_rank,
            forget_pre,
            decays,
            q,
            k,
            v,
            gate_pre,
            mixed,
            states,
            scale,
            gated,
            middle,
            scale_mid,
            normed_mid,
            a,
            b,
            hidden,
        )
        return out.astype(BF), kept

    def backward(x, weights, kept, d_out):
        w_attn, w_up, bias, gain_in, gain_mid, w_mix, w_ff, w_down = weights
        (
            normed_in,
            low_rank,
            forget_pre,
            decays,
            q,
            k,
            v,
            gate_pre,
            mixed,
            states,
            scale,
            gated,
            middle,
            scale_mid,
            normed_mid,
            a,
            b,
            hidden,
        ) = kept
        dff = jnp.concatenate(gather_blocks(d_out.astype(BF)), axis=0)
        d_hidden = jnp.pad(mm_back(dff, w_down), ((0, 0), (0, ff_pad - ff_own)))
        sig = jax.nn.sigmoid(a)
        d_a = (d_hidden * b * (sig * (1.0 + a * (1.0 - sig)))).astype(BF)
        d_b = (d_hidden * (a * sig)).astype(BF)
        d_ab = jnp.concatenate([d_a, d_b], axis=1)
        d_normed_mid = return_blocks(mm_back(d_ab, w_ff))
        grad_down = mm_rows(hidden, dff).astype(BF)
        grad_ff = mm_rows(normed_mid, d_ab).astype(BF)
        d_mid_part, grad_gain_mid = norm_back(middle, scale_mid, gain_mid, d_normed_mid)
        d_middle = d_out + d_mid_part

        d_branch = in_order(gather_blocks(d_middle.astype(BF)))
        d_gated = mm_back(d_branch, w_mix)
        grad_out = mm_rows(gated, d_branch).astype(BF)
        sig_gate = jax.nn.sigmoid(gate_pre)
        silu_gate = gate_pre * sig_gate
        normed = mixed * scale
        d_gate = d_gated * normed * (sig_gate * (1.0 + gate_pre * (1.0 - sig_gate)))
        d_normed = d_gated * silu_gate
        inner = over_head(jnp.sum(d_normed * normed, axis=-1, keepdims=True), repeats) / VH
        d_mixed = scale * (d_normed - normed * inner)
        d_q, d_k, d_v, d_g = gla_bwd(q, k, v, decays, seg_col, seg_row, states, d_mixed)
        d_forget = d_g * jax.nn.sigmoid(-forget_pre) / 16.0
        grad_bias = jnp.sum(d_forget, axis=0)
        d_forget = d_forget.astype(BF)
        grad_up = mm_rows(low_rank, d_forget)
        d_low = mm_back(d_forget, w_up).astype(BF)
        d_pre = jnp.concatenate(
            [
                (d_q * KH ** (-0.5)).astype(BF),
                d_k.astype(BF),
                d_v.astype(BF),
                d_gate.astype(BF),
                d_low,
            ],
            axis=1,
        )
        d_normed_in = return_ordered(mm_back(d_pre, w_attn))
        grad_attn = mm_rows(normed_in, d_pre).astype(BF)
        x_own = x.astype(F32)
        d_in_part, grad_gain_in = norm_back(x_own, inv_rms(x_own), gain_in, d_normed_in)
        d_in = d_middle + d_in_part

        up_whole = lax.dynamic_update_slice_in_dim(
            jnp.zeros((RANK, HEADS * KH), F32), grad_up, head * KH, 1
        )
        up_whole = up_whole.reshape(RANK, owners, up_cols).transpose(1, 0, 2)
        bias_whole = lax.dynamic_update_slice_in_dim(
            jnp.zeros((HEADS * KH,), F32), grad_bias, head * KH, 0
        )
        tiny = jnp.concatenate(
            [
                up_whole.reshape(owners, RANK * up_cols),
                bias_whole.reshape(owners, bias_cols),
                grad_gain_in.reshape(owners, gain_cols),
                grad_gain_mid.reshape(owners, gain_cols),
            ],
            axis=1,
        )
        tiny = jnp.pad(tiny, ((0, 0), (0, small_cols * rows - small_count)))
        tiny = tiny.reshape(model, small_cols).astype(BF)
        spare = jnp.zeros((model, attn_cols - low_end - small_cols), BF)
        grad_attn = jnp.concatenate([grad_attn, tiny, spare], axis=1)
        return d_in, (grad_attn, grad_out, grad_ff, grad_down)

    weights = [layer_weights(layer) for layer in range(sections)]
    x = own_micro(block_in)
    layer_x, layer_kept, layer_y = [], [], []
    for layer in range(sections):
        layer_x.append(x)
        x, kept = forward(x, weights[layer])
        layer_kept.append(kept)
        layer_y.append(x)
    d_x = own_micro(out_grad).astype(F32)
    layer_dx, layer_grads = [None] * sections, [None] * sections
    for layer in reversed(range(sections)):
        upstream = d_x if layer == sections - 1 else d_x.astype(BF).astype(F32)
        d_x, grads = backward(layer_x[layer], weights[layer], layer_kept[layer], upstream)
        layer_dx[layer] = d_x
        grad_attn, grad_out, grad_ff, grad_down = grads
        grad_out = lax.all_to_all(
            grad_out.reshape(ctx, rows, model), "ctx", 0, 0, tiled=True
        ).reshape(dp * rows, model)
        layer_grads[layer] = [
            lax.psum_scatter(g, "dp", scatter_dimension=0, tiled=True)
            for g in (grad_down, grad_ff, grad_out, grad_attn)
        ]

    def to_owner(low, high):
        mine = jnp.where(first, low, high)
        return mine, swap_sections(jnp.where(first, high, low))

    def both(low, high):
        mine, other = to_owner(low, high)
        return jnp.stack([jnp.where(first, mine, other), jnp.where(first, other, mine)])

    def total(index):
        mine, other = to_owner(layer_grads[0][index], layer_grads[1][index])
        return mine.astype(F32) + other.astype(F32)

    def to_rows(array):
        cols = array.shape[1]
        return lax.all_to_all(
            array.astype(BF).reshape(ctx, rows, cols), "ctx", 0, 0, tiled=True
        ).astype(F32)

    outputs = both(*layer_y)
    input_grads = both(*layer_dx)
    own_down = total(0)
    own_ff = to_rows(total(1))
    own_out = total(2)
    own_attn = to_rows(total(3))

    def hidden_whole(parts):
        parts = parts.reshape(ctx, rows, dp, ff_rows).transpose(1, 2, 0, 3)
        return parts.reshape(rows, owners * ff_rows)

    def head_whole(parts):
        parts = parts.reshape(HEADS, repeats, rows, KH).sum(1)
        return parts.transpose(1, 0, 2).reshape(rows, HEADS * KH)

    def value_whole(parts):
        return parts.transpose(1, 0, 2).reshape(rows, HEADS * VH)

    tiny = jnp.sum(own_attn[:, :, low_end : low_end + small_cols], axis=0).reshape(-1)
    up_end = RANK * up_cols
    bias_end = up_end + bias_cols
    mix_end = bias_end + gain_cols
    return (
        outputs[None, :, None],
        input_grads[None, :, None],
        head_whole(own_attn[:, :, :KH])[None],
        head_whole(own_attn[:, :, KH : 2 * KH])[None],
        value_whole(own_attn[:, :, 2 * KH : 2 * KH + width])[None],
        jnp.sum(own_attn[:, :, mix_cols:low_end], axis=0)[None],
        tiny[:up_end].reshape(1, RANK, up_cols),
        tiny[up_end:bias_end][None],
        value_whole(own_attn[:, :, 2 * KH + width : mix_cols])[None],
        own_out[None],
        tiny[bias_end:mix_end][None],
        tiny[mix_end : mix_end + gain_cols][None],
        hidden_whole(own_ff[:, :, :ff_own])[None],
        hidden_whole(own_ff[:, :, ff_pad : ff_pad + ff_own])[None],
        own_down[None],
    )


def solution(mesh):
    rows = P("section", ("dp", "ctx"), None)
    columns = P("section", None, ("dp", "ctx"))
    vector = P("section", ("dp", "ctx"))
    tokens = P(None, "dp", "ctx", None)
    stacked = P("section", None, "dp", "ctx", None)
    return jax.shard_map(
        per_device,
        mesh=mesh,
        in_specs=(
            tokens,
            P(None, "dp", None),
            rows,
            rows,
            rows,
            rows,
            columns,
            vector,
            rows,
            rows,
            vector,
            vector,
            rows,
            rows,
            rows,
            tokens,
        ),
        out_specs=(
            stacked,
            stacked,
            rows,
            rows,
            rows,
            rows,
            columns,
            vector,
            rows,
            rows,
            vector,
            vector,
            rows,
            rows,
            rows,
        ),
        check_vma=False,
    )
```

```python
import functools

import jax
import jax.numpy as jnp
from jax import lax
from jax.experimental import pallas as pl
from jax.experimental.pallas import tpu as pltpu
from jax.sharding import PartitionSpec as P

HEADS = 4
KH = 128
VH = 256
RANK = 16
STRETCH = 64
CHUNK = 2 * STRETCH

norm_eps = 1e-06
head_eps = 0.1
BF = jnp.bfloat16
F32 = jnp.float32
highest = lax.Precision.HIGHEST


def mm(left, right):
    return jnp.dot(left, right, preferred_element_type=F32)


def mm_back(left, right):
    return lax.dot_general(left, right, (((1,), (1,)), ((), ())), preferred_element_type=F32)


def mm_rows(left, right):
    return lax.dot_general(left, right, (((0,), (0,)), ((), ())), preferred_element_type=F32)


def dot_nn(a, b):
    return lax.dot_general(
        a, b, (((1,), (0,)), ((), ())), precision=highest, preferred_element_type=F32
    )


def dot_nt(a, b):
    return lax.dot_general(
        a, b, (((1,), (1,)), ((), ())), precision=highest, preferred_element_type=F32
    )


def dot_tn(a, b):
    return lax.dot_general(
        a, b, (((0,), (0,)), ((), ())), precision=highest, preferred_element_type=F32
    )


def chunk_parts(n, q_ref, k_ref, g_ref, seg_col_ref, seg_row_ref, low_tri):
    at = pl.ds(n * CHUNK, CHUNK)
    summed = dot_nn(low_tri, g_ref[at, :])
    middle = summed[STRETCH - 1 : STRETCH, :]
    last = summed[CHUNK - 1 : CHUNK, :]
    seg = seg_col_ref[at, :]
    seg_last = seg[CHUNK - 1 : CHUNK, :]
    seg_row = seg_row_ref[:, at]
    if n > 0:
        seg_prev = seg_col_ref[pl.ds(n * CHUNK - 1, 1), :]
    else:
        seg_prev = jnp.full((1, 1), -1.0, F32)
    up = jnp.exp(summed - middle)
    down = jnp.exp(middle - summed)
    entry = jnp.where(seg == seg_prev, jnp.exp(summed), 0.0)
    tail = jnp.where(seg == seg_last, jnp.exp(last - summed), 0.0)
    keep = jnp.where(seg_last == seg_prev, jnp.exp(last), 0.0)
    return at, seg, seg_row, up, down, entry, tail, keep


def tri_masks():
    rows = lax.broadcasted_iota(jnp.int32, (CHUNK, CHUNK), 0)
    cols = lax.broadcasted_iota(jnp.int32, (CHUNK, CHUNK), 1)
    return rows >= cols, rows <= cols


def gla_fwd_kernel(count, q_ref, k_ref, v_ref, g_ref, seg_col_ref, seg_row_ref, mixed_ref, st_ref):
    lower, _ = tri_masks()
    low_tri = lower.astype(F32)
    state = jnp.zeros(st_ref.shape[1:], F32)
    for n in range(count):
        at, seg, seg_row, up, down, entry, tail, keep = chunk_parts(
            n, q_ref, k_ref, g_ref, seg_col_ref, seg_row_ref, low_tri
        )
        q, k, v = q_ref[at, :], k_ref[at, :], v_ref[at, :]
        scores = dot_nt(q * up, k * down)
        scores = jnp.where(lower & (seg == seg_row), scores, 0.0)
        out = dot_nn(scores, v)
        st_ref[n] = state
        if n > 0:
            out = out + dot_nt(q * entry, state)
        mixed_ref[at, :] = out
        if n + 1 < count:
            state = state * keep + dot_tn(v, k * tail)


def gla_bwd_kernel(
    count,
    q_ref,
    k_ref,
    v_ref,
    g_ref,
    seg_col_ref,
    seg_row_ref,
    st_ref,
    do_ref,
    dq_ref,
    dk_ref,
    dv_ref,
    dg_ref,
):
    lower, upper = tri_masks()
    low_tri = lower.astype(F32)
    up_tri = upper.astype(F32)
    d_state = jnp.zeros(st_ref.shape[1:], F32)
    for n in reversed(range(count)):
        at, seg, seg_row, up, down, entry, tail, keep = chunk_parts(
            n, q_ref, k_ref, g_ref, seg_col_ref, seg_row_ref, low_tri
        )
        q, k, v, do = q_ref[at, :], k_ref[at, :], v_ref[at, :], do_ref[at, :]
        mask = lower & (seg == seg_row)
        q_up, k_down = q * up, k * down
        scores = jnp.where(mask, dot_nt(q_up, k_down), 0.0)
        d_scores = jnp.where(mask, dot_nt(do, v), 0.0)
        dq = dot_nn(d_scores, k_down) * up
        dk = dot_tn(d_scores, q_up) * down
        dv = dot_tn(scores, do)
        d_last = None
        if n + 1 < count:
            k_tail = k * tail
            dk_tail = dot_nn(v, d_state)
            dk = dk + dk_tail * tail
            dv = dv + dot_nt(k_tail, d_state)
            d_last = jnp.sum(dk_tail * k_tail, axis=0, keepdims=True)
        if n > 0:
            state = st_ref[n]
            dq = dq + dot_nn(do, state) * entry
            if d_last is not None:
                d_last = d_last + keep * jnp.sum(d_state * state, axis=0, keepdims=True)
            d_state = d_state * keep + dot_tn(do, q * entry)
        dg = dot_nn(up_tri, q * dq - k * dk)
        if d_last is not None:
            dg = dg + d_last
        dq_ref[at, :] = dq
        dk_ref[at, :] = dk
        dv_ref[at, :] = dv
        dg_ref[at, :] = dg


KERNEL_PARAMS = pltpu.CompilerParams(vmem_limit_bytes=40 * 1024 * 1024)


def gla_fwd(q, k, v, g, seg_col, seg_row):
    length, width = v.shape
    count = length // CHUNK
    return pl.pallas_call(
        functools.partial(gla_fwd_kernel, count),
        out_shape=(
            jax.ShapeDtypeStruct((length, width), F32),
            jax.ShapeDtypeStruct((count, width, KH), F32),
        ),
        compiler_params=KERNEL_PARAMS,
        name="gla_fwd",
    )(q, k, v, g, seg_col, seg_row)


def gla_bwd(q, k, v, g, seg_col, seg_row, states, do):
    length, width = v.shape
    count = length // CHUNK
    return pl.pallas_call(
        functools.partial(gla_bwd_kernel, count),
        out_shape=(
            jax.ShapeDtypeStruct((length, KH), F32),
            jax.ShapeDtypeStruct((length, KH), F32),
            jax.ShapeDtypeStruct((length, width), F32),
            jax.ShapeDtypeStruct((length, KH), F32),
        ),
        compiler_params=KERNEL_PARAMS,
        name="gla_bwd",
    )(q, k, v, g, seg_col, seg_row, states, do)


def silu_parts(values):
    sig = 1.0 / (1.0 + jnp.exp(-values))
    return values * sig, sig * (1.0 + values * (1.0 - sig))


def out_weight(w_ref, col, block, dp, ctx, rows, out_cols):
    parts = []
    for i in range(dp):
        start = (i * ctx + block) * rows
        parts.append(w_ref[start : start + rows, col : col + out_cols])
    return jnp.concatenate(parts, axis=0)


def small_parts(head, w_ref, at, dims):
    _, _, dp, ctx, rows, _, up_cols = dims
    parts = []
    for j in range(KH // up_cols):
        start = pl.multiple_of(head * (ctx * rows), ctx * rows) + j * rows
        tile = w_ref[pl.ds(start, up_cols), at : at + 128]
        parts.append(tile[:, RANK : 2 * RANK + 1])
    return jnp.concatenate(parts, axis=0)


def project(dims, head, x_ref, w_ref, normed_ref, q_ref, k_ref, v_ref, gate_ref, low_ref, g_ref):
    attn_cols = dims[1]
    mix_cols = 2 * KH + 2 * VH
    gains = jnp.transpose(w_ref[:, mix_cols : mix_cols + 128].astype(F32))
    gains = gains[2 * RANK + 1 : 2 * RANK + 3, :]
    x = x_ref[...].astype(F32)
    unit = x * lax.rsqrt(jnp.mean(x * x, axis=-1, keepdims=True) + norm_eps)
    normed_ref[...] = (unit * gains[:1]).astype(BF)
    pre = mm(normed_ref[...], w_ref[:, :attn_cols])
    q_ref[...] = pre[:, :KH] * KH ** (-0.5)
    k_ref[...] = pre[:, KH : 2 * KH]
    v_ref[...] = pre[:, 2 * KH : 2 * KH + VH]
    gate_ref[...] = pre[:, 2 * KH + VH : mix_cols]
    low_ref[...] = pre[:, mix_cols : mix_cols + RANK].astype(BF)
    ups = small_parts(head, w_ref, mix_cols, dims)
    low_one = jnp.concatenate([low_ref[...], jnp.ones((x.shape[0], 1), BF)], axis=1)
    pre_f = mm_back(low_one, ups)
    g_ref[...] = (jnp.minimum(pre_f, 0.0) - jnp.log1p(jnp.exp(-jnp.abs(pre_f)))) / 16.0
    return gains, unit, ups, pre_f


def mixer_fwd_kernel(
    dims,
    head_ref,
    x_ref,
    w_ref,
    seg_col_ref,
    seg_row_ref,
    part_ref,
    gains_ref,
    mixed_ref,
    st_ref,
    normed_ref,
    q_ref,
    k_ref,
    v_ref,
    gate_ref,
    low_ref,
    g_ref,
):
    count, attn_cols, dp, ctx, rows, out_cols, _ = dims
    gains, _, _, _ = project(
        dims, head_ref[0], x_ref, w_ref, normed_ref, q_ref, k_ref, v_ref, gate_ref, low_ref, g_ref
    )
    gains_ref[...] = gains
    gla_fwd_kernel(
        count, q_ref, k_ref, v_ref, g_ref, seg_col_ref, seg_row_ref, mixed_ref, st_ref
    )
    mixed = mixed_ref[...]
    head_scale = lax.rsqrt(jnp.mean(mixed * mixed, axis=-1, keepdims=True) + head_eps)
    gated = (mixed * head_scale * silu_parts(gate_ref[...])[0]).astype(BF)
    for block in range(ctx):
        w_block = out_weight(w_ref, attn_cols, block, dp, ctx, rows, out_cols)
        part_ref[:, block * out_cols : (block + 1) * out_cols] = mm(gated, w_block).astype(BF)


def mixer_bwd_kernel(
    dims,
    head_ref,
    d_branch_ref,
    x_ref,
    w_ref,
    seg_col_ref,
    seg_row_ref,
    d_gain_ref,
    mixed_ref,
    st_ref,
    part_ref,
    grad_ref,
    normed_ref,
    q_ref,
    k_ref,
    v_ref,
    gate_ref,
    low_ref,
    g_ref,
    d_mixed_ref,
    dq_ref,
    dk_ref,
    dv_ref,
    dg_ref,
    d_pre_ref,
):
    count, attn_cols, dp, ctx, rows, out_cols, up_cols = dims
    half = ctx * rows // 2
    head = head_ref[0]
    _, unit, ups, pre_f = project(
        dims, head, x_ref, w_ref, normed_ref, q_ref, k_ref, v_ref, gate_ref, low_ref, g_ref
    )
    mixed = mixed_ref[...]
    head_scale = lax.rsqrt(jnp.mean(mixed * mixed, axis=-1, keepdims=True) + head_eps)
    normed = mixed * head_scale
    silu_gate, silu_slope = silu_parts(gate_ref[...])
    gated = (normed * silu_gate).astype(BF)
    d_gated = None
    for block in range(ctx):
        d_block = d_branch_ref[:, block * out_cols : (block + 1) * out_cols]
        w_block = out_weight(w_ref, attn_cols, block, dp, ctx, rows, out_cols)
        term = mm_back(d_block, w_block)
        d_gated = term if d_gated is None else d_gated + term
        grad_block = mm_rows(gated, d_block).astype(BF)
        side, spot = divmod(block, ctx // 2)
        for i in range(dp):
            start = (i * (ctx // 2) + spot) * rows
            grad_ref[side, start : start + rows, attn_cols:] = grad_block[
                i * rows : (i + 1) * rows
            ]
    d_normed = d_gated * silu_gate
    mix_cols = 2 * KH + 2 * VH
    d_pre_ref[:, 2 * KH + VH : mix_cols] = (d_gated * normed * silu_slope).astype(BF)
    inner = jnp.mean(d_normed * normed, axis=-1, keepdims=True)
    d_mixed_ref[...] = head_scale * (d_normed - normed * inner)
    gla_bwd_kernel(
        count,
        q_ref,
        k_ref,
        v_ref,
        g_ref,
        seg_col_ref,
        seg_row_ref,
        st_ref,
        d_mixed_ref,
        dq_ref,
        dk_ref,
        dv_ref,
        dg_ref,
    )
    d_forget = dg_ref[...] * (1.0 / (1.0 + jnp.exp(pre_f))) / 16.0
    ones = jnp.ones((d_forget.shape[0], 1), F32)
    grad_up = mm_rows(d_forget.astype(BF), low_ref[...])
    grad_bias = dot_tn(d_forget, ones)
    d_low = mm(d_forget.astype(BF), ups[:, :RANK]).astype(BF)
    d_pre_ref[:, :KH] = (dq_ref[...] * KH ** (-0.5)).astype(BF)
    d_pre_ref[:, KH : 2 * KH] = dk_ref[...].astype(BF)
    d_pre_ref[:, 2 * KH : 2 * KH + VH] = dv_ref[...].astype(BF)
    spare = jnp.zeros((d_low.shape[0], attn_cols - mix_cols - RANK), BF)
    d_pre_ref[:, mix_cols:] = jnp.concatenate([d_low, spare], axis=1)
    part = mm_back(d_pre_ref[...], w_ref[:, :attn_cols])
    part_ref[...] = part.astype(BF)

    model = part.shape[1]
    d_mix = jnp.sum(part * unit, axis=0, keepdims=True)
    gain_rows = jnp.concatenate([d_mix, d_gain_ref[...], jnp.zeros((6, model), F32)], axis=0)
    gain_cols = jnp.transpose(gain_rows)
    before = jnp.zeros((model, 2 * RANK + 1), F32)
    after = jnp.zeros((model, 128 - 2 * RANK - 3), F32)
    gain_tile = jnp.concatenate([before, gain_cols[:, :2], after], axis=1)
    for side in range(2):
        starts = [(2 * i + side) * half for i in range(dp)]
        own = jnp.concatenate([normed_ref[:, a : a + half] for a in starts], axis=1)
        grads = mm_rows(own, d_pre_ref[...])
        tile = jnp.concatenate([gain_tile[a : a + half] for a in starts], axis=0)
        grad_ref[side, :, :mix_cols] = grads[:, :mix_cols].astype(BF)
        grad_ref[side, :, mix_cols:attn_cols] = (grads[:, mix_cols:] + tile).astype(BF)
    pad_low = jnp.zeros((KH, RANK), F32)
    pad_high = jnp.zeros((KH, 128 - 2 * RANK - 1), F32)
    up_tile = jnp.concatenate([pad_low, grad_up, grad_bias, pad_high], axis=1).astype(BF)
    for j in range(KH // up_cols):
        side, spot = divmod(j, ctx // 2)
        at = pl.ds(pl.multiple_of(head * half, half) + spot * rows, up_cols)
        grad_ref[side, at, mix_cols:attn_cols] += up_tile[j * up_cols : (j + 1) * up_cols]


def mixer_call(kernel, name, shapes, scratch, operands):
    specs = [pl.BlockSpec(memory_space=pltpu.SMEM)]
    specs += [pl.BlockSpec(memory_space=pltpu.VMEM)] * (len(operands) - 1)
    return pl.pallas_call(
        kernel,
        in_specs=specs,
        out_specs=[pl.BlockSpec(memory_space=pltpu.VMEM)] * len(shapes),
        out_shape=[jax.ShapeDtypeStruct(*shape) for shape in shapes],
        scratch_shapes=[pltpu.VMEM(*shape) for shape in scratch],
        compiler_params=KERNEL_PARAMS,
        name=name,
    )(*operands)


def project_scratch(length, model):
    return [
        ((length, model), BF),
        ((length, KH), F32),
        ((length, KH), F32),
        ((length, VH), F32),
        ((length, VH), F32),
        ((length, RANK), BF),
        ((length, KH), F32),
    ]


def mixer_fwd(dims, head, x, w, seg_col, seg_row):
    length, model = x.shape
    shapes = [
        ((length, model), BF),
        ((2, model), F32),
        ((length, VH), F32),
        ((dims[0], VH, KH), F32),
    ]
    return mixer_call(
        functools.partial(mixer_fwd_kernel, dims),
        "mixer_fwd",
        shapes,
        project_scratch(length, model),
        (head, x, w, seg_col, seg_row),
    )


def mixer_bwd(dims, head, d_branch, x, w, seg_col, seg_row, d_gain, mixed, states):
    length, model = x.shape
    shapes = [((length, model), BF), ((2, w.shape[0] // 2, w.shape[1]), BF)]
    scratch = project_scratch(length, model) + [
        ((length, VH), F32),
        ((length, KH), F32),
        ((length, KH), F32),
        ((length, VH), F32),
        ((length, KH), F32),
        ((length, dims[1]), BF),
    ]
    return mixer_call(
        functools.partial(mixer_bwd_kernel, dims),
        "mixer_bwd",
        shapes,
        scratch,
        (head, d_branch, x, w, seg_col, seg_row, d_gain, mixed, states),
    )


def shift(block, distance):
    size = lax.axis_size("ctx")
    return lax.ppermute(block, "ctx", [(i, (i + distance) % size) for i in range(size)])


def gather_blocks(block):
    return [block] + [shift(block, s) for s in range(1, lax.axis_size("ctx"))]


def in_order(blocks):
    size, place = lax.axis_size("ctx"), lax.axis_index("ctx")
    rows = blocks[0].shape[0]
    whole = jnp.zeros((size * rows,) + blocks[0].shape[1:], blocks[0].dtype)
    for s, block in enumerate(blocks):
        whole = lax.dynamic_update_slice_in_dim(whole, block, ((place - s) % size) * rows, 0)
    return whole


def return_blocks(whole):
    size = lax.axis_size("ctx")
    rows = whole.shape[0] // size
    total = whole[:rows].astype(F32)
    for s in range(1, size):
        total = total + shift(whole[s * rows : (s + 1) * rows].astype(BF), -s).astype(F32)
    return total


def return_ordered(whole):
    size, place = lax.axis_size("ctx"), lax.axis_index("ctx")
    rows = whole.shape[0] // size
    total = lax.dynamic_slice_in_dim(whole, place * rows, rows, 0).astype(F32)
    for s in range(1, size):
        part = lax.dynamic_slice_in_dim(whole, ((place - s) % size) * rows, rows, 0)
        total = total + shift(part.astype(BF), -s).astype(F32)
    return total


def over_head(values, repeats):
    if repeats == 1:
        return values
    size = lax.axis_size("ctx")
    total = values
    for s in range(1, repeats):
        route = [(i, i - i % repeats + (i + s) % repeats) for i in range(size)]
        total = total + lax.ppermute(values, "ctx", route)
    return total


def transpose_devices(block):
    size = lax.axis_size("ctx")
    route = [(i * size + j, j * size + i) for i in range(size) for j in range(size)]
    return lax.ppermute(block, ("dp", "ctx"), route)


def swap_sections(block):
    return lax.ppermute(block, "section", [(0, 1), (1, 0)])


def hold(value, other):
    return lax.optimization_barrier((value, other))


def inv_rms(values):
    return lax.rsqrt(jnp.mean(values * values, axis=-1, keepdims=True) + norm_eps)


def norm_back(values, scale, gain, d_out):
    normed = values * scale
    d_normed = d_out * gain
    inner = jnp.mean(d_normed * normed, axis=-1, keepdims=True)
    return scale * (d_normed - normed * inner), jnp.sum(d_out * normed, axis=0)


def per_device(
    block_in,
    doc_lengths,
    w_query,
    w_key,
    w_value,
    forget_down,
    forget_up,
    forget_bias,
    w_gate,
    w_out,
    mix_gain,
    ffn_gain,
    ff_gate,
    ff_up,
    ff_down,
    out_grad,
):
    sections = lax.axis_size("section")
    dp, ctx = lax.axis_size("dp"), lax.axis_size("ctx")
    section, place = lax.axis_index("section"), lax.axis_index("ctx")
    first = section == 0
    owners = dp * ctx
    repeats = ctx // HEADS
    width = VH // repeats
    span = block_in.shape[2]
    model = block_in.shape[3]
    rows = w_query.shape[1]
    ff_rows = ff_down.shape[1]
    ff_own = ff_rows * dp
    ff_pad = -(-ff_own // 128) * 128
    up_cols = forget_up.shape[2]
    head = place // repeats

    def own_micro(array):
        return jnp.where(first, array[0], array[1])[0]

    lengths = own_micro(doc_lengths)
    begins = jnp.cumsum(lengths) - lengths
    positions = jnp.arange(span * ctx, dtype=jnp.int32)
    seg = jnp.sum((begins[None, :] <= positions[:, None]).astype(F32), axis=1)
    seg_col, seg_row = seg[:, None], seg[None, :]

    def head_blocks(shard):
        parts = shard[0].reshape(rows, HEADS, KH).transpose(1, 0, 2)
        return jnp.repeat(parts, repeats, axis=0) if repeats > 1 else parts

    def value_blocks(shard):
        return shard[0].reshape(rows, ctx, width).transpose(1, 0, 2)

    def hidden_blocks(shard):
        parts = shard[0].reshape(rows, dp, ctx, ff_rows).transpose(2, 0, 1, 3)
        parts = parts.reshape(ctx, rows, ff_own)
        return jnp.pad(parts, ((0, 0), (0, 0), (0, ff_pad - ff_own)))

    def to_all(block):
        return jnp.broadcast_to(block[None], (ctx,) + block.shape)

    up_rows = jnp.concatenate([forget_up[0].T, forget_bias[0][:, None]], axis=1)
    up_rows = jnp.pad(up_rows, ((0, rows - up_cols), (0, 0)))
    small = jnp.concatenate([up_rows, mix_gain[0][:, None], ffn_gain[0][:, None]], axis=1)
    small_cols = RANK + 3
    mix_cols = 2 * KH + 2 * width
    low_end = mix_cols + RANK
    small_end = low_end + small_cols
    attn_cols = -(-small_end // 128) * 128
    out_cols = model // ctx
    attn_send = jnp.concatenate(
        [
            head_blocks(w_query),
            head_blocks(w_key),
            value_blocks(w_value),
            value_blocks(w_gate),
            to_all(forget_down[0]),
            to_all(small),
            jnp.zeros((ctx, rows, attn_cols - small_end), BF),
        ],
        axis=2,
    )
    ff_send = jnp.concatenate([hidden_blocks(ff_gate), hidden_blocks(ff_up)], axis=2)

    half_rows = ctx * rows // 2
    half_cols = model // 2

    def exchange(send):
        got = lax.all_to_all(send, "ctx", 0, 0, tiled=True)
        return got.reshape(ctx * rows, send.shape[2])

    def layer_pieces(low, high):
        own = jnp.where(first, low, high)
        got = swap_sections(jnp.where(first, high, low))
        return jnp.where(first, own, got), jnp.where(first, got, own)

    def gathered(piece):
        return lax.all_gather(piece, "dp", axis=0, tiled=True)

    down_pieces = layer_pieces(ff_down[0][:, :half_cols], ff_down[0][:, half_cols:])
    down_piece = jnp.concatenate(down_pieces, axis=0)
    down_all = gathered(down_piece).reshape(dp, sections, ff_rows, half_cols)
    down_halves = [down_all[:, layer].reshape(ff_own, half_cols) for layer in range(sections)]

    out_block = transpose_devices(w_out[0]).reshape(rows, ctx, out_cols)
    out_block = out_block.transpose(1, 0, 2).reshape(ctx * rows, out_cols)
    attn_block = jnp.concatenate([exchange(attn_send), out_block], axis=1)
    attn_block = hold(attn_block, down_piece)[0]
    attn_pieces = layer_pieces(attn_block[:half_rows], attn_block[half_rows:])
    ff_block = exchange(hold(ff_send, attn_block)[0])
    ff_pieces = layer_pieces(ff_block[:half_rows], ff_block[half_rows:])

    attn_halves, ff_halves = [], []
    for layer in range(sections):
        attn_piece, ff_piece = attn_pieces[layer], ff_pieces[layer]
        if layer > 0:
            attn_piece, attn_halves[0] = hold(attn_piece, attn_halves[0])
            ff_piece, ff_halves[0] = hold(ff_piece, ff_halves[0])
        attn_halves.append(gathered(attn_piece))
        ff_halves.append(gathered(ff_piece))

    def both_halves(own):
        other = swap_sections(own)
        return jnp.where(first, own, other), jnp.where(first, other, own)

    def whole_rows(own):
        cols = own.shape[1]
        parts = [part.reshape(dp, 1, half_rows, cols) for part in both_halves(own)]
        return jnp.concatenate(parts, axis=1).reshape(model, cols)

    def whole_cols(own):
        return jnp.concatenate(both_halves(own), axis=1)

    def layer_smalls(w_attn):
        small = w_attn[:, low_end:small_end]
        ups = small[:, : RANK + 1].reshape(owners, rows, RANK + 1)[:, :up_cols]
        ups = ups.reshape(HEADS * KH, RANK + 1)
        gains = small[:, RANK + 1 :].T.astype(F32)
        return lax.dynamic_slice_in_dim(ups, head * KH, KH, 0), gains[:1], gains[1:]

    dims = (span * ctx // CHUNK, attn_cols, dp, ctx, rows, out_cols, up_cols)
    head_index = head.astype(jnp.int32)[None]

    def unpack_out(w_attn):
        out = w_attn[:, attn_cols:].reshape(dp, ctx, rows, out_cols)
        return out.transpose(0, 2, 1, 3).reshape(width, model)

    def mixer_forward(x_all, w_attn):
        if repeats == 1:
            part, gains, *kept = mixer_fwd(dims, head_index, x_all, w_attn, seg_col, seg_row)
            return part, gains, kept
        w_up, gain_in, gain_mid = layer_smalls(w_attn)
        x_all = x_all.astype(F32)
        normed_in = (x_all * inv_rms(x_all) * gain_in).astype(BF)
        pre = mm(normed_in, w_attn[:, :attn_cols])
        low_rank = pre[:, mix_cols:low_end].astype(BF)
        pre_f = mm_back(low_rank, w_up[:, :RANK]) + w_up[:, RANK].astype(F32)
        g = jax.nn.log_sigmoid(pre_f) / 16.0
        q = pre[:, :KH] * KH ** (-0.5)
        k = pre[:, KH : 2 * KH]
        v = pre[:, 2 * KH : 2 * KH + width]
        gate = pre[:, 2 * KH + width : mix_cols]
        mixed, states = gla_fwd(q, k, v, g, seg_col, seg_row)
        square = over_head(jnp.sum(mixed * mixed, axis=-1, keepdims=True), repeats)
        gated = mixed * lax.rsqrt(square / VH + head_eps) * silu_parts(gate)[0]
        gated = gated.astype(BF)
        part = mm(gated, unpack_out(w_attn)).astype(BF)
        gains = jnp.concatenate([gain_in, gain_mid], axis=0)
        kept = (w_up, normed_in, q, k, v, gate, low_rank, pre_f, g, mixed, states, gated)
        return part, gains, kept

    def mixer_backward(d_branch, w_attn, x_all, d_gain_mid, kept):
        if repeats == 1:
            return mixer_bwd(
                dims, head_index, d_branch, x_all, w_attn, seg_col, seg_row, d_gain_mid, *kept
            )
        w_up, normed_in, q, k, v, gate, low_rank, pre_f, g, mixed, states, gated = kept
        square = over_head(jnp.sum(mixed * mixed, axis=-1, keepdims=True), repeats)
        scale = lax.rsqrt(square / VH + head_eps)
        d_gated = mm_back(d_branch, unpack_out(w_attn))
        grad_out = mm_rows(gated, d_branch).astype(BF).reshape(dp, rows, ctx, out_cols)
        grad_out = grad_out.transpose(0, 2, 1, 3).reshape(model, out_cols)
        silu_gate, silu_slope = silu_parts(gate)
        normed = mixed * scale
        d_gate = d_gated * normed * silu_slope
        d_normed = d_gated * silu_gate
        inner = over_head(jnp.sum(d_normed * normed, axis=-1, keepdims=True), repeats) / VH
        d_mixed = scale * (d_normed - normed * inner)
        d_q, d_k, d_v, d_g = gla_bwd(q, k, v, g, seg_col, seg_row, states, d_mixed)
        d_forget = d_g * jax.nn.sigmoid(-pre_f) / 16.0
        grad_bias = jnp.sum(d_forget, axis=0)[:, None]
        d_forget = d_forget.astype(BF)
        grad_up = jnp.concatenate([mm_rows(d_forget, low_rank), grad_bias], axis=1)
        d_low = mm(d_forget, w_up[:, :RANK])
        spare = jnp.zeros((d_low.shape[0], attn_cols - low_end), F32)
        d_pre = [d_q * KH ** (-0.5), d_k, d_v, d_gate, d_low, spare]
        d_pre = jnp.concatenate([part.astype(BF) for part in d_pre], axis=1)
        part = mm_back(d_pre, w_attn[:, :attn_cols])
        x_all = x_all.astype(F32)
        grad_gain = jnp.sum(part * (x_all * inv_rms(x_all)), axis=0, keepdims=True)
        grads = jnp.concatenate([mm_rows(normed_in, d_pre).astype(BF), grad_out], axis=1)
        grads = grads.reshape(dp, 2, half_rows, attn_cols + out_cols).transpose(1, 0, 2, 3)
        grads = grads.reshape(2, dp * half_rows, attn_cols + out_cols)
        tiny = lax.dynamic_update_slice(
            jnp.zeros((owners, rows, RANK + 1), F32),
            grad_up.reshape(KH // up_cols, up_cols, RANK + 1),
            (head * (KH // up_cols), 0, 0),
        )
        tiny = jnp.concatenate(
            [tiny.reshape(model, RANK + 1), grad_gain.T, d_gain_mid.T], axis=1
        )
        tiny = tiny.astype(BF).reshape(dp, 2, half_rows, small_cols).transpose(1, 0, 2, 3)
        tiny = tiny.reshape(2, dp * half_rows, small_cols)
        return part.astype(BF), lax.dynamic_update_slice(grads, tiny, (0, 0, low_end))

    def forward(layer, x):
        x_all = in_order(gather_blocks(x))
        w_attn = whole_rows(attn_halves[layer])
        part, gains, mixer_kept = mixer_forward(x_all, w_attn)
        gain_in, gain_mid = gains[:1], gains[1:]
        part, ff_halves[layer] = hold(part, ff_halves[layer])
        w_ff = whole_rows(ff_halves[layer])
        w_down = whole_cols(down_halves[layer])
        middle = x.astype(F32) + return_ordered(part)
        scale_mid = inv_rms(middle)
        normed_mid = jnp.concatenate(
            gather_blocks((middle * scale_mid * gain_mid).astype(BF)), axis=0
        )
        ff_pre = mm(normed_mid, w_ff)
        if layer + 1 < sections:
            ff_pre, attn_halves[layer + 1] = hold(ff_pre, attn_halves[layer + 1])
        a, b = ff_pre[:, :ff_pad], ff_pre[:, ff_pad:]
        hidden = (silu_parts(a)[0] * b).astype(BF)[:, :ff_own]
        out = middle + return_blocks(mm(hidden, w_down))
        kept = (x_all, mixer_kept, middle, scale_mid, normed_mid, a, b, hidden)
        return out.astype(BF), (w_attn, w_ff, w_down, gain_in, gain_mid), kept

    def model_halves(array):
        low, high = [], []
        for i in range(dp):
            start = 2 * i * half_rows
            low.append(array[:, start : start + half_rows])
            high.append(array[:, start + half_rows : start + 2 * half_rows])
        low, high = jnp.concatenate(low, axis=1), jnp.concatenate(high, axis=1)
        return jnp.where(first, low, high), jnp.where(first, high, low)

    def over_dp(grad):
        return lax.psum_scatter(grad, "dp", scatter_dimension=0, tiled=True)

    def backward(layer, d_out, early, late):
        w_attn, w_ff, w_down, gain_in, gain_mid = weights[layer]
        x_all, mixer_kept, middle, scale_mid, normed_mid, a, b, hidden = layer_kept[layer]
        ff_keep, ff_send = model_halves(normed_mid)
        dff = jnp.concatenate(gather_blocks(d_out.astype(BF)), axis=0)
        d_hidden = jnp.pad(mm_back(dff, w_down), ((0, 0), (0, ff_pad - ff_own)))
        silu_a, slope_a = silu_parts(a)
        d_a = (d_hidden * b * slope_a).astype(BF)
        d_b = (d_hidden * silu_a).astype(BF)
        d_ab = jnp.concatenate([d_a, d_b], axis=1)
        d_normed_mid = return_blocks(mm_back(d_ab, w_ff))
        send_ff = mm_rows(ff_send, d_ab).astype(BF)
        grad_down = mm_rows(hidden, dff)
        down_low, down_high = grad_down[:, :half_cols], grad_down[:, half_cols:]
        if layer > 0:
            grad_down = grad_down.astype(BF)
        else:
            keep_down = jnp.where(first, down_low, down_high).astype(BF)
            grad_down = jnp.where(first, down_high, down_low).astype(BF)
        d_normed_mid, send_ff, grad_down, early = lax.optimization_barrier(
            (d_normed_mid, send_ff, grad_down, early)
        )
        got_ff = swap_sections(send_ff)
        if layer > 0:
            sum_down = over_dp(grad_down)
        else:
            got_down = swap_sections(grad_down)
            sum_down = (keep_down.astype(F32) + got_down.astype(F32)).astype(BF)
        d_mid_part, grad_gain_mid = norm_back(middle, scale_mid, gain_mid, d_normed_mid)
        d_middle = d_out + d_mid_part

        d_branch = in_order(gather_blocks(d_middle.astype(BF)))
        part, grad_attn = mixer_backward(d_branch, w_attn, x_all, grad_gain_mid[None], mixer_kept)
        send_attn = jnp.where(first, grad_attn[1], grad_attn[0])
        keep_attn = jnp.where(first, grad_attn[0], grad_attn[1])
        grad_ff = (mm_rows(ff_keep, d_ab) + got_ff.astype(F32)).astype(BF)
        if layer == 0:
            sum_down = over_dp(hold(sum_down, part)[0])
            late = over_dp(late)
        part, send_attn, late, grad_ff = lax.optimization_barrier(
            (part, send_attn, late, grad_ff)
        )
        grad_attn = keep_attn.astype(F32) + swap_sections(send_attn).astype(F32)
        grad_attn = grad_attn.astype(BF)
        d_normed_in = return_ordered(part)
        x_own = layer_x[layer].astype(F32)
        d_in_part, _ = norm_back(x_own, inv_rms(x_own), gain_in, d_normed_in)
        return d_middle + d_in_part, sum_down, over_dp(grad_ff), grad_attn, early, late

    x = own_micro(block_in)
    weights, layer_x, layer_kept, layer_y = [], [], [], []
    for layer in range(sections):
        layer_x.append(x)
        x, layer_weight, kept = forward(layer, x)
        weights.append(layer_weight)
        layer_kept.append(kept)
        layer_y.append(x)
    def to_owner(low, high, kind=None):
        mine = jnp.where(first, low, high)
        send = jnp.where(first, high, low)
        return mine, swap_sections(send if kind is None else send.astype(kind))

    def both(low, high):
        mine, other = to_owner(low, high)
        return jnp.stack([jnp.where(first, mine, other), jnp.where(first, other, mine)])

    outputs = both(*layer_y)
    d_x = own_micro(out_grad).astype(F32)
    d_in, down_high, ff_high, attn_high, _, outputs = backward(1, d_x, (), outputs)
    upstream = d_in.astype(BF).astype(F32)
    d_first, down_low, ff_low, attn_low, early, attn_high = backward(
        0, upstream, (attn_high, down_high, ff_high), attn_high
    )
    _, down_high, ff_high = early
    attn_low = over_dp(attn_low)

    def halves_of_owner(low, high):
        mine, other = to_owner(low, high)
        return jnp.where(first, mine, other), jnp.where(first, other, mine)

    def to_rows(array):
        cols = array.shape[1]
        return lax.all_to_all(array.reshape(ctx, rows, cols), "ctx", 0, 0, tiled=True).astype(F32)

    def summed(low, high):
        mine, other = to_owner(low, high)
        return mine.astype(F32) + other.astype(F32)

    mine, other = to_owner(d_first, d_in, BF)
    other = other.astype(F32)
    input_grads = jnp.stack([jnp.where(first, mine, other), jnp.where(first, other, mine)])
    got = swap_sections(jnp.where(first, down_high, jnp.pad(down_low, ((0, 0), (0, half_cols)))))
    own_low = jnp.concatenate([down_low, got[:, :half_cols]], axis=1).astype(F32)
    own_down = jnp.where(first, own_low, down_high.astype(F32) + got.astype(F32))
    own_ff = to_rows(jnp.concatenate(halves_of_owner(ff_low, ff_high), axis=0))
    attn_low, own_down, own_ff, input_grads = lax.optimization_barrier(
        (attn_low, own_down, own_ff, input_grads)
    )

    half_ctx = ctx // 2
    pieces = jnp.stack([attn_low[:, :attn_cols], attn_high[:, :attn_cols]])
    pieces = pieces.reshape(ctx, rows, attn_cols)
    arrived = []
    for step in range(ctx):
        route = []
        for s in range(sections):
            for j in range(ctx):
                to_layer, k = divmod((j + step) % ctx, half_ctx)
                route.append((s * ctx + j, to_layer * ctx + s * half_ctx + k))
        piece = lax.dynamic_index_in_dim(pieces, (place + step) % ctx, 0, False)
        arrived.append(lax.ppermute(piece, ("section", "ctx"), route))
    arrived = jnp.stack(arrived)
    mine = section * half_ctx + place % half_ctx
    own_attn = jnp.stack(
        [
            lax.dynamic_index_in_dim(arrived, (mine - source) % ctx, 0, False)
            for source in range(ctx)
        ]
    ).astype(F32)
    outs = jnp.stack([attn_low[:, attn_cols:], attn_high[:, attn_cols:]])
    came = []
    for step in range(sections):
        route = []
        for s in range(sections):
            for i in range(dp):
                for j in range(ctx):
                    to_layer = (s + step) % sections
                    route.append(((s * dp + i) * ctx + j, (to_layer * ctx + j) * dp + i))
        block = lax.dynamic_index_in_dim(outs, (section + step) % sections, 0, False)
        came.append(lax.ppermute(block, ("section", "dp", "ctx"), route))
    out_halves = [jnp.where(first, came[0], came[1]), jnp.where(first, came[1], came[0])]
    own_out = jnp.concatenate(out_halves, axis=0).reshape(ctx, rows, out_cols)
    own_out = own_out.transpose(1, 0, 2).reshape(rows, model).astype(F32)

    def hidden_whole(parts):
        parts = parts.reshape(ctx, rows, dp, ff_rows).transpose(1, 2, 0, 3)
        return parts.reshape(rows, owners * ff_rows)

    def head_whole(parts):
        parts = parts.reshape(HEADS, repeats, rows, KH).sum(1)
        return parts.transpose(1, 0, 2).reshape(rows, HEADS * KH)

    def value_whole(parts):
        return parts.transpose(1, 0, 2).reshape(rows, HEADS * VH)

    tiny = jnp.sum(own_attn[:, :, low_end:small_end], axis=0)
    return (
        outputs[None, :, None],
        input_grads[None, :, None],
        head_whole(own_attn[:, :, :KH])[None],
        head_whole(own_attn[:, :, KH : 2 * KH])[None],
        value_whole(own_attn[:, :, 2 * KH : 2 * KH + width])[None],
        jnp.sum(own_attn[:, :, mix_cols:low_end], axis=0)[None],
        tiny[:up_cols, :RANK].T[None],
        tiny[:up_cols, RANK][None],
        value_whole(own_attn[:, :, 2 * KH + width : mix_cols])[None],
        own_out[None],
        tiny[:, RANK + 1][None],
        tiny[:, RANK + 2][None],
        hidden_whole(own_ff[:, :, :ff_own])[None],
        hidden_whole(own_ff[:, :, ff_pad : ff_pad + ff_own])[None],
        own_down[None],
    )


def solution(mesh):
    rows = P("section", ("dp", "ctx"), None)
    columns = P("section", None, ("dp", "ctx"))
    vector = P("section", ("dp", "ctx"))
    tokens = P(None, "dp", "ctx", None)
    stacked = P("section", None, "dp", "ctx", None)
    return jax.shard_map(
        per_device,
        mesh=mesh,
        in_specs=(
            tokens,
            P(None, "dp", None),
            rows,
            rows,
            rows,
            rows,
            columns,
            vector,
            rows,
            rows,
            vector,
            vector,
            rows,
            rows,
            rows,
            tokens,
        ),
        out_specs=(
            stacked,
            stacked,
            rows,
            rows,
            rows,
            rows,
            columns,
            vector,
            rows,
            rows,
            vector,
            vector,
            rows,
            rows,
            rows,
        ),
        check_vma=False,
    )
```

```python
import functools

import jax
import jax.numpy as jnp
from jax import lax
from jax.experimental import pallas as pl
from jax.experimental.pallas import tpu as pltpu
from jax.sharding import PartitionSpec as P

HEADS = 4
KH = 128
VH = 256
RANK = 16
STRETCH = 64
CHUNK = 2 * STRETCH

norm_eps = 1e-06
head_eps = 0.1
BF = jnp.bfloat16
F32 = jnp.float32
highest = lax.Precision.HIGHEST


def mm(left, right):
    return jnp.dot(left, right, preferred_element_type=F32)


def mm_back(left, right):
    return lax.dot_general(left, right, (((1,), (1,)), ((), ())), preferred_element_type=F32)


def mm_rows(left, right):
    return lax.dot_general(left, right, (((0,), (0,)), ((), ())), preferred_element_type=F32)


def dot_nn(a, b):
    return lax.dot_general(
        a, b, (((1,), (0,)), ((), ())), precision=highest, preferred_element_type=F32
    )


def dot_nt(a, b):
    return lax.dot_general(
        a, b, (((1,), (1,)), ((), ())), precision=highest, preferred_element_type=F32
    )


def dot_tn(a, b):
    return lax.dot_general(
        a, b, (((0,), (0,)), ((), ())), precision=highest, preferred_element_type=F32
    )


def chunk_parts(n, q_ref, k_ref, g_ref, seg_col_ref, seg_row_ref, low_tri):
    at = pl.ds(n * CHUNK, CHUNK)
    summed = dot_nn(low_tri, g_ref[at, :])
    middle = summed[STRETCH - 1 : STRETCH, :]
    last = summed[CHUNK - 1 : CHUNK, :]
    seg = seg_col_ref[at, :]
    seg_last = seg[CHUNK - 1 : CHUNK, :]
    seg_row = seg_row_ref[:, at]
    if n > 0:
        seg_prev = seg_col_ref[pl.ds(n * CHUNK - 1, 1), :]
    else:
        seg_prev = jnp.full((1, 1), -1.0, F32)
    up = jnp.exp(summed - middle)
    down = jnp.exp(middle - summed)
    entry = jnp.where(seg == seg_prev, jnp.exp(summed), 0.0)
    tail = jnp.where(seg == seg_last, jnp.exp(last - summed), 0.0)
    keep = jnp.where(seg_last == seg_prev, jnp.exp(last), 0.0)
    return at, seg, seg_row, up, down, entry, tail, keep


def tri_masks():
    rows = lax.broadcasted_iota(jnp.int32, (CHUNK, CHUNK), 0)
    cols = lax.broadcasted_iota(jnp.int32, (CHUNK, CHUNK), 1)
    return rows >= cols, rows <= cols


def gla_fwd_kernel(count, q_ref, k_ref, v_ref, g_ref, seg_col_ref, seg_row_ref, mixed_ref, st_ref):
    lower, _ = tri_masks()
    low_tri = lower.astype(F32)
    state = jnp.zeros(st_ref.shape[1:], F32)
    for n in range(count):
        at, seg, seg_row, up, down, entry, tail, keep = chunk_parts(
            n, q_ref, k_ref, g_ref, seg_col_ref, seg_row_ref, low_tri
        )
        q, k, v = q_ref[at, :], k_ref[at, :], v_ref[at, :]
        scores = dot_nt(q * up, k * down)
        scores = jnp.where(lower & (seg == seg_row), scores, 0.0)
        out = dot_nn(scores, v)
        st_ref[n] = state
        if n > 0:
            out = out + dot_nt(q * entry, state)
        mixed_ref[at, :] = out
        if n + 1 < count:
            state = state * keep + dot_tn(v, k * tail)


def gla_bwd_kernel(
    count,
    q_ref,
    k_ref,
    v_ref,
    g_ref,
    seg_col_ref,
    seg_row_ref,
    st_ref,
    do_ref,
    dq_ref,
    dk_ref,
    dv_ref,
    dg_ref,
):
    lower, upper = tri_masks()
    low_tri = lower.astype(F32)
    up_tri = upper.astype(F32)
    d_state = jnp.zeros(st_ref.shape[1:], F32)
    for n in reversed(range(count)):
        at, seg, seg_row, up, down, entry, tail, keep = chunk_parts(
            n, q_ref, k_ref, g_ref, seg_col_ref, seg_row_ref, low_tri
        )
        q, k, v, do = q_ref[at, :], k_ref[at, :], v_ref[at, :], do_ref[at, :]
        mask = lower & (seg == seg_row)
        q_up, k_down = q * up, k * down
        scores = jnp.where(mask, dot_nt(q_up, k_down), 0.0)
        d_scores = jnp.where(mask, dot_nt(do, v), 0.0)
        dq = dot_nn(d_scores, k_down) * up
        dk = dot_tn(d_scores, q_up) * down
        dv = dot_tn(scores, do)
        d_last = None
        if n + 1 < count:
            k_tail = k * tail
            dk_tail = dot_nn(v, d_state)
            dk = dk + dk_tail * tail
            dv = dv + dot_nt(k_tail, d_state)
            d_last = jnp.sum(dk_tail * k_tail, axis=0, keepdims=True)
        if n > 0:
            state = st_ref[n]
            dq = dq + dot_nn(do, state) * entry
            if d_last is not None:
                d_last = d_last + keep * jnp.sum(d_state * state, axis=0, keepdims=True)
            d_state = d_state * keep + dot_tn(do, q * entry)
        dg = dot_nn(up_tri, q * dq - k * dk)
        if d_last is not None:
            dg = dg + d_last
        dq_ref[at, :] = dq
        dk_ref[at, :] = dk
        dv_ref[at, :] = dv
        dg_ref[at, :] = dg


KERNEL_PARAMS = pltpu.CompilerParams(vmem_limit_bytes=40 * 1024 * 1024)


def gla_fwd(q, k, v, g, seg_col, seg_row):
    length, width = v.shape
    count = length // CHUNK
    return pl.pallas_call(
        functools.partial(gla_fwd_kernel, count),
        out_shape=(
            jax.ShapeDtypeStruct((length, width), F32),
            jax.ShapeDtypeStruct((count, width, KH), F32),
        ),
        compiler_params=KERNEL_PARAMS,
        name="gla_fwd",
    )(q, k, v, g, seg_col, seg_row)


def gla_bwd(q, k, v, g, seg_col, seg_row, states, do):
    length, width = v.shape
    count = length // CHUNK
    return pl.pallas_call(
        functools.partial(gla_bwd_kernel, count),
        out_shape=(
            jax.ShapeDtypeStruct((length, KH), F32),
            jax.ShapeDtypeStruct((length, KH), F32),
            jax.ShapeDtypeStruct((length, width), F32),
            jax.ShapeDtypeStruct((length, KH), F32),
        ),
        compiler_params=KERNEL_PARAMS,
        name="gla_bwd",
    )(q, k, v, g, seg_col, seg_row, states, do)


def silu_parts(values):
    sig = 1.0 / (1.0 + jnp.exp(-values))
    return values * sig, sig * (1.0 + values * (1.0 - sig))


def out_weight(w_ref, col, block, dp, ctx, rows, out_cols):
    parts = []
    for i in range(dp):
        start = (i * ctx + block) * rows
        parts.append(w_ref[start : start + rows, col : col + out_cols])
    return jnp.concatenate(parts, axis=0)


def small_parts(head, w_ref, at, dims):
    _, _, dp, ctx, rows, _, up_cols = dims
    parts = []
    for j in range(KH // up_cols):
        start = pl.multiple_of(head * (ctx * rows), ctx * rows) + j * rows
        tile = w_ref[pl.ds(start, up_cols), at : at + 128]
        parts.append(tile[:, RANK : 2 * RANK + 1])
    return jnp.concatenate(parts, axis=0)


def project(dims, head, x_ref, w_ref, normed_ref, q_ref, k_ref, v_ref, gate_ref, low_ref, g_ref):
    attn_cols = dims[1]
    mix_cols = 2 * KH + 2 * VH
    gains = jnp.transpose(w_ref[:, mix_cols : mix_cols + 128].astype(F32))
    gains = gains[2 * RANK + 1 : 2 * RANK + 3, :]
    x = x_ref[...].astype(F32)
    unit = x * lax.rsqrt(jnp.mean(x * x, axis=-1, keepdims=True) + norm_eps)
    normed_ref[...] = (unit * gains[:1]).astype(BF)
    pre = mm(normed_ref[...], w_ref[:, :attn_cols])
    q_ref[...] = pre[:, :KH] * KH ** (-0.5)
    k_ref[...] = pre[:, KH : 2 * KH]
    v_ref[...] = pre[:, 2 * KH : 2 * KH + VH]
    gate_ref[...] = pre[:, 2 * KH + VH : mix_cols]
    low_ref[...] = pre[:, mix_cols : mix_cols + RANK].astype(BF)
    ups = small_parts(head, w_ref, mix_cols, dims)
    low_one = jnp.concatenate([low_ref[...], jnp.ones((x.shape[0], 1), BF)], axis=1)
    pre_f = mm_back(low_one, ups)
    g_ref[...] = (jnp.minimum(pre_f, 0.0) - jnp.log1p(jnp.exp(-jnp.abs(pre_f)))) / 16.0
    return gains, unit, ups, pre_f


def mixer_fwd_kernel(
    dims,
    head_ref,
    x_ref,
    w_ref,
    seg_col_ref,
    seg_row_ref,
    part_ref,
    gains_ref,
    mixed_ref,
    st_ref,
    normed_ref,
    q_ref,
    k_ref,
    v_ref,
    gate_ref,
    low_ref,
    g_ref,
):
    count, attn_cols, dp, ctx, rows, out_cols, _ = dims
    gains, _, _, _ = project(
        dims, head_ref[0], x_ref, w_ref, normed_ref, q_ref, k_ref, v_ref, gate_ref, low_ref, g_ref
    )
    gains_ref[...] = gains
    gla_fwd_kernel(
        count, q_ref, k_ref, v_ref, g_ref, seg_col_ref, seg_row_ref, mixed_ref, st_ref
    )
    mixed = mixed_ref[...]
    head_scale = lax.rsqrt(jnp.mean(mixed * mixed, axis=-1, keepdims=True) + head_eps)
    gated = (mixed * head_scale * silu_parts(gate_ref[...])[0]).astype(BF)
    for block in range(ctx):
        w_block = out_weight(w_ref, attn_cols, block, dp, ctx, rows, out_cols)
        part_ref[:, block * out_cols : (block + 1) * out_cols] = mm(gated, w_block).astype(BF)


def mixer_bwd_kernel(
    dims,
    head_ref,
    d_branch_ref,
    x_ref,
    w_ref,
    seg_col_ref,
    seg_row_ref,
    d_gain_ref,
    mixed_ref,
    st_ref,
    part_ref,
    grad_ref,
    normed_ref,
    q_ref,
    k_ref,
    v_ref,
    gate_ref,
    low_ref,
    g_ref,
    d_mixed_ref,
    dq_ref,
    dk_ref,
    dv_ref,
    dg_ref,
    d_pre_ref,
):
    count, attn_cols, dp, ctx, rows, out_cols, up_cols = dims
    half = ctx * rows // 2
    head = head_ref[0]
    _, unit, ups, pre_f = project(
        dims, head, x_ref, w_ref, normed_ref, q_ref, k_ref, v_ref, gate_ref, low_ref, g_ref
    )
    mixed = mixed_ref[...]
    head_scale = lax.rsqrt(jnp.mean(mixed * mixed, axis=-1, keepdims=True) + head_eps)
    normed = mixed * head_scale
    silu_gate, silu_slope = silu_parts(gate_ref[...])
    gated = (normed * silu_gate).astype(BF)
    d_gated = None
    for block in range(ctx):
        d_block = d_branch_ref[:, block * out_cols : (block + 1) * out_cols]
        w_block = out_weight(w_ref, attn_cols, block, dp, ctx, rows, out_cols)
        term = mm_back(d_block, w_block)
        d_gated = term if d_gated is None else d_gated + term
        grad_block = mm_rows(gated, d_block).astype(BF)
        side, spot = divmod(block, ctx // 2)
        for i in range(dp):
            start = (i * (ctx // 2) + spot) * rows
            grad_ref[side, start : start + rows, attn_cols:] = grad_block[
                i * rows : (i + 1) * rows
            ]
    d_normed = d_gated * silu_gate
    mix_cols = 2 * KH + 2 * VH
    d_pre_ref[:, 2 * KH + VH : mix_cols] = (d_gated * normed * silu_slope).astype(BF)
    inner = jnp.mean(d_normed * normed, axis=-1, keepdims=True)
    d_mixed_ref[...] = head_scale * (d_normed - normed * inner)
    gla_bwd_kernel(
        count,
        q_ref,
        k_ref,
        v_ref,
        g_ref,
        seg_col_ref,
        seg_row_ref,
        st_ref,
        d_mixed_ref,
        dq_ref,
        dk_ref,
        dv_ref,
        dg_ref,
    )
    d_forget = dg_ref[...] * (1.0 / (1.0 + jnp.exp(pre_f))) / 16.0
    ones = jnp.ones((d_forget.shape[0], 1), F32)
    grad_up = mm_rows(d_forget.astype(BF), low_ref[...])
    grad_bias = dot_tn(d_forget, ones)
    d_low = mm(d_forget.astype(BF), ups[:, :RANK]).astype(BF)
    d_pre_ref[:, :KH] = (dq_ref[...] * KH ** (-0.5)).astype(BF)
    d_pre_ref[:, KH : 2 * KH] = dk_ref[...].astype(BF)
    d_pre_ref[:, 2 * KH : 2 * KH + VH] = dv_ref[...].astype(BF)
    spare = jnp.zeros((d_low.shape[0], attn_cols - mix_cols - RANK), BF)
    d_pre_ref[:, mix_cols:] = jnp.concatenate([d_low, spare], axis=1)
    part = mm_back(d_pre_ref[...], w_ref[:, :attn_cols])
    part_ref[...] = part.astype(BF)

    model = part.shape[1]
    d_mix = jnp.sum(part * unit, axis=0, keepdims=True)
    gain_rows = jnp.concatenate([d_mix, d_gain_ref[...], jnp.zeros((6, model), F32)], axis=0)
    gain_cols = jnp.transpose(gain_rows)
    before = jnp.zeros((model, 2 * RANK + 1), F32)
    after = jnp.zeros((model, 128 - 2 * RANK - 3), F32)
    gain_tile = jnp.concatenate([before, gain_cols[:, :2], after], axis=1)
    for side in range(2):
        starts = [(2 * i + side) * half for i in range(dp)]
        own = jnp.concatenate([normed_ref[:, a : a + half] for a in starts], axis=1)
        grads = mm_rows(own, d_pre_ref[...])
        tile = jnp.concatenate([gain_tile[a : a + half] for a in starts], axis=0)
        grad_ref[side, :, :mix_cols] = grads[:, :mix_cols].astype(BF)
        grad_ref[side, :, mix_cols:attn_cols] = (grads[:, mix_cols:] + tile).astype(BF)
    pad_low = jnp.zeros((KH, RANK), F32)
    pad_high = jnp.zeros((KH, 128 - 2 * RANK - 1), F32)
    up_tile = jnp.concatenate([pad_low, grad_up, grad_bias, pad_high], axis=1).astype(BF)
    for j in range(KH // up_cols):
        side, spot = divmod(j, ctx // 2)
        at = pl.ds(pl.multiple_of(head * half, half) + spot * rows, up_cols)
        grad_ref[side, at, mix_cols:attn_cols] += up_tile[j * up_cols : (j + 1) * up_cols]


def mixer_call(kernel, name, shapes, scratch, operands):
    specs = [pl.BlockSpec(memory_space=pltpu.SMEM)]
    specs += [pl.BlockSpec(memory_space=pltpu.VMEM)] * (len(operands) - 1)
    return pl.pallas_call(
        kernel,
        in_specs=specs,
        out_specs=[pl.BlockSpec(memory_space=pltpu.VMEM)] * len(shapes),
        out_shape=[jax.ShapeDtypeStruct(*shape) for shape in shapes],
        scratch_shapes=[pltpu.VMEM(*shape) for shape in scratch],
        compiler_params=KERNEL_PARAMS,
        name=name,
    )(*operands)


def project_scratch(length, model):
    return [
        ((length, model), BF),
        ((length, KH), F32),
        ((length, KH), F32),
        ((length, VH), F32),
        ((length, VH), F32),
        ((length, RANK), BF),
        ((length, KH), F32),
    ]


def mixer_fwd(dims, head, x, w, seg_col, seg_row):
    length, model = x.shape
    shapes = [
        ((length, model), BF),
        ((2, model), F32),
        ((length, VH), F32),
        ((dims[0], VH, KH), F32),
    ]
    return mixer_call(
        functools.partial(mixer_fwd_kernel, dims),
        "mixer_fwd",
        shapes,
        project_scratch(length, model),
        (head, x, w, seg_col, seg_row),
    )


def mixer_bwd(dims, head, d_branch, x, w, seg_col, seg_row, d_gain, mixed, states):
    length, model = x.shape
    shapes = [((length, model), BF), ((2, w.shape[0] // 2, w.shape[1]), BF)]
    scratch = project_scratch(length, model) + [
        ((length, VH), F32),
        ((length, KH), F32),
        ((length, KH), F32),
        ((length, VH), F32),
        ((length, KH), F32),
        ((length, dims[1]), BF),
    ]
    return mixer_call(
        functools.partial(mixer_bwd_kernel, dims),
        "mixer_bwd",
        shapes,
        scratch,
        (head, d_branch, x, w, seg_col, seg_row, d_gain, mixed, states),
    )


def shift(block, distance):
    size = lax.axis_size("ctx")
    return lax.ppermute(block, "ctx", [(i, (i + distance) % size) for i in range(size)])


def gather_blocks(block):
    return [block] + [shift(block, s) for s in range(1, lax.axis_size("ctx"))]


def in_order(blocks):
    size, place = lax.axis_size("ctx"), lax.axis_index("ctx")
    rows = blocks[0].shape[0]
    whole = jnp.zeros((size * rows,) + blocks[0].shape[1:], blocks[0].dtype)
    for s, block in enumerate(blocks):
        whole = lax.dynamic_update_slice_in_dim(whole, block, ((place - s) % size) * rows, 0)
    return whole


def return_blocks(whole):
    size = lax.axis_size("ctx")
    rows = whole.shape[0] // size
    total = whole[:rows].astype(F32)
    for s in range(1, size):
        total = total + shift(whole[s * rows : (s + 1) * rows].astype(BF), -s).astype(F32)
    return total


def return_ordered(whole):
    size, place = lax.axis_size("ctx"), lax.axis_index("ctx")
    rows = whole.shape[0] // size
    total = lax.dynamic_slice_in_dim(whole, place * rows, rows, 0).astype(F32)
    for s in range(1, size):
        part = lax.dynamic_slice_in_dim(whole, ((place - s) % size) * rows, rows, 0)
        total = total + shift(part.astype(BF), -s).astype(F32)
    return total


def over_head(values, repeats):
    if repeats == 1:
        return values
    size = lax.axis_size("ctx")
    total = values
    for s in range(1, repeats):
        route = [(i, i - i % repeats + (i + s) % repeats) for i in range(size)]
        total = total + lax.ppermute(values, "ctx", route)
    return total


def transpose_devices(block):
    size = lax.axis_size("ctx")
    route = [(i * size + j, j * size + i) for i in range(size) for j in range(size)]
    return lax.ppermute(block, ("dp", "ctx"), route)


def swap_sections(block):
    return lax.ppermute(block, "section", [(0, 1), (1, 0)])


def hold(value, other):
    return lax.optimization_barrier((value, other))


def inv_rms(values):
    return lax.rsqrt(jnp.mean(values * values, axis=-1, keepdims=True) + norm_eps)


def norm_back(values, scale, gain, d_out):
    normed = values * scale
    d_normed = d_out * gain
    inner = jnp.mean(d_normed * normed, axis=-1, keepdims=True)
    return scale * (d_normed - normed * inner), jnp.sum(d_out * normed, axis=0)


def per_device(
    block_in,
    doc_lengths,
    w_query,
    w_key,
    w_value,
    forget_down,
    forget_up,
    forget_bias,
    w_gate,
    w_out,
    mix_gain,
    ffn_gain,
    ff_gate,
    ff_up,
    ff_down,
    out_grad,
):
    sections = lax.axis_size("section")
    dp, ctx = lax.axis_size("dp"), lax.axis_size("ctx")
    section, place = lax.axis_index("section"), lax.axis_index("ctx")
    first = section == 0
    owners = dp * ctx
    repeats = ctx // HEADS
    width = VH // repeats
    span = block_in.shape[2]
    model = block_in.shape[3]
    rows = w_query.shape[1]
    ff_rows = ff_down.shape[1]
    ff_own = ff_rows * dp
    ff_pad = -(-ff_own // 128) * 128
    up_cols = forget_up.shape[2]
    head = place // repeats

    def own_micro(array):
        return jnp.where(first, array[0], array[1])[0]

    lengths = own_micro(doc_lengths)
    begins = jnp.cumsum(lengths) - lengths
    positions = jnp.arange(span * ctx, dtype=jnp.int32)
    seg = jnp.sum((begins[None, :] <= positions[:, None]).astype(F32), axis=1)
    seg_col, seg_row = seg[:, None], seg[None, :]

    def head_blocks(shard):
        parts = shard[0].reshape(rows, HEADS, KH).transpose(1, 0, 2)
        return jnp.repeat(parts, repeats, axis=0) if repeats > 1 else parts

    def value_blocks(shard):
        return shard[0].reshape(rows, ctx, width).transpose(1, 0, 2)

    def hidden_blocks(shard):
        parts = shard[0].reshape(rows, dp, ctx, ff_rows).transpose(2, 0, 1, 3)
        parts = parts.reshape(ctx, rows, ff_own)
        return jnp.pad(parts, ((0, 0), (0, 0), (0, ff_pad - ff_own)))

    def to_all(block):
        return jnp.broadcast_to(block[None], (ctx,) + block.shape)

    up_rows = jnp.concatenate([forget_up[0].T, forget_bias[0][:, None]], axis=1)
    up_rows = jnp.pad(up_rows, ((0, rows - up_cols), (0, 0)))
    small = jnp.concatenate([up_rows, mix_gain[0][:, None], ffn_gain[0][:, None]], axis=1)
    small_cols = RANK + 3
    mix_cols = 2 * KH + 2 * width
    low_end = mix_cols + RANK
    small_end = low_end + small_cols
    attn_cols = -(-small_end // 128) * 128
    out_cols = model // ctx
    attn_send = jnp.concatenate(
        [
            head_blocks(w_query),
            head_blocks(w_key),
            value_blocks(w_value),
            value_blocks(w_gate),
            to_all(forget_down[0]),
            to_all(small),
            jnp.zeros((ctx, rows, attn_cols - small_end), BF),
        ],
        axis=2,
    )
    ff_send = jnp.concatenate([hidden_blocks(ff_gate), hidden_blocks(ff_up)], axis=2)

    half_rows = ctx * rows // 2
    half_cols = model // 2

    def exchange(send):
        got = lax.all_to_all(send, "ctx", 0, 0, tiled=True)
        return got.reshape(ctx * rows, send.shape[2])

    def layer_pieces(low, high):
        own = jnp.where(first, low, high)
        got = swap_sections(jnp.where(first, high, low))
        return jnp.where(first, own, got), jnp.where(first, got, own)

    def whole_block(own, low_half):
        high_half = lax.ppermute(own[half_rows:], "section", [(1, 0)])
        return jnp.where(first, jnp.concatenate([low_half, high_half], axis=0), own)

    def gathered(piece):
        return lax.all_gather(piece, "dp", axis=0, tiled=True)

    def gathered_direct(piece):
        place_dp = lax.axis_index("dp")
        size = piece.shape[0]
        whole = jnp.zeros((dp * size, piece.shape[1]), piece.dtype)
        whole = lax.dynamic_update_slice_in_dim(whole, piece, place_dp * size, 0)
        for step in range(1, dp):
            route = [(i, (i + step) % dp) for i in range(dp)]
            block = lax.ppermute(piece, "dp", route)
            start = ((place_dp - step) % dp) * size
            whole = lax.dynamic_update_slice_in_dim(whole, block, start, 0)
        return whole

    down_pieces = layer_pieces(ff_down[0][:, :half_cols], ff_down[0][:, half_cols:])
    down_piece = jnp.concatenate(down_pieces, axis=0)
    down_all = gathered_direct(down_piece).reshape(dp, sections, ff_rows, half_cols)
    down_halves = [down_all[:, layer].reshape(ff_own, half_cols) for layer in range(sections)]

    out_block = transpose_devices(w_out[0]).reshape(rows, ctx, out_cols)
    out_block = out_block.transpose(1, 0, 2).reshape(ctx * rows, out_cols)
    attn_block = jnp.concatenate([exchange(attn_send), out_block], axis=1)
    attn_block = hold(attn_block, down_piece)[0]
    attn_pieces = layer_pieces(attn_block[:half_rows], attn_block[half_rows:])
    attn_high = whole_block(attn_block, attn_pieces[1])
    ff_block = exchange(hold(ff_send, attn_block)[0])
    ff_pieces = layer_pieces(ff_block[:half_rows], ff_block[half_rows:])
    ff_high = whole_block(ff_block, ff_pieces[1])

    attn_half, ff_half = gathered(attn_pieces[0]), gathered(ff_pieces[0])
    attn_high, attn_half = hold(attn_high, attn_half)
    ff_high, ff_half = hold(ff_high, ff_half)
    attn_high, ff_high = gathered(attn_high), gathered(ff_high)

    def both_halves(own):
        other = swap_sections(own)
        return jnp.where(first, own, other), jnp.where(first, other, own)

    def whole_rows(own):
        cols = own.shape[1]
        parts = [part.reshape(dp, 1, half_rows, cols) for part in both_halves(own)]
        return jnp.concatenate(parts, axis=1).reshape(model, cols)

    def whole_cols(own):
        return jnp.concatenate(both_halves(own), axis=1)

    def layer_smalls(w_attn):
        small = w_attn[:, low_end:small_end]
        ups = small[:, : RANK + 1].reshape(owners, rows, RANK + 1)[:, :up_cols]
        ups = ups.reshape(HEADS * KH, RANK + 1)
        gains = small[:, RANK + 1 :].T.astype(F32)
        return lax.dynamic_slice_in_dim(ups, head * KH, KH, 0), gains[:1], gains[1:]

    dims = (span * ctx // CHUNK, attn_cols, dp, ctx, rows, out_cols, up_cols)
    head_index = head.astype(jnp.int32)[None]

    def unpack_out(w_attn):
        out = w_attn[:, attn_cols:].reshape(dp, ctx, rows, out_cols)
        return out.transpose(0, 2, 1, 3).reshape(width, model)

    def mixer_forward(x_all, w_attn):
        if repeats == 1:
            part, gains, *kept = mixer_fwd(dims, head_index, x_all, w_attn, seg_col, seg_row)
            return part, gains, kept
        w_up, gain_in, gain_mid = layer_smalls(w_attn)
        x_all = x_all.astype(F32)
        normed_in = (x_all * inv_rms(x_all) * gain_in).astype(BF)
        pre = mm(normed_in, w_attn[:, :attn_cols])
        low_rank = pre[:, mix_cols:low_end].astype(BF)
        pre_f = mm_back(low_rank, w_up[:, :RANK]) + w_up[:, RANK].astype(F32)
        g = jax.nn.log_sigmoid(pre_f) / 16.0
        q = pre[:, :KH] * KH ** (-0.5)
        k = pre[:, KH : 2 * KH]
        v = pre[:, 2 * KH : 2 * KH + width]
        gate = pre[:, 2 * KH + width : mix_cols]
        mixed, states = gla_fwd(q, k, v, g, seg_col, seg_row)
        square = over_head(jnp.sum(mixed * mixed, axis=-1, keepdims=True), repeats)
        gated = mixed * lax.rsqrt(square / VH + head_eps) * silu_parts(gate)[0]
        gated = gated.astype(BF)
        part = mm(gated, unpack_out(w_attn)).astype(BF)
        gains = jnp.concatenate([gain_in, gain_mid], axis=0)
        kept = (w_up, normed_in, q, k, v, gate, low_rank, pre_f, g, mixed, states, gated)
        return part, gains, kept

    def mixer_backward(d_branch, w_attn, x_all, d_gain_mid, kept):
        if repeats == 1:
            return mixer_bwd(
                dims, head_index, d_branch, x_all, w_attn, seg_col, seg_row, d_gain_mid, *kept
            )
        w_up, normed_in, q, k, v, gate, low_rank, pre_f, g, mixed, states, gated = kept
        square = over_head(jnp.sum(mixed * mixed, axis=-1, keepdims=True), repeats)
        scale = lax.rsqrt(square / VH + head_eps)
        d_gated = mm_back(d_branch, unpack_out(w_attn))
        grad_out = mm_rows(gated, d_branch).astype(BF).reshape(dp, rows, ctx, out_cols)
        grad_out = grad_out.transpose(0, 2, 1, 3).reshape(model, out_cols)
        silu_gate, silu_slope = silu_parts(gate)
        normed = mixed * scale
        d_gate = d_gated * normed * silu_slope
        d_normed = d_gated * silu_gate
        inner = over_head(jnp.sum(d_normed * normed, axis=-1, keepdims=True), repeats) / VH
        d_mixed = scale * (d_normed - normed * inner)
        d_q, d_k, d_v, d_g = gla_bwd(q, k, v, g, seg_col, seg_row, states, d_mixed)
        d_forget = d_g * jax.nn.sigmoid(-pre_f) / 16.0
        grad_bias = jnp.sum(d_forget, axis=0)[:, None]
        d_forget = d_forget.astype(BF)
        grad_up = jnp.concatenate([mm_rows(d_forget, low_rank), grad_bias], axis=1)
        d_low = mm(d_forget, w_up[:, :RANK])
        spare = jnp.zeros((d_low.shape[0], attn_cols - low_end), F32)
        d_pre = [d_q * KH ** (-0.5), d_k, d_v, d_gate, d_low, spare]
        d_pre = jnp.concatenate([part.astype(BF) for part in d_pre], axis=1)
        part = mm_back(d_pre, w_attn[:, :attn_cols])
        x_all = x_all.astype(F32)
        grad_gain = jnp.sum(part * (x_all * inv_rms(x_all)), axis=0, keepdims=True)
        grads = jnp.concatenate([mm_rows(normed_in, d_pre).astype(BF), grad_out], axis=1)
        grads = grads.reshape(dp, 2, half_rows, attn_cols + out_cols).transpose(1, 0, 2, 3)
        grads = grads.reshape(2, dp * half_rows, attn_cols + out_cols)
        tiny = lax.dynamic_update_slice(
            jnp.zeros((owners, rows, RANK + 1), F32),
            grad_up.reshape(KH // up_cols, up_cols, RANK + 1),
            (head * (KH // up_cols), 0, 0),
        )
        tiny = jnp.concatenate(
            [tiny.reshape(model, RANK + 1), grad_gain.T, d_gain_mid.T], axis=1
        )
        tiny = tiny.astype(BF).reshape(dp, 2, half_rows, small_cols).transpose(1, 0, 2, 3)
        tiny = tiny.reshape(2, dp * half_rows, small_cols)
        return part.astype(BF), lax.dynamic_update_slice(grads, tiny, (0, 0, low_end))

    def forward(layer, x):
        x_all = in_order(gather_blocks(x))
        w_attn = whole_rows(attn_half) if layer == 0 else attn_high
        part, gains, mixer_kept = mixer_forward(x_all, w_attn)
        gain_in, gain_mid = gains[:1], gains[1:]
        if layer == 0:
            part, w_half = hold(part, ff_half)
            w_ff = whole_rows(w_half)
        else:
            w_ff = ff_high
        w_down = whole_cols(down_halves[layer])
        middle = x.astype(F32) + return_ordered(part)
        scale_mid = inv_rms(middle)
        normed_mid = jnp.concatenate(
            gather_blocks((middle * scale_mid * gain_mid).astype(BF)), axis=0
        )
        ff_pre = mm(normed_mid, w_ff)
        a, b = ff_pre[:, :ff_pad], ff_pre[:, ff_pad:]
        hidden = (silu_parts(a)[0] * b).astype(BF)[:, :ff_own]
        out = middle + return_blocks(mm(hidden, w_down))
        kept = (x_all, mixer_kept, middle, scale_mid, normed_mid, a, b, hidden)
        return out.astype(BF), (w_attn, w_ff, w_down, gain_in, gain_mid), kept

    def model_halves(array):
        low, high = [], []
        for i in range(dp):
            start = 2 * i * half_rows
            low.append(array[:, start : start + half_rows])
            high.append(array[:, start + half_rows : start + 2 * half_rows])
        low, high = jnp.concatenate(low, axis=1), jnp.concatenate(high, axis=1)
        return jnp.where(first, low, high), jnp.where(first, high, low)

    def over_dp(grad):
        return lax.psum_scatter(grad, "dp", scatter_dimension=0, tiled=True)

    def backward(layer, d_out, early, late):
        w_attn, w_ff, w_down, gain_in, gain_mid = weights[layer]
        x_all, mixer_kept, middle, scale_mid, normed_mid, a, b, hidden = layer_kept[layer]
        if layer == 0:
            ff_keep, ff_send = model_halves(normed_mid)
        else:
            ff_send = normed_mid
        dff = jnp.concatenate(gather_blocks(d_out.astype(BF)), axis=0)
        d_hidden = jnp.pad(mm_back(dff, w_down), ((0, 0), (0, ff_pad - ff_own)))
        silu_a, slope_a = silu_parts(a)
        d_a = (d_hidden * b * slope_a).astype(BF)
        d_b = (d_hidden * silu_a).astype(BF)
        d_ab = jnp.concatenate([d_a, d_b], axis=1)
        d_normed_mid = return_blocks(mm_back(d_ab, w_ff))
        send_ff = mm_rows(ff_send, d_ab).astype(BF)
        grad_down = mm_rows(hidden, dff)
        down_low, down_high = grad_down[:, :half_cols], grad_down[:, half_cols:]
        if layer > 0:
            grad_down = grad_down.astype(BF)
        else:
            keep_down = jnp.where(first, down_low, down_high).astype(BF)
            grad_down = jnp.where(first, down_high, down_low).astype(BF)
        d_normed_mid, send_ff, grad_down, early = lax.optimization_barrier(
            (d_normed_mid, send_ff, grad_down, early)
        )
        if layer > 0:
            sum_down, sum_ff = over_dp(grad_down), over_dp(send_ff)
        else:
            got_ff = swap_sections(send_ff)
            got_down = swap_sections(grad_down)
            sum_down = (keep_down.astype(F32) + got_down.astype(F32)).astype(BF)
        d_mid_part, grad_gain_mid = norm_back(middle, scale_mid, gain_mid, d_normed_mid)
        d_middle = d_out + d_mid_part

        d_branch = in_order(gather_blocks(d_middle.astype(BF)))
        part, grad_attn = mixer_backward(d_branch, w_attn, x_all, grad_gain_mid[None], mixer_kept)
        send_attn = jnp.where(first, grad_attn[1], grad_attn[0])
        keep_attn = jnp.where(first, grad_attn[0], grad_attn[1])
        if layer == 0:
            grad_ff = (mm_rows(ff_keep, d_ab) + got_ff.astype(F32)).astype(BF)
            late = tuple(over_dp(grad) if i == 0 else grad for i, grad in enumerate(late))
            part, send_attn, late, grad_ff, sum_down = lax.optimization_barrier(
                (part, send_attn, late, grad_ff, sum_down)
            )
            sum_down, sum_ff = over_dp(sum_down), over_dp(grad_ff)
        else:
            part, send_attn, late = lax.optimization_barrier((part, send_attn, late))
        grad_attn = keep_attn.astype(F32) + swap_sections(send_attn).astype(F32)
        grad_attn = grad_attn.astype(BF)
        d_normed_in = return_ordered(part)
        x_own = layer_x[layer].astype(F32)
        d_in_part, _ = norm_back(x_own, inv_rms(x_own), gain_in, d_normed_in)
        return d_middle + d_in_part, sum_down, sum_ff, grad_attn, early, late

    x = own_micro(block_in)
    weights, layer_x, layer_kept, layer_y = [], [], [], []
    for layer in range(sections):
        layer_x.append(x)
        x, layer_weight, kept = forward(layer, x)
        weights.append(layer_weight)
        layer_kept.append(kept)
        layer_y.append(x)
    def to_owner(low, high, kind=None):
        mine = jnp.where(first, low, high)
        send = jnp.where(first, high, low)
        return mine, swap_sections(send if kind is None else send.astype(kind))

    def both(low, high):
        mine, other = to_owner(low, high)
        return jnp.stack([jnp.where(first, mine, other), jnp.where(first, other, mine)])

    outputs = both(*layer_y)
    d_x = own_micro(out_grad).astype(F32)
    d_in, down_high, ff_high, attn_high, _, outputs = backward(1, d_x, (), outputs)
    upstream = d_in.astype(BF).astype(F32)
    d_first, down_low, ff_low, attn_low, early, late = backward(
        0, upstream, (attn_high, down_high), (attn_high, ff_high)
    )
    down_high, (attn_high, ff_high) = early[1], late
    attn_low = over_dp(attn_low)

    def halves_of_owner(low, high):
        mine, other = to_owner(low, high)
        return jnp.where(first, mine, other), jnp.where(first, other, mine)

    def to_rows(array):
        cols = array.shape[1]
        return lax.all_to_all(array.reshape(ctx, rows, cols), "ctx", 0, 0, tiled=True).astype(F32)

    def summed(low, high):
        mine, other = to_owner(low, high)
        return mine.astype(F32) + other.astype(F32)

    mine, other = to_owner(d_first, d_in, BF)
    other = other.astype(F32)
    input_grads = jnp.stack([jnp.where(first, mine, other), jnp.where(first, other, mine)])
    def ff_total(low, high, axis):
        got_low = lax.ppermute(low, "section", [(1, 0)])
        got_high = lax.ppermute(high, "section", [(0, 1)])
        layer_low = jnp.concatenate([low, got_low], axis=axis).astype(F32)
        return jnp.where(first, layer_low, high.astype(F32) + got_high.astype(F32))

    own_down = ff_total(down_low, down_high, 1)
    own_ff = to_rows(ff_total(ff_low, ff_high, 0).astype(BF))
    attn_low, own_down, own_ff, input_grads = lax.optimization_barrier(
        (attn_low, own_down, own_ff, input_grads)
    )

    half_ctx = ctx // 2
    pieces = jnp.stack([attn_low[:, :attn_cols], attn_high[:, :attn_cols]])
    pieces = pieces.reshape(ctx, rows, attn_cols)
    arrived = []
    for step in range(ctx):
        route = []
        for s in range(sections):
            for j in range(ctx):
                to_layer, k = divmod((j + step) % ctx, half_ctx)
                route.append((s * ctx + j, to_layer * ctx + s * half_ctx + k))
        piece = lax.dynamic_index_in_dim(pieces, (place + step) % ctx, 0, False)
        arrived.append(lax.ppermute(piece, ("section", "ctx"), route))
    arrived = jnp.stack(arrived)
    mine = section * half_ctx + place % half_ctx
    own_attn = jnp.stack(
        [
            lax.dynamic_index_in_dim(arrived, (mine - source) % ctx, 0, False)
            for source in range(ctx)
        ]
    ).astype(F32)
    outs = jnp.stack([attn_low[:, attn_cols:], attn_high[:, attn_cols:]])
    came = []
    for step in range(sections):
        route = []
        for s in range(sections):
            for i in range(dp):
                for j in range(ctx):
                    to_layer = (s + step) % sections
                    route.append(((s * dp + i) * ctx + j, (to_layer * ctx + j) * dp + i))
        block = lax.dynamic_index_in_dim(outs, (section + step) % sections, 0, False)
        came.append(lax.ppermute(block, ("section", "dp", "ctx"), route))
    out_halves = [jnp.where(first, came[0], came[1]), jnp.where(first, came[1], came[0])]
    own_out = jnp.concatenate(out_halves, axis=0).reshape(ctx, rows, out_cols)
    own_out = own_out.transpose(1, 0, 2).reshape(rows, model).astype(F32)

    def hidden_whole(parts):
        parts = parts.reshape(ctx, rows, dp, ff_rows).transpose(1, 2, 0, 3)
        return parts.reshape(rows, owners * ff_rows)

    def head_whole(parts):
        parts = parts.reshape(HEADS, repeats, rows, KH).sum(1)
        return parts.transpose(1, 0, 2).reshape(rows, HEADS * KH)

    def value_whole(parts):
        return parts.transpose(1, 0, 2).reshape(rows, HEADS * VH)

    tiny = jnp.sum(own_attn[:, :, low_end:small_end], axis=0)
    return (
        outputs[None, :, None],
        input_grads[None, :, None],
        head_whole(own_attn[:, :, :KH])[None],
        head_whole(own_attn[:, :, KH : 2 * KH])[None],
        value_whole(own_attn[:, :, 2 * KH : 2 * KH + width])[None],
        jnp.sum(own_attn[:, :, mix_cols:low_end], axis=0)[None],
        tiny[:up_cols, :RANK].T[None],
        tiny[:up_cols, RANK][None],
        value_whole(own_attn[:, :, 2 * KH + width : mix_cols])[None],
        own_out[None],
        tiny[:, RANK + 1][None],
        tiny[:, RANK + 2][None],
        hidden_whole(own_ff[:, :, :ff_own])[None],
        hidden_whole(own_ff[:, :, ff_pad : ff_pad + ff_own])[None],
        own_down[None],
    )


def solution(mesh):
    rows = P("section", ("dp", "ctx"), None)
    columns = P("section", None, ("dp", "ctx"))
    vector = P("section", ("dp", "ctx"))
    tokens = P(None, "dp", "ctx", None)
    stacked = P("section", None, "dp", "ctx", None)
    return jax.shard_map(
        per_device,
        mesh=mesh,
        in_specs=(
            tokens,
            P(None, "dp", None),
            rows,
            rows,
            rows,
            rows,
            columns,
            vector,
            rows,
            rows,
            vector,
            vector,
            rows,
            rows,
            rows,
            tokens,
        ),
        out_specs=(
            stacked,
            stacked,
            rows,
            rows,
            rows,
            rows,
            columns,
            vector,
            rows,
            rows,
            vector,
            vector,
            rows,
            rows,
            rows,
        ),
        check_vma=False,
    )
```

```python
import functools

import jax
import jax.numpy as jnp
from jax import lax
from jax.experimental import pallas as pl
from jax.experimental.pallas import tpu as pltpu
from jax.sharding import PartitionSpec as P

HEADS = 4
KH = 128
VH = 256
RANK = 16
STRETCH = 64
CHUNK = 2 * STRETCH

norm_eps = 1e-06
head_eps = 0.1
BF = jnp.bfloat16
F32 = jnp.float32
highest = lax.Precision.HIGHEST


def mm(left, right):
    return jnp.dot(left, right, preferred_element_type=F32)


def mm_back(left, right):
    return lax.dot_general(left, right, (((1,), (1,)), ((), ())), preferred_element_type=F32)


def mm_rows(left, right):
    return lax.dot_general(left, right, (((0,), (0,)), ((), ())), preferred_element_type=F32)


def dot_nn(a, b):
    return lax.dot_general(
        a, b, (((1,), (0,)), ((), ())), precision=highest, preferred_element_type=F32
    )


def dot_nt(a, b):
    return lax.dot_general(
        a, b, (((1,), (1,)), ((), ())), precision=highest, preferred_element_type=F32
    )


def dot_tn(a, b):
    return lax.dot_general(
        a, b, (((0,), (0,)), ((), ())), precision=highest, preferred_element_type=F32
    )


def chunk_parts(n, q_ref, k_ref, g_ref, seg_col_ref, seg_row_ref, low_tri):
    at = pl.ds(n * CHUNK, CHUNK)
    summed = dot_nn(low_tri, g_ref[at, :])
    middle = summed[STRETCH - 1 : STRETCH, :]
    last = summed[CHUNK - 1 : CHUNK, :]
    seg = seg_col_ref[at, :]
    seg_last = seg[CHUNK - 1 : CHUNK, :]
    seg_row = seg_row_ref[:, at]
    if n > 0:
        seg_prev = seg_col_ref[pl.ds(n * CHUNK - 1, 1), :]
    else:
        seg_prev = jnp.full((1, 1), -1.0, F32)
    up = jnp.exp(summed - middle)
    down = jnp.exp(middle - summed)
    entry = jnp.where(seg == seg_prev, jnp.exp(summed), 0.0)
    tail = jnp.where(seg == seg_last, jnp.exp(last - summed), 0.0)
    keep = jnp.where(seg_last == seg_prev, jnp.exp(last), 0.0)
    return at, seg, seg_row, up, down, entry, tail, keep


def tri_masks():
    rows = lax.broadcasted_iota(jnp.int32, (CHUNK, CHUNK), 0)
    cols = lax.broadcasted_iota(jnp.int32, (CHUNK, CHUNK), 1)
    return rows >= cols, rows <= cols


def gla_fwd_kernel(count, q_ref, k_ref, v_ref, g_ref, seg_col_ref, seg_row_ref, mixed_ref, st_ref):
    lower, _ = tri_masks()
    low_tri = lower.astype(F32)
    state = jnp.zeros(st_ref.shape[1:], F32)
    for n in range(count):
        at, seg, seg_row, up, down, entry, tail, keep = chunk_parts(
            n, q_ref, k_ref, g_ref, seg_col_ref, seg_row_ref, low_tri
        )
        q, k, v = q_ref[at, :], k_ref[at, :], v_ref[at, :]
        scores = dot_nt(q * up, k * down)
        scores = jnp.where(lower & (seg == seg_row), scores, 0.0)
        out = dot_nn(scores, v)
        st_ref[n] = state
        if n > 0:
            out = out + dot_nt(q * entry, state)
        mixed_ref[at, :] = out
        if n + 1 < count:
            state = state * keep + dot_tn(v, k * tail)


def gla_bwd_kernel(
    count,
    q_ref,
    k_ref,
    v_ref,
    g_ref,
    seg_col_ref,
    seg_row_ref,
    st_ref,
    do_ref,
    dq_ref,
    dk_ref,
    dv_ref,
    dg_ref,
):
    lower, upper = tri_masks()
    low_tri = lower.astype(F32)
    up_tri = upper.astype(F32)
    d_state = jnp.zeros(st_ref.shape[1:], F32)
    for n in reversed(range(count)):
        at, seg, seg_row, up, down, entry, tail, keep = chunk_parts(
            n, q_ref, k_ref, g_ref, seg_col_ref, seg_row_ref, low_tri
        )
        q, k, v, do = q_ref[at, :], k_ref[at, :], v_ref[at, :], do_ref[at, :]
        mask = lower & (seg == seg_row)
        q_up, k_down = q * up, k * down
        scores = jnp.where(mask, dot_nt(q_up, k_down), 0.0)
        d_scores = jnp.where(mask, dot_nt(do, v), 0.0)
        dq = dot_nn(d_scores, k_down) * up
        dk = dot_tn(d_scores, q_up) * down
        dv = dot_tn(scores, do)
        d_last = None
        if n + 1 < count:
            k_tail = k * tail
            dk_tail = dot_nn(v, d_state)
            dk = dk + dk_tail * tail
            dv = dv + dot_nt(k_tail, d_state)
            d_last = jnp.sum(dk_tail * k_tail, axis=0, keepdims=True)
        if n > 0:
            state = st_ref[n]
            dq = dq + dot_nn(do, state) * entry
            if d_last is not None:
                d_last = d_last + keep * jnp.sum(d_state * state, axis=0, keepdims=True)
            d_state = d_state * keep + dot_tn(do, q * entry)
        dg = dot_nn(up_tri, q * dq - k * dk)
        if d_last is not None:
            dg = dg + d_last
        dq_ref[at, :] = dq
        dk_ref[at, :] = dk
        dv_ref[at, :] = dv
        dg_ref[at, :] = dg


KERNEL_PARAMS = pltpu.CompilerParams(vmem_limit_bytes=40 * 1024 * 1024)


def gla_fwd(q, k, v, g, seg_col, seg_row):
    length, width = v.shape
    count = length // CHUNK
    return pl.pallas_call(
        functools.partial(gla_fwd_kernel, count),
        out_shape=(
            jax.ShapeDtypeStruct((length, width), F32),
            jax.ShapeDtypeStruct((count, width, KH), F32),
        ),
        compiler_params=KERNEL_PARAMS,
        name="gla_fwd",
    )(q, k, v, g, seg_col, seg_row)


def gla_bwd(q, k, v, g, seg_col, seg_row, states, do):
    length, width = v.shape
    count = length // CHUNK
    return pl.pallas_call(
        functools.partial(gla_bwd_kernel, count),
        out_shape=(
            jax.ShapeDtypeStruct((length, KH), F32),
            jax.ShapeDtypeStruct((length, KH), F32),
            jax.ShapeDtypeStruct((length, width), F32),
            jax.ShapeDtypeStruct((length, KH), F32),
        ),
        compiler_params=KERNEL_PARAMS,
        name="gla_bwd",
    )(q, k, v, g, seg_col, seg_row, states, do)


def silu_parts(values):
    sig = 1.0 / (1.0 + jnp.exp(-values))
    return values * sig, sig * (1.0 + values * (1.0 - sig))


def out_weight(w_ref, col, block, dp, ctx, rows, out_cols):
    parts = []
    for i in range(dp):
        start = (i * ctx + block) * rows
        parts.append(w_ref[start : start + rows, col : col + out_cols])
    return jnp.concatenate(parts, axis=0)


def small_parts(head, w_ref, at, dims):
    _, _, dp, ctx, rows, _, up_cols = dims
    parts = []
    for j in range(KH // up_cols):
        start = pl.multiple_of(head * (ctx * rows), ctx * rows) + j * rows
        tile = w_ref[pl.ds(start, up_cols), at : at + 128]
        parts.append(tile[:, RANK : 2 * RANK + 1])
    return jnp.concatenate(parts, axis=0)


def project(dims, head, x_ref, w_ref, normed_ref, q_ref, k_ref, v_ref, gate_ref, low_ref, g_ref):
    attn_cols = dims[1]
    mix_cols = 2 * KH + 2 * VH
    gains = jnp.transpose(w_ref[:, mix_cols : mix_cols + 128].astype(F32))
    gains = gains[2 * RANK + 1 : 2 * RANK + 3, :]
    x = x_ref[...].astype(F32)
    unit = x * lax.rsqrt(jnp.mean(x * x, axis=-1, keepdims=True) + norm_eps)
    normed_ref[...] = (unit * gains[:1]).astype(BF)
    pre = mm(normed_ref[...], w_ref[:, :attn_cols])
    q_ref[...] = pre[:, :KH] * KH ** (-0.5)
    k_ref[...] = pre[:, KH : 2 * KH]
    v_ref[...] = pre[:, 2 * KH : 2 * KH + VH]
    gate_ref[...] = pre[:, 2 * KH + VH : mix_cols]
    low_ref[...] = pre[:, mix_cols : mix_cols + RANK].astype(BF)
    ups = small_parts(head, w_ref, mix_cols, dims)
    low_one = jnp.concatenate([low_ref[...], jnp.ones((x.shape[0], 1), BF)], axis=1)
    pre_f = mm_back(low_one, ups)
    g_ref[...] = (jnp.minimum(pre_f, 0.0) - jnp.log1p(jnp.exp(-jnp.abs(pre_f)))) / 16.0
    return gains, unit, ups, pre_f


def mixer_fwd_kernel(
    dims,
    head_ref,
    x_ref,
    w_ref,
    seg_col_ref,
    seg_row_ref,
    part_ref,
    gains_ref,
    mixed_ref,
    st_ref,
    normed_ref,
    q_ref,
    k_ref,
    v_ref,
    gate_ref,
    low_ref,
    g_ref,
):
    count, attn_cols, dp, ctx, rows, out_cols, _ = dims
    gains, _, _, _ = project(
        dims, head_ref[0], x_ref, w_ref, normed_ref, q_ref, k_ref, v_ref, gate_ref, low_ref, g_ref
    )
    gains_ref[...] = gains
    gla_fwd_kernel(
        count, q_ref, k_ref, v_ref, g_ref, seg_col_ref, seg_row_ref, mixed_ref, st_ref
    )
    mixed = mixed_ref[...]
    head_scale = lax.rsqrt(jnp.mean(mixed * mixed, axis=-1, keepdims=True) + head_eps)
    gated = (mixed * head_scale * silu_parts(gate_ref[...])[0]).astype(BF)
    for block in range(ctx):
        w_block = out_weight(w_ref, attn_cols, block, dp, ctx, rows, out_cols)
        part_ref[:, block * out_cols : (block + 1) * out_cols] = mm(gated, w_block).astype(BF)


def mixer_bwd_kernel(
    dims,
    head_ref,
    d_branch_ref,
    x_ref,
    w_ref,
    seg_col_ref,
    seg_row_ref,
    d_gain_ref,
    mixed_ref,
    st_ref,
    part_ref,
    grad_ref,
    normed_ref,
    q_ref,
    k_ref,
    v_ref,
    gate_ref,
    low_ref,
    g_ref,
    d_mixed_ref,
    dq_ref,
    dk_ref,
    dv_ref,
    dg_ref,
    d_pre_ref,
):
    count, attn_cols, dp, ctx, rows, out_cols, up_cols = dims
    half = ctx * rows // 2
    head = head_ref[0]
    _, unit, ups, pre_f = project(
        dims, head, x_ref, w_ref, normed_ref, q_ref, k_ref, v_ref, gate_ref, low_ref, g_ref
    )
    mixed = mixed_ref[...]
    head_scale = lax.rsqrt(jnp.mean(mixed * mixed, axis=-1, keepdims=True) + head_eps)
    normed = mixed * head_scale
    silu_gate, silu_slope = silu_parts(gate_ref[...])
    gated = (normed * silu_gate).astype(BF)
    d_gated = None
    for block in range(ctx):
        d_block = d_branch_ref[:, block * out_cols : (block + 1) * out_cols]
        w_block = out_weight(w_ref, attn_cols, block, dp, ctx, rows, out_cols)
        term = mm_back(d_block, w_block)
        d_gated = term if d_gated is None else d_gated + term
        grad_block = mm_rows(gated, d_block).astype(BF)
        side, spot = divmod(block, ctx // 2)
        for i in range(dp):
            start = (i * (ctx // 2) + spot) * rows
            grad_ref[side, start : start + rows, attn_cols:] = grad_block[
                i * rows : (i + 1) * rows
            ]
    d_normed = d_gated * silu_gate
    mix_cols = 2 * KH + 2 * VH
    d_pre_ref[:, 2 * KH + VH : mix_cols] = (d_gated * normed * silu_slope).astype(BF)
    inner = jnp.mean(d_normed * normed, axis=-1, keepdims=True)
    d_mixed_ref[...] = head_scale * (d_normed - normed * inner)
    gla_bwd_kernel(
        count,
        q_ref,
        k_ref,
        v_ref,
        g_ref,
        seg_col_ref,
        seg_row_ref,
        st_ref,
        d_mixed_ref,
        dq_ref,
        dk_ref,
        dv_ref,
        dg_ref,
    )
    d_forget = dg_ref[...] * (1.0 / (1.0 + jnp.exp(pre_f))) / 16.0
    ones = jnp.ones((d_forget.shape[0], 1), F32)
    grad_up = mm_rows(d_forget.astype(BF), low_ref[...])
    grad_bias = dot_tn(d_forget, ones)
    d_low = mm(d_forget.astype(BF), ups[:, :RANK]).astype(BF)
    d_pre_ref[:, :KH] = (dq_ref[...] * KH ** (-0.5)).astype(BF)
    d_pre_ref[:, KH : 2 * KH] = dk_ref[...].astype(BF)
    d_pre_ref[:, 2 * KH : 2 * KH + VH] = dv_ref[...].astype(BF)
    spare = jnp.zeros((d_low.shape[0], attn_cols - mix_cols - RANK), BF)
    d_pre_ref[:, mix_cols:] = jnp.concatenate([d_low, spare], axis=1)
    part = mm_back(d_pre_ref[...], w_ref[:, :attn_cols])
    part_ref[...] = part.astype(BF)

    model = part.shape[1]
    d_mix = jnp.sum(part * unit, axis=0, keepdims=True)
    gain_rows = jnp.concatenate([d_mix, d_gain_ref[...], jnp.zeros((6, model), F32)], axis=0)
    gain_cols = jnp.transpose(gain_rows)
    before = jnp.zeros((model, 2 * RANK + 1), F32)
    after = jnp.zeros((model, 128 - 2 * RANK - 3), F32)
    gain_tile = jnp.concatenate([before, gain_cols[:, :2], after], axis=1)
    for side in range(2):
        starts = [(2 * i + side) * half for i in range(dp)]
        own = jnp.concatenate([normed_ref[:, a : a + half] for a in starts], axis=1)
        grads = mm_rows(own, d_pre_ref[...])
        tile = jnp.concatenate([gain_tile[a : a + half] for a in starts], axis=0)
        grad_ref[side, :, :mix_cols] = grads[:, :mix_cols].astype(BF)
        grad_ref[side, :, mix_cols:attn_cols] = (grads[:, mix_cols:] + tile).astype(BF)
    pad_low = jnp.zeros((KH, RANK), F32)
    pad_high = jnp.zeros((KH, 128 - 2 * RANK - 1), F32)
    up_tile = jnp.concatenate([pad_low, grad_up, grad_bias, pad_high], axis=1).astype(BF)
    for j in range(KH // up_cols):
        side, spot = divmod(j, ctx // 2)
        at = pl.ds(pl.multiple_of(head * half, half) + spot * rows, up_cols)
        grad_ref[side, at, mix_cols:attn_cols] += up_tile[j * up_cols : (j + 1) * up_cols]


def mixer_call(kernel, name, shapes, scratch, operands):
    specs = [pl.BlockSpec(memory_space=pltpu.SMEM)]
    specs += [pl.BlockSpec(memory_space=pltpu.VMEM)] * (len(operands) - 1)
    return pl.pallas_call(
        kernel,
        in_specs=specs,
        out_specs=[pl.BlockSpec(memory_space=pltpu.VMEM)] * len(shapes),
        out_shape=[jax.ShapeDtypeStruct(*shape) for shape in shapes],
        scratch_shapes=[pltpu.VMEM(*shape) for shape in scratch],
        compiler_params=KERNEL_PARAMS,
        name=name,
    )(*operands)


def project_scratch(length, model):
    return [
        ((length, model), BF),
        ((length, KH), F32),
        ((length, KH), F32),
        ((length, VH), F32),
        ((length, VH), F32),
        ((length, RANK), BF),
        ((length, KH), F32),
    ]


def mixer_fwd(dims, head, x, w, seg_col, seg_row):
    length, model = x.shape
    shapes = [
        ((length, model), BF),
        ((2, model), F32),
        ((length, VH), F32),
        ((dims[0], VH, KH), F32),
    ]
    return mixer_call(
        functools.partial(mixer_fwd_kernel, dims),
        "mixer_fwd",
        shapes,
        project_scratch(length, model),
        (head, x, w, seg_col, seg_row),
    )


def mixer_bwd(dims, head, d_branch, x, w, seg_col, seg_row, d_gain, mixed, states):
    length, model = x.shape
    shapes = [((length, model), BF), ((2, w.shape[0] // 2, w.shape[1]), BF)]
    scratch = project_scratch(length, model) + [
        ((length, VH), F32),
        ((length, KH), F32),
        ((length, KH), F32),
        ((length, VH), F32),
        ((length, KH), F32),
        ((length, dims[1]), BF),
    ]
    return mixer_call(
        functools.partial(mixer_bwd_kernel, dims),
        "mixer_bwd",
        shapes,
        scratch,
        (head, d_branch, x, w, seg_col, seg_row, d_gain, mixed, states),
    )


def shift(block, distance):
    size = lax.axis_size("ctx")
    return lax.ppermute(block, "ctx", [(i, (i + distance) % size) for i in range(size)])


def gather_blocks(block):
    return [block] + [shift(block, s) for s in range(1, lax.axis_size("ctx"))]


def in_order(blocks):
    size, place = lax.axis_size("ctx"), lax.axis_index("ctx")
    rows = blocks[0].shape[0]
    whole = jnp.zeros((size * rows,) + blocks[0].shape[1:], blocks[0].dtype)
    for s, block in enumerate(blocks):
        whole = lax.dynamic_update_slice_in_dim(whole, block, ((place - s) % size) * rows, 0)
    return whole


def return_blocks(whole):
    size = lax.axis_size("ctx")
    rows = whole.shape[0] // size
    total = whole[:rows].astype(F32)
    for s in range(1, size):
        total = total + shift(whole[s * rows : (s + 1) * rows].astype(BF), -s).astype(F32)
    return total


def return_ordered(whole):
    size, place = lax.axis_size("ctx"), lax.axis_index("ctx")
    rows = whole.shape[0] // size
    total = lax.dynamic_slice_in_dim(whole, place * rows, rows, 0).astype(F32)
    for s in range(1, size):
        part = lax.dynamic_slice_in_dim(whole, ((place - s) % size) * rows, rows, 0)
        total = total + shift(part.astype(BF), -s).astype(F32)
    return total


def over_head(values, repeats):
    if repeats == 1:
        return values
    size = lax.axis_size("ctx")
    total = values
    for s in range(1, repeats):
        route = [(i, i - i % repeats + (i + s) % repeats) for i in range(size)]
        total = total + lax.ppermute(values, "ctx", route)
    return total


def transpose_devices(block):
    size = lax.axis_size("ctx")
    route = [(i * size + j, j * size + i) for i in range(size) for j in range(size)]
    return lax.ppermute(block, ("dp", "ctx"), route)


def swap_sections(block):
    return lax.ppermute(block, "section", [(0, 1), (1, 0)])


def hold(value, other):
    return lax.optimization_barrier((value, other))


def inv_rms(values):
    return lax.rsqrt(jnp.mean(values * values, axis=-1, keepdims=True) + norm_eps)


def norm_back(values, scale, gain, d_out):
    normed = values * scale
    d_normed = d_out * gain
    inner = jnp.mean(d_normed * normed, axis=-1, keepdims=True)
    return scale * (d_normed - normed * inner), jnp.sum(d_out * normed, axis=0)


def per_device(
    block_in,
    doc_lengths,
    w_query,
    w_key,
    w_value,
    forget_down,
    forget_up,
    forget_bias,
    w_gate,
    w_out,
    mix_gain,
    ffn_gain,
    ff_gate,
    ff_up,
    ff_down,
    out_grad,
):
    sections = lax.axis_size("section")
    dp, ctx = lax.axis_size("dp"), lax.axis_size("ctx")
    section, place = lax.axis_index("section"), lax.axis_index("ctx")
    first = section == 0
    owners = dp * ctx
    repeats = ctx // HEADS
    width = VH // repeats
    span = block_in.shape[2]
    model = block_in.shape[3]
    rows = w_query.shape[1]
    ff_rows = ff_down.shape[1]
    ff_own = ff_rows * dp
    ff_pad = -(-ff_own // 128) * 128
    up_cols = forget_up.shape[2]
    head = place // repeats

    def own_micro(array):
        return jnp.where(first, array[0], array[1])[0]

    lengths = own_micro(doc_lengths)
    begins = jnp.cumsum(lengths) - lengths
    positions = jnp.arange(span * ctx, dtype=jnp.int32)
    seg = jnp.sum((begins[None, :] <= positions[:, None]).astype(F32), axis=1)
    seg_col, seg_row = seg[:, None], seg[None, :]

    def head_blocks(shard):
        parts = shard[0].reshape(rows, HEADS, KH).transpose(1, 0, 2)
        return jnp.repeat(parts, repeats, axis=0) if repeats > 1 else parts

    def value_blocks(shard):
        return shard[0].reshape(rows, ctx, width).transpose(1, 0, 2)

    def hidden_blocks(shard):
        parts = shard[0].reshape(rows, dp, ctx, ff_rows).transpose(2, 0, 1, 3)
        parts = parts.reshape(ctx, rows, ff_own)
        return jnp.pad(parts, ((0, 0), (0, 0), (0, ff_pad - ff_own)))

    def to_all(block):
        return jnp.broadcast_to(block[None], (ctx,) + block.shape)

    up_rows = jnp.concatenate([forget_up[0].T, forget_bias[0][:, None]], axis=1)
    up_rows = jnp.pad(up_rows, ((0, rows - up_cols), (0, 0)))
    small = jnp.concatenate([up_rows, mix_gain[0][:, None], ffn_gain[0][:, None]], axis=1)
    small_cols = RANK + 3
    mix_cols = 2 * KH + 2 * width
    low_end = mix_cols + RANK
    small_end = low_end + small_cols
    attn_cols = -(-small_end // 128) * 128
    out_cols = model // ctx
    attn_send = jnp.concatenate(
        [
            head_blocks(w_query),
            head_blocks(w_key),
            value_blocks(w_value),
            value_blocks(w_gate),
            to_all(forget_down[0]),
            to_all(small),
            jnp.zeros((ctx, rows, attn_cols - small_end), BF),
        ],
        axis=2,
    )
    ff_send = jnp.concatenate([hidden_blocks(ff_gate), hidden_blocks(ff_up)], axis=2)

    half_rows = ctx * rows // 2
    half_cols = model // 2

    def exchange(send):
        got = lax.all_to_all(send, "ctx", 0, 0, tiled=True)
        return got.reshape(ctx * rows, send.shape[2])

    def layer_pieces(low, high):
        own = jnp.where(first, low, high)
        got = swap_sections(jnp.where(first, high, low))
        return jnp.where(first, own, got), jnp.where(first, got, own)

    def whole_block(own, low_half):
        high_half = lax.ppermute(own[half_rows:], "section", [(1, 0)])
        return jnp.where(first, jnp.concatenate([low_half, high_half], axis=0), own)

    def gathered(piece):
        return lax.all_gather(piece, "dp", axis=0, tiled=True)

    def gathered_direct(piece):
        place_dp = lax.axis_index("dp")
        size = piece.shape[0]
        whole = jnp.zeros((dp * size, piece.shape[1]), piece.dtype)
        whole = lax.dynamic_update_slice_in_dim(whole, piece, place_dp * size, 0)
        for step in range(1, dp):
            route = [(i, (i + step) % dp) for i in range(dp)]
            block = lax.ppermute(piece, "dp", route)
            start = ((place_dp - step) % dp) * size
            whole = lax.dynamic_update_slice_in_dim(whole, block, start, 0)
        return whole

    down_pieces = layer_pieces(ff_down[0][:, :half_cols], ff_down[0][:, half_cols:])
    down_piece = jnp.concatenate(down_pieces, axis=0)
    down_all = gathered_direct(down_piece).reshape(dp, sections, ff_rows, half_cols)
    down_halves = [down_all[:, layer].reshape(ff_own, half_cols) for layer in range(sections)]

    out_block = transpose_devices(w_out[0]).reshape(rows, ctx, out_cols)
    out_block = out_block.transpose(1, 0, 2).reshape(ctx * rows, out_cols)
    attn_block = jnp.concatenate([exchange(attn_send), out_block], axis=1)
    attn_block = hold(attn_block, down_piece)[0]
    attn_pieces = layer_pieces(attn_block[:half_rows], attn_block[half_rows:])
    attn_high = whole_block(attn_block, attn_pieces[1])
    ff_block = exchange(hold(ff_send, (attn_block, down_all))[0])
    ff_pieces = layer_pieces(ff_block[:half_rows], ff_block[half_rows:])
    ff_high = whole_block(ff_block, ff_pieces[1])

    attn_half, ff_half = gathered(attn_pieces[0]), gathered(ff_pieces[0])
    attn_high, attn_half = hold(attn_high, attn_half)
    ff_high, ff_half = hold(ff_high, ff_half)
    attn_high, ff_high = gathered(attn_high), gathered(ff_high)

    def both_halves(own):
        other = swap_sections(own)
        return jnp.where(first, own, other), jnp.where(first, other, own)

    def whole_rows(own):
        cols = own.shape[1]
        parts = [part.reshape(dp, 1, half_rows, cols) for part in both_halves(own)]
        return jnp.concatenate(parts, axis=1).reshape(model, cols)

    def whole_cols(own):
        return jnp.concatenate(both_halves(own), axis=1)

    def layer_smalls(w_attn):
        small = w_attn[:, low_end:small_end]
        ups = small[:, : RANK + 1].reshape(owners, rows, RANK + 1)[:, :up_cols]
        ups = ups.reshape(HEADS * KH, RANK + 1)
        gains = small[:, RANK + 1 :].T.astype(F32)
        return lax.dynamic_slice_in_dim(ups, head * KH, KH, 0), gains[:1], gains[1:]

    dims = (span * ctx // CHUNK, attn_cols, dp, ctx, rows, out_cols, up_cols)
    head_index = head.astype(jnp.int32)[None]

    def unpack_out(w_attn):
        out = w_attn[:, attn_cols:].reshape(dp, ctx, rows, out_cols)
        return out.transpose(0, 2, 1, 3).reshape(width, model)

    def mixer_forward(x_all, w_attn):
        if repeats == 1:
            part, gains, *kept = mixer_fwd(dims, head_index, x_all, w_attn, seg_col, seg_row)
            return part, gains, kept
        w_up, gain_in, gain_mid = layer_smalls(w_attn)
        x_all = x_all.astype(F32)
        normed_in = (x_all * inv_rms(x_all) * gain_in).astype(BF)
        pre = mm(normed_in, w_attn[:, :attn_cols])
        low_rank = pre[:, mix_cols:low_end].astype(BF)
        pre_f = mm_back(low_rank, w_up[:, :RANK]) + w_up[:, RANK].astype(F32)
        g = jax.nn.log_sigmoid(pre_f) / 16.0
        q = pre[:, :KH] * KH ** (-0.5)
        k = pre[:, KH : 2 * KH]
        v = pre[:, 2 * KH : 2 * KH + width]
        gate = pre[:, 2 * KH + width : mix_cols]
        mixed, states = gla_fwd(q, k, v, g, seg_col, seg_row)
        square = over_head(jnp.sum(mixed * mixed, axis=-1, keepdims=True), repeats)
        gated = mixed * lax.rsqrt(square / VH + head_eps) * silu_parts(gate)[0]
        gated = gated.astype(BF)
        part = mm(gated, unpack_out(w_attn)).astype(BF)
        gains = jnp.concatenate([gain_in, gain_mid], axis=0)
        kept = (w_up, normed_in, q, k, v, gate, low_rank, pre_f, g, mixed, states, gated)
        return part, gains, kept

    def mixer_backward(d_branch, w_attn, x_all, d_gain_mid, kept):
        if repeats == 1:
            return mixer_bwd(
                dims, head_index, d_branch, x_all, w_attn, seg_col, seg_row, d_gain_mid, *kept
            )
        w_up, normed_in, q, k, v, gate, low_rank, pre_f, g, mixed, states, gated = kept
        square = over_head(jnp.sum(mixed * mixed, axis=-1, keepdims=True), repeats)
        scale = lax.rsqrt(square / VH + head_eps)
        d_gated = mm_back(d_branch, unpack_out(w_attn))
        grad_out = mm_rows(gated, d_branch).astype(BF).reshape(dp, rows, ctx, out_cols)
        grad_out = grad_out.transpose(0, 2, 1, 3).reshape(model, out_cols)
        silu_gate, silu_slope = silu_parts(gate)
        normed = mixed * scale
        d_gate = d_gated * normed * silu_slope
        d_normed = d_gated * silu_gate
        inner = over_head(jnp.sum(d_normed * normed, axis=-1, keepdims=True), repeats) / VH
        d_mixed = scale * (d_normed - normed * inner)
        d_q, d_k, d_v, d_g = gla_bwd(q, k, v, g, seg_col, seg_row, states, d_mixed)
        d_forget = d_g * jax.nn.sigmoid(-pre_f) / 16.0
        grad_bias = jnp.sum(d_forget, axis=0)[:, None]
        d_forget = d_forget.astype(BF)
        grad_up = jnp.concatenate([mm_rows(d_forget, low_rank), grad_bias], axis=1)
        d_low = mm(d_forget, w_up[:, :RANK])
        spare = jnp.zeros((d_low.shape[0], attn_cols - low_end), F32)
        d_pre = [d_q * KH ** (-0.5), d_k, d_v, d_gate, d_low, spare]
        d_pre = jnp.concatenate([part.astype(BF) for part in d_pre], axis=1)
        part = mm_back(d_pre, w_attn[:, :attn_cols])
        x_all = x_all.astype(F32)
        grad_gain = jnp.sum(part * (x_all * inv_rms(x_all)), axis=0, keepdims=True)
        grads = jnp.concatenate([mm_rows(normed_in, d_pre).astype(BF), grad_out], axis=1)
        grads = grads.reshape(dp, 2, half_rows, attn_cols + out_cols).transpose(1, 0, 2, 3)
        grads = grads.reshape(2, dp * half_rows, attn_cols + out_cols)
        tiny = lax.dynamic_update_slice(
            jnp.zeros((owners, rows, RANK + 1), F32),
            grad_up.reshape(KH // up_cols, up_cols, RANK + 1),
            (head * (KH // up_cols), 0, 0),
        )
        tiny = jnp.concatenate(
            [tiny.reshape(model, RANK + 1), grad_gain.T, d_gain_mid.T], axis=1
        )
        tiny = tiny.astype(BF).reshape(dp, 2, half_rows, small_cols).transpose(1, 0, 2, 3)
        tiny = tiny.reshape(2, dp * half_rows, small_cols)
        return part.astype(BF), lax.dynamic_update_slice(grads, tiny, (0, 0, low_end))

    def forward(layer, x):
        x_all = in_order(gather_blocks(x))
        w_attn = whole_rows(attn_half) if layer == 0 else attn_high
        part, gains, mixer_kept = mixer_forward(x_all, w_attn)
        gain_in, gain_mid = gains[:1], gains[1:]
        if layer == 0:
            part, w_half = hold(part, ff_half)
            w_ff = whole_rows(w_half)
        else:
            w_ff = ff_high
        w_down = whole_cols(down_halves[layer])
        middle = x.astype(F32) + return_ordered(part)
        scale_mid = inv_rms(middle)
        normed_mid = jnp.concatenate(
            gather_blocks((middle * scale_mid * gain_mid).astype(BF)), axis=0
        )
        ff_pre = mm(normed_mid, w_ff)
        a, b = ff_pre[:, :ff_pad], ff_pre[:, ff_pad:]
        hidden = (silu_parts(a)[0] * b).astype(BF)[:, :ff_own]
        out = middle + return_blocks(mm(hidden, w_down))
        kept = (x_all, mixer_kept, middle, scale_mid, normed_mid, a, b, hidden)
        return out.astype(BF), (w_attn, w_ff, w_down, gain_in, gain_mid), kept

    def model_halves(array):
        low, high = [], []
        for i in range(dp):
            start = 2 * i * half_rows
            low.append(array[:, start : start + half_rows])
            high.append(array[:, start + half_rows : start + 2 * half_rows])
        low, high = jnp.concatenate(low, axis=1), jnp.concatenate(high, axis=1)
        return jnp.where(first, low, high), jnp.where(first, high, low)

    def over_dp(grad):
        return lax.psum_scatter(grad, "dp", scatter_dimension=0, tiled=True)

    def backward(layer, d_out, early, late):
        w_attn, w_ff, w_down, gain_in, gain_mid = weights[layer]
        x_all, mixer_kept, middle, scale_mid, normed_mid, a, b, hidden = layer_kept[layer]
        ff_keep, ff_send = model_halves(normed_mid)
        dff = jnp.concatenate(gather_blocks(d_out.astype(BF)), axis=0)
        d_hidden = jnp.pad(mm_back(dff, w_down), ((0, 0), (0, ff_pad - ff_own)))
        silu_a, slope_a = silu_parts(a)
        d_a = (d_hidden * b * slope_a).astype(BF)
        d_b = (d_hidden * silu_a).astype(BF)
        d_ab = jnp.concatenate([d_a, d_b], axis=1)
        d_normed_mid = return_blocks(mm_back(d_ab, w_ff))
        send_ff = mm_rows(ff_send, d_ab).astype(BF)
        grad_down = mm_rows(hidden, dff)
        down_low, down_high = grad_down[:, :half_cols], grad_down[:, half_cols:]
        if layer > 0:
            grad_down = grad_down.astype(BF)
        else:
            keep_down = jnp.where(first, down_low, down_high).astype(BF)
            grad_down = jnp.where(first, down_high, down_low).astype(BF)
        d_normed_mid, send_ff, grad_down, early = lax.optimization_barrier(
            (d_normed_mid, send_ff, grad_down, early)
        )
        got_ff = swap_sections(send_ff)
        if layer > 0:
            sum_down = over_dp(grad_down)
        else:
            got_down = swap_sections(grad_down)
            sum_down = (keep_down.astype(F32) + got_down.astype(F32)).astype(BF)
        d_mid_part, grad_gain_mid = norm_back(middle, scale_mid, gain_mid, d_normed_mid)
        d_middle = d_out + d_mid_part

        d_branch = in_order(gather_blocks(d_middle.astype(BF)))
        part, grad_attn = mixer_backward(d_branch, w_attn, x_all, grad_gain_mid[None], mixer_kept)
        send_attn = jnp.where(first, grad_attn[1], grad_attn[0])
        keep_attn = jnp.where(first, grad_attn[0], grad_attn[1])
        grad_ff = (mm_rows(ff_keep, d_ab) + got_ff.astype(F32)).astype(BF)
        if layer == 0:
            sum_down = over_dp(hold(sum_down, part)[0])
            late = over_dp(late)
        part, send_attn, late, grad_ff = lax.optimization_barrier(
            (part, send_attn, late, grad_ff)
        )
        grad_attn = keep_attn.astype(F32) + swap_sections(send_attn).astype(F32)
        grad_attn = grad_attn.astype(BF)
        d_normed_in = return_ordered(part)
        x_own = layer_x[layer].astype(F32)
        d_in_part, _ = norm_back(x_own, inv_rms(x_own), gain_in, d_normed_in)
        return d_middle + d_in_part, sum_down, over_dp(grad_ff), grad_attn, early, late

    x = own_micro(block_in)
    weights, layer_x, layer_kept, layer_y = [], [], [], []
    for layer in range(sections):
        layer_x.append(x)
        x, layer_weight, kept = forward(layer, x)
        weights.append(layer_weight)
        layer_kept.append(kept)
        layer_y.append(x)
    def to_owner(low, high, kind=None):
        mine = jnp.where(first, low, high)
        send = jnp.where(first, high, low)
        return mine, swap_sections(send if kind is None else send.astype(kind))

    def both(low, high):
        mine, other = to_owner(low, high)
        return jnp.stack([jnp.where(first, mine, other), jnp.where(first, other, mine)])

    outputs = both(*layer_y)
    d_x = own_micro(out_grad).astype(F32)
    d_in, down_high, ff_high, attn_high, _, outputs = backward(1, d_x, (), outputs)
    upstream = d_in.astype(BF).astype(F32)
    d_first, down_low, ff_low, attn_low, early, attn_high = backward(
        0, upstream, (attn_high, down_high, ff_high), attn_high
    )
    _, down_high, ff_high = early
    attn_low = over_dp(attn_low)

    def halves_of_owner(low, high):
        mine, other = to_owner(low, high)
        return jnp.where(first, mine, other), jnp.where(first, other, mine)

    def to_rows(array):
        cols = array.shape[1]
        return lax.all_to_all(array.reshape(ctx, rows, cols), "ctx", 0, 0, tiled=True).astype(F32)

    def summed(low, high):
        mine, other = to_owner(low, high)
        return mine.astype(F32) + other.astype(F32)

    mine, other = to_owner(d_first, d_in, BF)
    other = other.astype(F32)
    input_grads = jnp.stack([jnp.where(first, mine, other), jnp.where(first, other, mine)])
    got = swap_sections(jnp.where(first, down_high, jnp.pad(down_low, ((0, 0), (0, half_cols)))))
    own_low = jnp.concatenate([down_low, got[:, :half_cols]], axis=1).astype(F32)
    own_down = jnp.where(first, own_low, down_high.astype(F32) + got.astype(F32))
    own_ff = to_rows(jnp.concatenate(halves_of_owner(ff_low, ff_high), axis=0))
    attn_low, own_down, own_ff, input_grads = lax.optimization_barrier(
        (attn_low, own_down, own_ff, input_grads)
    )

    half_ctx = ctx // 2
    pieces = jnp.stack([attn_low[:, :attn_cols], attn_high[:, :attn_cols]])
    pieces = pieces.reshape(ctx, rows, attn_cols)
    arrived = []
    for step in range(ctx):
        route = []
        for s in range(sections):
            for j in range(ctx):
                to_layer, k = divmod((j + step) % ctx, half_ctx)
                route.append((s * ctx + j, to_layer * ctx + s * half_ctx + k))
        piece = lax.dynamic_index_in_dim(pieces, (place + step) % ctx, 0, False)
        arrived.append(lax.ppermute(piece, ("section", "ctx"), route))
    arrived = jnp.stack(arrived)
    mine = section * half_ctx + place % half_ctx
    own_attn = jnp.stack(
        [
            lax.dynamic_index_in_dim(arrived, (mine - source) % ctx, 0, False)
            for source in range(ctx)
        ]
    ).astype(F32)
    outs = jnp.stack([attn_low[:, attn_cols:], attn_high[:, attn_cols:]])
    came = []
    for step in range(sections):
        route = []
        for s in range(sections):
            for i in range(dp):
                for j in range(ctx):
                    to_layer = (s + step) % sections
                    route.append(((s * dp + i) * ctx + j, (to_layer * ctx + j) * dp + i))
        block = lax.dynamic_index_in_dim(outs, (section + step) % sections, 0, False)
        came.append(lax.ppermute(block, ("section", "dp", "ctx"), route))
    out_halves = [jnp.where(first, came[0], came[1]), jnp.where(first, came[1], came[0])]
    own_out = jnp.concatenate(out_halves, axis=0).reshape(ctx, rows, out_cols)
    own_out = own_out.transpose(1, 0, 2).reshape(rows, model).astype(F32)

    def hidden_whole(parts):
        parts = parts.reshape(ctx, rows, dp, ff_rows).transpose(1, 2, 0, 3)
        return parts.reshape(rows, owners * ff_rows)

    def head_whole(parts):
        parts = parts.reshape(HEADS, repeats, rows, KH).sum(1)
        return parts.transpose(1, 0, 2).reshape(rows, HEADS * KH)

    def value_whole(parts):
        return parts.transpose(1, 0, 2).reshape(rows, HEADS * VH)

    tiny = jnp.sum(own_attn[:, :, low_end:small_end], axis=0)
    return (
        outputs[None, :, None],
        input_grads[None, :, None],
        head_whole(own_attn[:, :, :KH])[None],
        head_whole(own_attn[:, :, KH : 2 * KH])[None],
        value_whole(own_attn[:, :, 2 * KH : 2 * KH + width])[None],
        jnp.sum(own_attn[:, :, mix_cols:low_end], axis=0)[None],
        tiny[:up_cols, :RANK].T[None],
        tiny[:up_cols, RANK][None],
        value_whole(own_attn[:, :, 2 * KH + width : mix_cols])[None],
        own_out[None],
        tiny[:, RANK + 1][None],
        tiny[:, RANK + 2][None],
        hidden_whole(own_ff[:, :, :ff_own])[None],
        hidden_whole(own_ff[:, :, ff_pad : ff_pad + ff_own])[None],
        own_down[None],
    )


def solution(mesh):
    rows = P("section", ("dp", "ctx"), None)
    columns = P("section", None, ("dp", "ctx"))
    vector = P("section", ("dp", "ctx"))
    tokens = P(None, "dp", "ctx", None)
    stacked = P("section", None, "dp", "ctx", None)
    return jax.shard_map(
        per_device,
        mesh=mesh,
        in_specs=(
            tokens,
            P(None, "dp", None),
            rows,
            rows,
            rows,
            rows,
            columns,
            vector,
            rows,
            rows,
            vector,
            vector,
            rows,
            rows,
            rows,
            tokens,
        ),
        out_specs=(
            stacked,
            stacked,
            rows,
            rows,
            rows,
            rows,
            columns,
            vector,
            rows,
            rows,
            vector,
            vector,
            rows,
            rows,
            rows,
        ),
        check_vma=False,
    )
```

```python
import functools

import jax
import jax.numpy as jnp
from jax import lax
from jax.experimental import pallas as pl
from jax.experimental.pallas import tpu as pltpu
from jax.sharding import PartitionSpec as P

HEADS = 4
KH = 128
VH = 256
RANK = 16
STRETCH = 64
CHUNK = 2 * STRETCH

norm_eps = 1e-06
head_eps = 0.1
BF = jnp.bfloat16
F32 = jnp.float32
highest = lax.Precision.HIGHEST


def mm(left, right):
    return jnp.dot(left, right, preferred_element_type=F32)


def mm_back(left, right):
    return lax.dot_general(left, right, (((1,), (1,)), ((), ())), preferred_element_type=F32)


def mm_rows(left, right):
    return lax.dot_general(left, right, (((0,), (0,)), ((), ())), preferred_element_type=F32)


def dot_nn(a, b):
    return lax.dot_general(
        a, b, (((1,), (0,)), ((), ())), precision=highest, preferred_element_type=F32
    )


def dot_nt(a, b):
    return lax.dot_general(
        a, b, (((1,), (1,)), ((), ())), precision=highest, preferred_element_type=F32
    )


def dot_tn(a, b):
    return lax.dot_general(
        a, b, (((0,), (0,)), ((), ())), precision=highest, preferred_element_type=F32
    )


def chunk_parts(n, q_ref, k_ref, g_ref, seg_col_ref, seg_row_ref, low_tri):
    at = pl.ds(n * CHUNK, CHUNK)
    summed = dot_nn(low_tri, g_ref[at, :])
    middle = summed[STRETCH - 1 : STRETCH, :]
    last = summed[CHUNK - 1 : CHUNK, :]
    seg = seg_col_ref[at, :]
    seg_last = seg[CHUNK - 1 : CHUNK, :]
    seg_row = seg_row_ref[:, at]
    if n > 0:
        seg_prev = seg_col_ref[pl.ds(n * CHUNK - 1, 1), :]
    else:
        seg_prev = jnp.full((1, 1), -1.0, F32)
    up = jnp.exp(summed - middle)
    down = jnp.exp(middle - summed)
    entry = jnp.where(seg == seg_prev, jnp.exp(summed), 0.0)
    tail = jnp.where(seg == seg_last, jnp.exp(last - summed), 0.0)
    keep = jnp.where(seg_last == seg_prev, jnp.exp(last), 0.0)
    return at, seg, seg_row, up, down, entry, tail, keep


def tri_masks():
    rows = lax.broadcasted_iota(jnp.int32, (CHUNK, CHUNK), 0)
    cols = lax.broadcasted_iota(jnp.int32, (CHUNK, CHUNK), 1)
    return rows >= cols, rows <= cols


def gla_fwd_kernel(count, q_ref, k_ref, v_ref, g_ref, seg_col_ref, seg_row_ref, mixed_ref, st_ref):
    lower, _ = tri_masks()
    low_tri = lower.astype(F32)
    state = jnp.zeros(st_ref.shape[1:], F32)
    for n in range(count):
        at, seg, seg_row, up, down, entry, tail, keep = chunk_parts(
            n, q_ref, k_ref, g_ref, seg_col_ref, seg_row_ref, low_tri
        )
        q, k, v = q_ref[at, :], k_ref[at, :], v_ref[at, :]
        scores = dot_nt(q * up, k * down)
        scores = jnp.where(lower & (seg == seg_row), scores, 0.0)
        out = dot_nn(scores, v)
        st_ref[n] = state
        if n > 0:
            out = out + dot_nt(q * entry, state)
        mixed_ref[at, :] = out
        if n + 1 < count:
            state = state * keep + dot_tn(v, k * tail)


def gla_bwd_kernel(
    count,
    q_ref,
    k_ref,
    v_ref,
    g_ref,
    seg_col_ref,
    seg_row_ref,
    st_ref,
    do_ref,
    dq_ref,
    dk_ref,
    dv_ref,
    dg_ref,
):
    lower, upper = tri_masks()
    low_tri = lower.astype(F32)
    up_tri = upper.astype(F32)
    d_state = jnp.zeros(st_ref.shape[1:], F32)
    for n in reversed(range(count)):
        at, seg, seg_row, up, down, entry, tail, keep = chunk_parts(
            n, q_ref, k_ref, g_ref, seg_col_ref, seg_row_ref, low_tri
        )
        q, k, v, do = q_ref[at, :], k_ref[at, :], v_ref[at, :], do_ref[at, :]
        mask = lower & (seg == seg_row)
        q_up, k_down = q * up, k * down
        scores = jnp.where(mask, dot_nt(q_up, k_down), 0.0)
        d_scores = jnp.where(mask, dot_nt(do, v), 0.0)
        dq = dot_nn(d_scores, k_down) * up
        dk = dot_tn(d_scores, q_up) * down
        dv = dot_tn(scores, do)
        d_last = None
        if n + 1 < count:
            k_tail = k * tail
            dk_tail = dot_nn(v, d_state)
            dk = dk + dk_tail * tail
            dv = dv + dot_nt(k_tail, d_state)
            d_last = jnp.sum(dk_tail * k_tail, axis=0, keepdims=True)
        if n > 0:
            state = st_ref[n]
            dq = dq + dot_nn(do, state) * entry
            if d_last is not None:
                d_last = d_last + keep * jnp.sum(d_state * state, axis=0, keepdims=True)
            d_state = d_state * keep + dot_tn(do, q * entry)
        dg = dot_nn(up_tri, q * dq - k * dk)
        if d_last is not None:
            dg = dg + d_last
        dq_ref[at, :] = dq
        dk_ref[at, :] = dk
        dv_ref[at, :] = dv
        dg_ref[at, :] = dg


KERNEL_PARAMS = pltpu.CompilerParams(vmem_limit_bytes=40 * 1024 * 1024)


def gla_fwd(q, k, v, g, seg_col, seg_row):
    length, width = v.shape
    count = length // CHUNK
    return pl.pallas_call(
        functools.partial(gla_fwd_kernel, count),
        out_shape=(
            jax.ShapeDtypeStruct((length, width), F32),
            jax.ShapeDtypeStruct((count, width, KH), F32),
        ),
        compiler_params=KERNEL_PARAMS,
        name="gla_fwd",
    )(q, k, v, g, seg_col, seg_row)


def gla_bwd(q, k, v, g, seg_col, seg_row, states, do):
    length, width = v.shape
    count = length // CHUNK
    return pl.pallas_call(
        functools.partial(gla_bwd_kernel, count),
        out_shape=(
            jax.ShapeDtypeStruct((length, KH), F32),
            jax.ShapeDtypeStruct((length, KH), F32),
            jax.ShapeDtypeStruct((length, width), F32),
            jax.ShapeDtypeStruct((length, KH), F32),
        ),
        compiler_params=KERNEL_PARAMS,
        name="gla_bwd",
    )(q, k, v, g, seg_col, seg_row, states, do)


def silu_parts(values):
    sig = 1.0 / (1.0 + jnp.exp(-values))
    return values * sig, sig * (1.0 + values * (1.0 - sig))


def out_weight(w_ref, col, block, dp, ctx, rows, out_cols):
    parts = []
    for i in range(dp):
        start = (i * ctx + block) * rows
        parts.append(w_ref[start : start + rows, col : col + out_cols])
    return jnp.concatenate(parts, axis=0)


def small_parts(head, w_ref, at, dims):
    _, _, dp, ctx, rows, _, up_cols = dims
    parts = []
    for j in range(KH // up_cols):
        start = pl.multiple_of(head * (ctx * rows), ctx * rows) + j * rows
        tile = w_ref[pl.ds(start, up_cols), at : at + 128]
        parts.append(tile[:, RANK : 2 * RANK + 1])
    return jnp.concatenate(parts, axis=0)


def project(dims, head, x_ref, w_ref, normed_ref, q_ref, k_ref, v_ref, gate_ref, low_ref, g_ref):
    attn_cols = dims[1]
    mix_cols = 2 * KH + 2 * VH
    gains = jnp.transpose(w_ref[:, mix_cols : mix_cols + 128].astype(F32))
    gains = gains[2 * RANK + 1 : 2 * RANK + 3, :]
    x = x_ref[...].astype(F32)
    unit = x * lax.rsqrt(jnp.mean(x * x, axis=-1, keepdims=True) + norm_eps)
    normed_ref[...] = (unit * gains[:1]).astype(BF)
    pre = mm(normed_ref[...], w_ref[:, :attn_cols])
    q_ref[...] = pre[:, :KH] * KH ** (-0.5)
    k_ref[...] = pre[:, KH : 2 * KH]
    v_ref[...] = pre[:, 2 * KH : 2 * KH + VH]
    gate_ref[...] = pre[:, 2 * KH + VH : mix_cols]
    low_ref[...] = pre[:, mix_cols : mix_cols + RANK].astype(BF)
    ups = small_parts(head, w_ref, mix_cols, dims)
    low_one = jnp.concatenate([low_ref[...], jnp.ones((x.shape[0], 1), BF)], axis=1)
    pre_f = mm_back(low_one, ups)
    g_ref[...] = (jnp.minimum(pre_f, 0.0) - jnp.log1p(jnp.exp(-jnp.abs(pre_f)))) / 16.0
    return gains, unit, ups, pre_f


def mixer_fwd_kernel(
    dims,
    head_ref,
    x_ref,
    w_ref,
    seg_col_ref,
    seg_row_ref,
    part_ref,
    gains_ref,
    mixed_ref,
    st_ref,
    normed_ref,
    q_ref,
    k_ref,
    v_ref,
    gate_ref,
    low_ref,
    g_ref,
):
    count, attn_cols, dp, ctx, rows, out_cols, _ = dims
    gains, _, _, _ = project(
        dims, head_ref[0], x_ref, w_ref, normed_ref, q_ref, k_ref, v_ref, gate_ref, low_ref, g_ref
    )
    gains_ref[...] = gains
    gla_fwd_kernel(
        count, q_ref, k_ref, v_ref, g_ref, seg_col_ref, seg_row_ref, mixed_ref, st_ref
    )
    mixed = mixed_ref[...]
    head_scale = lax.rsqrt(jnp.mean(mixed * mixed, axis=-1, keepdims=True) + head_eps)
    gated = (mixed * head_scale * silu_parts(gate_ref[...])[0]).astype(BF)
    for block in range(ctx):
        w_block = out_weight(w_ref, attn_cols, block, dp, ctx, rows, out_cols)
        part_ref[:, block * out_cols : (block + 1) * out_cols] = mm(gated, w_block).astype(BF)


def mixer_bwd_kernel(
    dims,
    head_ref,
    d_branch_ref,
    x_ref,
    w_ref,
    seg_col_ref,
    seg_row_ref,
    d_gain_ref,
    mixed_ref,
    st_ref,
    part_ref,
    grad_ref,
    normed_ref,
    q_ref,
    k_ref,
    v_ref,
    gate_ref,
    low_ref,
    g_ref,
    d_mixed_ref,
    dq_ref,
    dk_ref,
    dv_ref,
    dg_ref,
    d_pre_ref,
):
    count, attn_cols, dp, ctx, rows, out_cols, up_cols = dims
    half = ctx * rows // 2
    head = head_ref[0]
    _, unit, ups, pre_f = project(
        dims, head, x_ref, w_ref, normed_ref, q_ref, k_ref, v_ref, gate_ref, low_ref, g_ref
    )
    mixed = mixed_ref[...]
    head_scale = lax.rsqrt(jnp.mean(mixed * mixed, axis=-1, keepdims=True) + head_eps)
    normed = mixed * head_scale
    silu_gate, silu_slope = silu_parts(gate_ref[...])
    gated = (normed * silu_gate).astype(BF)
    d_gated = None
    for block in range(ctx):
        d_block = d_branch_ref[:, block * out_cols : (block + 1) * out_cols]
        w_block = out_weight(w_ref, attn_cols, block, dp, ctx, rows, out_cols)
        term = mm_back(d_block, w_block)
        d_gated = term if d_gated is None else d_gated + term
        grad_block = mm_rows(gated, d_block).astype(BF)
        side, spot = divmod(block, ctx // 2)
        for i in range(dp):
            start = (i * (ctx // 2) + spot) * rows
            grad_ref[side, start : start + rows, attn_cols:] = grad_block[
                i * rows : (i + 1) * rows
            ]
    d_normed = d_gated * silu_gate
    mix_cols = 2 * KH + 2 * VH
    d_pre_ref[:, 2 * KH + VH : mix_cols] = (d_gated * normed * silu_slope).astype(BF)
    inner = jnp.mean(d_normed * normed, axis=-1, keepdims=True)
    d_mixed_ref[...] = head_scale * (d_normed - normed * inner)
    gla_bwd_kernel(
        count,
        q_ref,
        k_ref,
        v_ref,
        g_ref,
        seg_col_ref,
        seg_row_ref,
        st_ref,
        d_mixed_ref,
        dq_ref,
        dk_ref,
        dv_ref,
        dg_ref,
    )
    d_forget = dg_ref[...] * (1.0 / (1.0 + jnp.exp(pre_f))) / 16.0
    ones = jnp.ones((d_forget.shape[0], 1), F32)
    grad_up = mm_rows(d_forget.astype(BF), low_ref[...])
    grad_bias = dot_tn(d_forget, ones)
    d_low = mm(d_forget.astype(BF), ups[:, :RANK]).astype(BF)
    d_pre_ref[:, :KH] = (dq_ref[...] * KH ** (-0.5)).astype(BF)
    d_pre_ref[:, KH : 2 * KH] = dk_ref[...].astype(BF)
    d_pre_ref[:, 2 * KH : 2 * KH + VH] = dv_ref[...].astype(BF)
    spare = jnp.zeros((d_low.shape[0], attn_cols - mix_cols - RANK), BF)
    d_pre_ref[:, mix_cols:] = jnp.concatenate([d_low, spare], axis=1)
    part = mm_back(d_pre_ref[...], w_ref[:, :attn_cols])
    part_ref[...] = part.astype(BF)

    model = part.shape[1]
    d_mix = jnp.sum(part * unit, axis=0, keepdims=True)
    gain_rows = jnp.concatenate([d_mix, d_gain_ref[...], jnp.zeros((6, model), F32)], axis=0)
    gain_cols = jnp.transpose(gain_rows)
    before = jnp.zeros((model, 2 * RANK + 1), F32)
    after = jnp.zeros((model, 128 - 2 * RANK - 3), F32)
    gain_tile = jnp.concatenate([before, gain_cols[:, :2], after], axis=1)
    for side in range(2):
        starts = [(2 * i + side) * half for i in range(dp)]
        own = jnp.concatenate([normed_ref[:, a : a + half] for a in starts], axis=1)
        grads = mm_rows(own, d_pre_ref[...])
        tile = jnp.concatenate([gain_tile[a : a + half] for a in starts], axis=0)
        grad_ref[side, :, :mix_cols] = grads[:, :mix_cols].astype(BF)
        grad_ref[side, :, mix_cols:attn_cols] = (grads[:, mix_cols:] + tile).astype(BF)
    pad_low = jnp.zeros((KH, RANK), F32)
    pad_high = jnp.zeros((KH, 128 - 2 * RANK - 1), F32)
    up_tile = jnp.concatenate([pad_low, grad_up, grad_bias, pad_high], axis=1).astype(BF)
    for j in range(KH // up_cols):
        side, spot = divmod(j, ctx // 2)
        at = pl.ds(pl.multiple_of(head * half, half) + spot * rows, up_cols)
        grad_ref[side, at, mix_cols:attn_cols] += up_tile[j * up_cols : (j + 1) * up_cols]


def mixer_call(kernel, name, shapes, scratch, operands):
    specs = [pl.BlockSpec(memory_space=pltpu.SMEM)]
    specs += [pl.BlockSpec(memory_space=pltpu.VMEM)] * (len(operands) - 1)
    return pl.pallas_call(
        kernel,
        in_specs=specs,
        out_specs=[pl.BlockSpec(memory_space=pltpu.VMEM)] * len(shapes),
        out_shape=[jax.ShapeDtypeStruct(*shape) for shape in shapes],
        scratch_shapes=[pltpu.VMEM(*shape) for shape in scratch],
        compiler_params=KERNEL_PARAMS,
        name=name,
    )(*operands)


def project_scratch(length, model):
    return [
        ((length, model), BF),
        ((length, KH), F32),
        ((length, KH), F32),
        ((length, VH), F32),
        ((length, VH), F32),
        ((length, RANK), BF),
        ((length, KH), F32),
    ]


def mixer_fwd(dims, head, x, w, seg_col, seg_row):
    length, model = x.shape
    shapes = [
        ((length, model), BF),
        ((2, model), F32),
        ((length, VH), F32),
        ((dims[0], VH, KH), F32),
    ]
    return mixer_call(
        functools.partial(mixer_fwd_kernel, dims),
        "mixer_fwd",
        shapes,
        project_scratch(length, model),
        (head, x, w, seg_col, seg_row),
    )


def mixer_bwd(dims, head, d_branch, x, w, seg_col, seg_row, d_gain, mixed, states):
    length, model = x.shape
    shapes = [((length, model), BF), ((2, w.shape[0] // 2, w.shape[1]), BF)]
    scratch = project_scratch(length, model) + [
        ((length, VH), F32),
        ((length, KH), F32),
        ((length, KH), F32),
        ((length, VH), F32),
        ((length, KH), F32),
        ((length, dims[1]), BF),
    ]
    return mixer_call(
        functools.partial(mixer_bwd_kernel, dims),
        "mixer_bwd",
        shapes,
        scratch,
        (head, d_branch, x, w, seg_col, seg_row, d_gain, mixed, states),
    )


def shift(block, distance):
    size = lax.axis_size("ctx")
    return lax.ppermute(block, "ctx", [(i, (i + distance) % size) for i in range(size)])


def gather_blocks(block):
    return [block] + [shift(block, s) for s in range(1, lax.axis_size("ctx"))]


def in_order(blocks):
    size, place = lax.axis_size("ctx"), lax.axis_index("ctx")
    rows = blocks[0].shape[0]
    whole = jnp.zeros((size * rows,) + blocks[0].shape[1:], blocks[0].dtype)
    for s, block in enumerate(blocks):
        whole = lax.dynamic_update_slice_in_dim(whole, block, ((place - s) % size) * rows, 0)
    return whole


def return_blocks(whole):
    size = lax.axis_size("ctx")
    rows = whole.shape[0] // size
    total = whole[:rows].astype(F32)
    for s in range(1, size):
        total = total + shift(whole[s * rows : (s + 1) * rows].astype(BF), -s).astype(F32)
    return total


def return_ordered(whole):
    size, place = lax.axis_size("ctx"), lax.axis_index("ctx")
    rows = whole.shape[0] // size
    total = lax.dynamic_slice_in_dim(whole, place * rows, rows, 0).astype(F32)
    for s in range(1, size):
        part = lax.dynamic_slice_in_dim(whole, ((place - s) % size) * rows, rows, 0)
        total = total + shift(part.astype(BF), -s).astype(F32)
    return total


def over_head(values, repeats):
    if repeats == 1:
        return values
    size = lax.axis_size("ctx")
    total = values
    for s in range(1, repeats):
        route = [(i, i - i % repeats + (i + s) % repeats) for i in range(size)]
        total = total + lax.ppermute(values, "ctx", route)
    return total


def transpose_devices(block):
    size = lax.axis_size("ctx")
    route = [(i * size + j, j * size + i) for i in range(size) for j in range(size)]
    return lax.ppermute(block, ("dp", "ctx"), route)


def swap_sections(block):
    return lax.ppermute(block, "section", [(0, 1), (1, 0)])


def hold(value, other):
    return lax.optimization_barrier((value, other))


def inv_rms(values):
    return lax.rsqrt(jnp.mean(values * values, axis=-1, keepdims=True) + norm_eps)


def norm_back(values, scale, gain, d_out):
    normed = values * scale
    d_normed = d_out * gain
    inner = jnp.mean(d_normed * normed, axis=-1, keepdims=True)
    return scale * (d_normed - normed * inner), jnp.sum(d_out * normed, axis=0)


def per_device(
    block_in,
    doc_lengths,
    w_query,
    w_key,
    w_value,
    forget_down,
    forget_up,
    forget_bias,
    w_gate,
    w_out,
    mix_gain,
    ffn_gain,
    ff_gate,
    ff_up,
    ff_down,
    out_grad,
):
    sections = lax.axis_size("section")
    dp, ctx = lax.axis_size("dp"), lax.axis_size("ctx")
    section, place = lax.axis_index("section"), lax.axis_index("ctx")
    first = section == 0
    owners = dp * ctx
    repeats = ctx // HEADS
    width = VH // repeats
    span = block_in.shape[2]
    model = block_in.shape[3]
    rows = w_query.shape[1]
    ff_rows = ff_down.shape[1]
    ff_own = ff_rows * dp
    ff_pad = -(-ff_own // 128) * 128
    up_cols = forget_up.shape[2]
    head = place // repeats

    def own_micro(array):
        return jnp.where(first, array[0], array[1])[0]

    lengths = own_micro(doc_lengths)
    begins = jnp.cumsum(lengths) - lengths
    positions = jnp.arange(span * ctx, dtype=jnp.int32)
    seg = jnp.sum((begins[None, :] <= positions[:, None]).astype(F32), axis=1)
    seg_col, seg_row = seg[:, None], seg[None, :]

    def head_blocks(shard):
        parts = shard[0].reshape(rows, HEADS, KH).transpose(1, 0, 2)
        return jnp.repeat(parts, repeats, axis=0) if repeats > 1 else parts

    def value_blocks(shard):
        return shard[0].reshape(rows, ctx, width).transpose(1, 0, 2)

    def hidden_blocks(shard):
        parts = shard[0].reshape(rows, dp, ctx, ff_rows).transpose(2, 0, 1, 3)
        parts = parts.reshape(ctx, rows, ff_own)
        return jnp.pad(parts, ((0, 0), (0, 0), (0, ff_pad - ff_own)))

    def to_all(block):
        return jnp.broadcast_to(block[None], (ctx,) + block.shape)

    up_rows = jnp.concatenate([forget_up[0].T, forget_bias[0][:, None]], axis=1)
    up_rows = jnp.pad(up_rows, ((0, rows - up_cols), (0, 0)))
    small = jnp.concatenate([up_rows, mix_gain[0][:, None], ffn_gain[0][:, None]], axis=1)
    small_cols = RANK + 3
    mix_cols = 2 * KH + 2 * width
    low_end = mix_cols + RANK
    small_end = low_end + small_cols
    attn_cols = -(-small_end // 128) * 128
    out_cols = model // ctx
    attn_send = jnp.concatenate(
        [
            head_blocks(w_query),
            head_blocks(w_key),
            value_blocks(w_value),
            value_blocks(w_gate),
            to_all(forget_down[0]),
            to_all(small),
            jnp.zeros((ctx, rows, attn_cols - small_end), BF),
        ],
        axis=2,
    )
    ff_send = jnp.concatenate([hidden_blocks(ff_gate), hidden_blocks(ff_up)], axis=2)

    half_rows = ctx * rows // 2
    half_cols = model // 2

    def exchange(send):
        got = lax.all_to_all(send, "ctx", 0, 0, tiled=True)
        return got.reshape(ctx * rows, send.shape[2])

    def layer_pieces(low, high):
        own = jnp.where(first, low, high)
        got = swap_sections(jnp.where(first, high, low))
        return jnp.where(first, own, got), jnp.where(first, got, own)

    def whole_block(own, low_half):
        high_half = lax.ppermute(own[half_rows:], "section", [(1, 0)])
        return jnp.where(first, jnp.concatenate([low_half, high_half], axis=0), own)

    def gathered(piece):
        return lax.all_gather(piece, "dp", axis=0, tiled=True)

    def gathered_direct(piece):
        place_dp = lax.axis_index("dp")
        size = piece.shape[0]
        whole = jnp.zeros((dp * size, piece.shape[1]), piece.dtype)
        whole = lax.dynamic_update_slice_in_dim(whole, piece, place_dp * size, 0)
        for step in range(1, dp):
            route = [(i, (i + step) % dp) for i in range(dp)]
            block = lax.ppermute(piece, "dp", route)
            start = ((place_dp - step) % dp) * size
            whole = lax.dynamic_update_slice_in_dim(whole, block, start, 0)
        return whole

    down_pieces = layer_pieces(ff_down[0][:, :half_cols], ff_down[0][:, half_cols:])
    down_piece = jnp.concatenate(down_pieces, axis=0)
    down_all = gathered_direct(down_piece).reshape(dp, sections, ff_rows, half_cols)
    down_halves = [down_all[:, layer].reshape(ff_own, half_cols) for layer in range(sections)]

    out_block = transpose_devices(w_out[0]).reshape(rows, ctx, out_cols)
    out_block = out_block.transpose(1, 0, 2).reshape(ctx * rows, out_cols)
    attn_block = jnp.concatenate([exchange(attn_send), out_block], axis=1)
    attn_pieces = layer_pieces(attn_block[:half_rows], attn_block[half_rows:])
    attn_high = whole_block(attn_block, attn_pieces[1])
    ff_block = exchange(hold(ff_send, attn_pieces[0])[0])
    ff_pieces = layer_pieces(ff_block[:half_rows], ff_block[half_rows:])
    ff_high = whole_block(ff_block, ff_pieces[1])

    attn_half, ff_half = gathered(attn_pieces[0]), gathered(hold(ff_pieces[0], down_all)[0])
    attn_high, attn_half = hold(attn_high, attn_half)
    ff_high, ff_half = hold(ff_high, ff_half)
    attn_high, ff_high = gathered(attn_high), gathered(ff_high)

    def both_halves(own):
        other = swap_sections(own)
        return jnp.where(first, own, other), jnp.where(first, other, own)

    def whole_rows(own):
        cols = own.shape[1]
        parts = [part.reshape(dp, 1, half_rows, cols) for part in both_halves(own)]
        return jnp.concatenate(parts, axis=1).reshape(model, cols)

    def whole_cols(own):
        return jnp.concatenate(both_halves(own), axis=1)

    def layer_smalls(w_attn):
        small = w_attn[:, low_end:small_end]
        ups = small[:, : RANK + 1].reshape(owners, rows, RANK + 1)[:, :up_cols]
        ups = ups.reshape(HEADS * KH, RANK + 1)
        gains = small[:, RANK + 1 :].T.astype(F32)
        return lax.dynamic_slice_in_dim(ups, head * KH, KH, 0), gains[:1], gains[1:]

    dims = (span * ctx // CHUNK, attn_cols, dp, ctx, rows, out_cols, up_cols)
    head_index = head.astype(jnp.int32)[None]

    def unpack_out(w_attn):
        out = w_attn[:, attn_cols:].reshape(dp, ctx, rows, out_cols)
        return out.transpose(0, 2, 1, 3).reshape(width, model)

    def mixer_forward(x_all, w_attn):
        if repeats == 1:
            part, gains, *kept = mixer_fwd(dims, head_index, x_all, w_attn, seg_col, seg_row)
            return part, gains, kept
        w_up, gain_in, gain_mid = layer_smalls(w_attn)
        x_all = x_all.astype(F32)
        normed_in = (x_all * inv_rms(x_all) * gain_in).astype(BF)
        pre = mm(normed_in, w_attn[:, :attn_cols])
        low_rank = pre[:, mix_cols:low_end].astype(BF)
        pre_f = mm_back(low_rank, w_up[:, :RANK]) + w_up[:, RANK].astype(F32)
        g = jax.nn.log_sigmoid(pre_f) / 16.0
        q = pre[:, :KH] * KH ** (-0.5)
        k = pre[:, KH : 2 * KH]
        v = pre[:, 2 * KH : 2 * KH + width]
        gate = pre[:, 2 * KH + width : mix_cols]
        mixed, states = gla_fwd(q, k, v, g, seg_col, seg_row)
        square = over_head(jnp.sum(mixed * mixed, axis=-1, keepdims=True), repeats)
        gated = mixed * lax.rsqrt(square / VH + head_eps) * silu_parts(gate)[0]
        gated = gated.astype(BF)
        part = mm(gated, unpack_out(w_attn)).astype(BF)
        gains = jnp.concatenate([gain_in, gain_mid], axis=0)
        kept = (w_up, normed_in, q, k, v, gate, low_rank, pre_f, g, mixed, states, gated)
        return part, gains, kept

    def mixer_backward(d_branch, w_attn, x_all, d_gain_mid, kept):
        if repeats == 1:
            return mixer_bwd(
                dims, head_index, d_branch, x_all, w_attn, seg_col, seg_row, d_gain_mid, *kept
            )
        w_up, normed_in, q, k, v, gate, low_rank, pre_f, g, mixed, states, gated = kept
        square = over_head(jnp.sum(mixed * mixed, axis=-1, keepdims=True), repeats)
        scale = lax.rsqrt(square / VH + head_eps)
        d_gated = mm_back(d_branch, unpack_out(w_attn))
        grad_out = mm_rows(gated, d_branch).astype(BF).reshape(dp, rows, ctx, out_cols)
        grad_out = grad_out.transpose(0, 2, 1, 3).reshape(model, out_cols)
        silu_gate, silu_slope = silu_parts(gate)
        normed = mixed * scale
        d_gate = d_gated * normed * silu_slope
        d_normed = d_gated * silu_gate
        inner = over_head(jnp.sum(d_normed * normed, axis=-1, keepdims=True), repeats) / VH
        d_mixed = scale * (d_normed - normed * inner)
        d_q, d_k, d_v, d_g = gla_bwd(q, k, v, g, seg_col, seg_row, states, d_mixed)
        d_forget = d_g * jax.nn.sigmoid(-pre_f) / 16.0
        grad_bias = jnp.sum(d_forget, axis=0)[:, None]
        d_forget = d_forget.astype(BF)
        grad_up = jnp.concatenate([mm_rows(d_forget, low_rank), grad_bias], axis=1)
        d_low = mm(d_forget, w_up[:, :RANK])
        spare = jnp.zeros((d_low.shape[0], attn_cols - low_end), F32)
        d_pre = [d_q * KH ** (-0.5), d_k, d_v, d_gate, d_low, spare]
        d_pre = jnp.concatenate([part.astype(BF) for part in d_pre], axis=1)
        part = mm_back(d_pre, w_attn[:, :attn_cols])
        x_all = x_all.astype(F32)
        grad_gain = jnp.sum(part * (x_all * inv_rms(x_all)), axis=0, keepdims=True)
        grads = jnp.concatenate([mm_rows(normed_in, d_pre).astype(BF), grad_out], axis=1)
        grads = grads.reshape(dp, 2, half_rows, attn_cols + out_cols).transpose(1, 0, 2, 3)
        grads = grads.reshape(2, dp * half_rows, attn_cols + out_cols)
        tiny = lax.dynamic_update_slice(
            jnp.zeros((owners, rows, RANK + 1), F32),
            grad_up.reshape(KH // up_cols, up_cols, RANK + 1),
            (head * (KH // up_cols), 0, 0),
        )
        tiny = jnp.concatenate(
            [tiny.reshape(model, RANK + 1), grad_gain.T, d_gain_mid.T], axis=1
        )
        tiny = tiny.astype(BF).reshape(dp, 2, half_rows, small_cols).transpose(1, 0, 2, 3)
        tiny = tiny.reshape(2, dp * half_rows, small_cols)
        return part.astype(BF), lax.dynamic_update_slice(grads, tiny, (0, 0, low_end))

    def forward(layer, x):
        x_all = in_order(gather_blocks(x))
        w_attn = whole_rows(attn_half) if layer == 0 else attn_high
        part, gains, mixer_kept = mixer_forward(x_all, w_attn)
        gain_in, gain_mid = gains[:1], gains[1:]
        if layer == 0:
            part, w_half = hold(part, ff_half)
            w_ff = whole_rows(w_half)
        else:
            w_ff = ff_high
        w_down = whole_cols(down_halves[layer])
        middle = x.astype(F32) + return_ordered(part)
        scale_mid = inv_rms(middle)
        normed_mid = jnp.concatenate(
            gather_blocks((middle * scale_mid * gain_mid).astype(BF)), axis=0
        )
        ff_pre = mm(normed_mid, w_ff)
        a, b = ff_pre[:, :ff_pad], ff_pre[:, ff_pad:]
        hidden = (silu_parts(a)[0] * b).astype(BF)[:, :ff_own]
        out = middle + return_blocks(mm(hidden, w_down))
        kept = (x_all, mixer_kept, middle, scale_mid, normed_mid, a, b, hidden)
        return out.astype(BF), (w_attn, w_ff, w_down, gain_in, gain_mid), kept

    def model_halves(array):
        low, high = [], []
        for i in range(dp):
            start = 2 * i * half_rows
            low.append(array[:, start : start + half_rows])
            high.append(array[:, start + half_rows : start + 2 * half_rows])
        low, high = jnp.concatenate(low, axis=1), jnp.concatenate(high, axis=1)
        return jnp.where(first, low, high), jnp.where(first, high, low)

    def over_dp(grad):
        return lax.psum_scatter(grad, "dp", scatter_dimension=0, tiled=True)

    def backward(layer, d_out, early, late):
        w_attn, w_ff, w_down, gain_in, gain_mid = weights[layer]
        x_all, mixer_kept, middle, scale_mid, normed_mid, a, b, hidden = layer_kept[layer]
        ff_keep, ff_send = model_halves(normed_mid)
        dff = jnp.concatenate(gather_blocks(d_out.astype(BF)), axis=0)
        d_hidden = jnp.pad(mm_back(dff, w_down), ((0, 0), (0, ff_pad - ff_own)))
        silu_a, slope_a = silu_parts(a)
        d_a = (d_hidden * b * slope_a).astype(BF)
        d_b = (d_hidden * silu_a).astype(BF)
        d_ab = jnp.concatenate([d_a, d_b], axis=1)
        d_normed_mid = return_blocks(mm_back(d_ab, w_ff))
        send_ff = mm_rows(ff_send, d_ab).astype(BF)
        grad_down = mm_rows(hidden, dff)
        down_low, down_high = grad_down[:, :half_cols], grad_down[:, half_cols:]
        if layer > 0:
            grad_down = grad_down.astype(BF)
        else:
            keep_down = jnp.where(first, down_low, down_high).astype(BF)
            grad_down = jnp.where(first, down_high, down_low).astype(BF)
        d_normed_mid, send_ff, grad_down, early = lax.optimization_barrier(
            (d_normed_mid, send_ff, grad_down, early)
        )
        got_ff = swap_sections(send_ff)
        if layer > 0:
            sum_down = over_dp(grad_down)
        else:
            got_down = swap_sections(grad_down)
            sum_down = (keep_down.astype(F32) + got_down.astype(F32)).astype(BF)
        d_mid_part, grad_gain_mid = norm_back(middle, scale_mid, gain_mid, d_normed_mid)
        d_middle = d_out + d_mid_part

        d_branch = in_order(gather_blocks(d_middle.astype(BF)))
        part, grad_attn = mixer_backward(d_branch, w_attn, x_all, grad_gain_mid[None], mixer_kept)
        send_attn = jnp.where(first, grad_attn[1], grad_attn[0])
        keep_attn = jnp.where(first, grad_attn[0], grad_attn[1])
        grad_ff = (mm_rows(ff_keep, d_ab) + got_ff.astype(F32)).astype(BF)
        if layer == 0:
            sum_down = over_dp(hold(sum_down, part)[0])
            late = over_dp(late)
        part, send_attn, late, grad_ff = lax.optimization_barrier(
            (part, send_attn, late, grad_ff)
        )
        grad_attn = keep_attn.astype(F32) + swap_sections(send_attn).astype(F32)
        grad_attn = grad_attn.astype(BF)
        d_normed_in = return_ordered(part)
        x_own = layer_x[layer].astype(F32)
        d_in_part, _ = norm_back(x_own, inv_rms(x_own), gain_in, d_normed_in)
        return d_middle + d_in_part, sum_down, over_dp(grad_ff), grad_attn, early, late

    x = own_micro(block_in)
    weights, layer_x, layer_kept, layer_y = [], [], [], []
    for layer in range(sections):
        layer_x.append(x)
        x, layer_weight, kept = forward(layer, x)
        weights.append(layer_weight)
        layer_kept.append(kept)
        layer_y.append(x)
    def to_owner(low, high, kind=None):
        mine = jnp.where(first, low, high)
        send = jnp.where(first, high, low)
        return mine, swap_sections(send if kind is None else send.astype(kind))

    def both(low, high):
        mine, other = to_owner(low, high)
        return jnp.stack([jnp.where(first, mine, other), jnp.where(first, other, mine)])

    outputs = both(*layer_y)
    d_x = own_micro(out_grad).astype(F32)
    d_in, down_high, ff_high, attn_high, _, outputs = backward(1, d_x, (), outputs)
    upstream = d_in.astype(BF).astype(F32)
    d_first, down_low, ff_low, attn_low, early, attn_high = backward(
        0, upstream, (attn_high, down_high, ff_high), attn_high
    )
    _, down_high, ff_high = early
    attn_low = over_dp(attn_low)

    def halves_of_owner(low, high):
        mine, other = to_owner(low, high)
        return jnp.where(first, mine, other), jnp.where(first, other, mine)

    def to_rows(array):
        cols = array.shape[1]
        return lax.all_to_all(array.reshape(ctx, rows, cols), "ctx", 0, 0, tiled=True).astype(F32)

    def summed(low, high):
        mine, other = to_owner(low, high)
        return mine.astype(F32) + other.astype(F32)

    mine, other = to_owner(d_first, d_in, BF)
    other = other.astype(F32)
    input_grads = jnp.stack([jnp.where(first, mine, other), jnp.where(first, other, mine)])
    got = swap_sections(jnp.where(first, down_high, jnp.pad(down_low, ((0, 0), (0, half_cols)))))
    own_low = jnp.concatenate([down_low, got[:, :half_cols]], axis=1).astype(F32)
    own_down = jnp.where(first, own_low, down_high.astype(F32) + got.astype(F32))
    own_ff = to_rows(jnp.concatenate(halves_of_owner(ff_low, ff_high), axis=0))
    attn_low, own_down, own_ff, input_grads = lax.optimization_barrier(
        (attn_low, own_down, own_ff, input_grads)
    )

    half_ctx = ctx // 2
    pieces = jnp.stack([attn_low[:, :attn_cols], attn_high[:, :attn_cols]])
    pieces = pieces.reshape(ctx, rows, attn_cols)
    arrived = []
    for step in range(ctx):
        route = []
        for s in range(sections):
            for j in range(ctx):
                to_layer, k = divmod((j + step) % ctx, half_ctx)
                route.append((s * ctx + j, to_layer * ctx + s * half_ctx + k))
        piece = lax.dynamic_index_in_dim(pieces, (place + step) % ctx, 0, False)
        arrived.append(lax.ppermute(piece, ("section", "ctx"), route))
    arrived = jnp.stack(arrived)
    mine = section * half_ctx + place % half_ctx
    own_attn = jnp.stack(
        [
            lax.dynamic_index_in_dim(arrived, (mine - source) % ctx, 0, False)
            for source in range(ctx)
        ]
    ).astype(F32)
    outs = jnp.stack([attn_low[:, attn_cols:], attn_high[:, attn_cols:]])
    came = []
    for step in range(sections):
        route = []
        for s in range(sections):
            for i in range(dp):
                for j in range(ctx):
                    to_layer = (s + step) % sections
                    route.append(((s * dp + i) * ctx + j, (to_layer * ctx + j) * dp + i))
        block = lax.dynamic_index_in_dim(outs, (section + step) % sections, 0, False)
        came.append(lax.ppermute(block, ("section", "dp", "ctx"), route))
    out_halves = [jnp.where(first, came[0], came[1]), jnp.where(first, came[1], came[0])]
    own_out = jnp.concatenate(out_halves, axis=0).reshape(ctx, rows, out_cols)
    own_out = own_out.transpose(1, 0, 2).reshape(rows, model).astype(F32)

    def hidden_whole(parts):
        parts = parts.reshape(ctx, rows, dp, ff_rows).transpose(1, 2, 0, 3)
        return parts.reshape(rows, owners * ff_rows)

    def head_whole(parts):
        parts = parts.reshape(HEADS, repeats, rows, KH).sum(1)
        return parts.transpose(1, 0, 2).reshape(rows, HEADS * KH)

    def value_whole(parts):
        return parts.transpose(1, 0, 2).reshape(rows, HEADS * VH)

    tiny = jnp.sum(own_attn[:, :, low_end:small_end], axis=0)
    return (
        outputs[None, :, None],
        input_grads[None, :, None],
        head_whole(own_attn[:, :, :KH])[None],
        head_whole(own_attn[:, :, KH : 2 * KH])[None],
        value_whole(own_attn[:, :, 2 * KH : 2 * KH + width])[None],
        jnp.sum(own_attn[:, :, mix_cols:low_end], axis=0)[None],
        tiny[:up_cols, :RANK].T[None],
        tiny[:up_cols, RANK][None],
        value_whole(own_attn[:, :, 2 * KH + width : mix_cols])[None],
        own_out[None],
        tiny[:, RANK + 1][None],
        tiny[:, RANK + 2][None],
        hidden_whole(own_ff[:, :, :ff_own])[None],
        hidden_whole(own_ff[:, :, ff_pad : ff_pad + ff_own])[None],
        own_down[None],
    )


def solution(mesh):
    rows = P("section", ("dp", "ctx"), None)
    columns = P("section", None, ("dp", "ctx"))
    vector = P("section", ("dp", "ctx"))
    tokens = P(None, "dp", "ctx", None)
    stacked = P("section", None, "dp", "ctx", None)
    return jax.shard_map(
        per_device,
        mesh=mesh,
        in_specs=(
            tokens,
            P(None, "dp", None),
            rows,
            rows,
            rows,
            rows,
            columns,
            vector,
            rows,
            rows,
            vector,
            vector,
            rows,
            rows,
            rows,
            tokens,
        ),
        out_specs=(
            stacked,
            stacked,
            rows,
            rows,
            rows,
            rows,
            columns,
            vector,
            rows,
            rows,
            vector,
            vector,
            rows,
            rows,
            rows,
        ),
        check_vma=False,
    )
```
